32 devices in a mesh: comp: 2 (over y), gx: 8 (over z, x), gy: 2 (over core).
Axes of the slice: x: 2, y: 2, z: 4, core: 2. Of those that a mesh axis runs over, the one named last changes fastest.
Arguments:
- air_state: float32 [2, 64, 512, 512], P(None, None, 'gx', ('comp', 'gy')), may hold values from -6 to 6
- coupling: float32 [63, 512, 512], P(None, 'gx', ('comp', 'gy')), may hold values from 0.05 to 10
- forcing: float32 [6, 512, 512], P(None, 'gx', ('comp', 'gy')), may hold values from -6 to 6
- surface_temp: float32 [512, 512], P('gx', ('comp', 'gy')), may hold values from -6 to 6
- remap_weight: bfloat16 [8192, 128, 128], P(('comp', 'gx', 'gy')), may hold values from -0.5 to 0.5
- block_owner: int32 [8192, 1], P(('comp', 'gx', 'gy')), may hold values from 0 to 31; in each aligned block of 256 rows (0 to 255, 256 to 511, ...) at most 8 rows name the same one
- block_row: int32 [8192], P(('comp', 'gx', 'gy')), may hold values from 0 to 63
- block_column: int32 [8192], P(('comp', 'gx', 'gy')), may hold values from 0 to 63
- land_mask: int32 [2048, 128], P(('comp', 'gx', 'gy')), may hold values 0 or 1
- ocean_temp: float32 [2048, 128], P(('comp', 'gx', 'gy')), may hold values from -6 to 6
- ocean_ice: float32 [2048, 128], P(('comp', 'gx', 'gy')), may hold values from 0 to 1
- layer_depth: float32 [2048, 128], P(('comp', 'gx', 'gy')), may hold values from 0.5 to 4
Outputs:
- air_new: float32 [2, 64, 512, 512], P(None, None, 'gx', ('comp', 'gy'))
- surface_seen: float32 [2, 512, 512], P(None, 'gx', ('comp', 'gy'))
- ocean_temp_new: float32 [2048, 128], P(('comp', 'gx', 'gy'))
- ocean_ice_new: float32 [2048, 128], P(('comp', 'gx', 'gy'))
The draws below stay inside these ranges and needn't reach their ends.
Inputs may be any that keep to these rules, and one draw needn't show every extreme that they name: `block_owner`: at most 8 of one device's 256 nonzero blocks name the same owner.
All inputs are finite; a program needn't handle non-finite values. No bound on the sum of `land_mask` on one device may be relied on, other than what follows from the above.
Results may differ from the reference program's by a relative error of at most 0.0035.
Values may be sent and summed in bfloat16 or wider, within the bound.
No kernel may reach another device: no remote copies, remote signals or barrier semaphores. Data moves between devices by JAX's collectives and lax.ppermute only.
A program may use at most 128 MiB of HBM per device.

```python
import math
import jax
import jax.numpy as jnp
import numpy as np
from jax import lax

CELL = 128
LEV = 64
SUBSTEPS = 2
NF = 8
AXD = 64
NZ_DEV = 256
CAP = 8
OB_DEV = 64
AX = 512
AY = 512
NZ_TOTAL = 8192
OBLOCKS = 2048
N_COMP = 2
N_GX = 8
N_GY = 2
DEVICES = 32


def set_ends(drawn, own_key, least, high):
    dims = drawn.shape
    place = [jax.random.randint(jax.random.fold_in(own_key, axis), (), 0, dims[axis]) for axis in range(len(dims))]
    drawn = drawn.at[tuple(place)].set(least)
    longest = dims.index(max(dims))
    place[longest] = (place[longest] + 1) % dims[longest]
    return drawn.at[tuple(place)].set(high)


def shard_levels(rng, shape, cuts, smallest, high):
    loudness = 1.0
    for position, parts in cuts:
        heights = jax.random.uniform(jax.random.fold_in(jax.random.fold_in(rng, 6), position), (parts,), jnp.float32, smallest / len(cuts), high / len(cuts))
        loudness = loudness * jnp.repeat(jnp.exp(heights), shape[position] // parts).reshape((-1,) + (1,) * (len(shape) - 1 - position))
    return loudness


def routed_block(rng, own, number, rows, amount, top, bound, lean):
    order = jax.random.permutation(rng, amount)
    heavy_load, ordinary = portions_of(amount, rows * top, bound, lean, True), portions_of(amount, rows * top, bound, lean, False)
    places = jnp.arange(amount)

    def named(lengths, turn):
        used = int((lengths > 0).sum())
        fixed = max(1, used // 4)
        moved = fixed + (places - fixed + turn * (used - fixed)) % max(1, amount - fixed)
        return jnp.zeros((amount,), jnp.int32).at[order[jnp.where(places < fixed, places, moved)]].set(jnp.asarray(lengths, jnp.int32))

    lengths = jnp.where(number % 4 == 0, named(heavy_load, number // 4), named(ordinary, number - number // 4 - 1))
    mixed = jax.random.permutation(jax.random.fold_in(own, 3), amount)
    giver, sink = mixed[0:amount // 2 * 2:2], mixed[1:amount // 2 * 2:2]
    margin = jnp.minimum(lengths[giver] - 1, bound - lengths[sink]) // 2
    margin = jnp.where((giver == order[0]) | (sink == order[0]) | (lengths[sink] == 0), 0, jnp.maximum(margin, 0))
    moved = jax.random.randint(jax.random.fold_in(own, 4), (amount // 2,), 0, 1 << 20) % (margin + 1)
    lengths = lengths.at[giver].add(-moved).at[sink].add(moved)
    items = jnp.searchsorted(jnp.cumsum(lengths), jnp.arange(rows * top), side="right").astype(jnp.int32)
    listing = items.reshape(top, rows).T
    listing = listing[jax.random.permutation(jax.random.fold_in(own, 1), rows)]
    turn = jax.random.randint(jax.random.fold_in(own, 2), (rows, 1), 0, top)
    return jnp.take_along_axis(listing, (jnp.arange(top)[None, :] + turn) % top, axis=1)


def portions_of(count, total, bound, lean, full):
    loads = [(1 << 20) // math.isqrt(grade ** lean) + 1 for grade in range(1, count + 1)]
    largest = bound if full else min(bound, max(-(-total // count), total * loads[0] // sum(loads)))
    least = 1 if total - largest >= count - 1 else 0
    given, rest = [largest] + [least] * (count - 1), total - largest - least * (count - 1)
    while rest > 0:
        candidates = [i for i in range(1, count) if given[i] < largest] or [i for i in range(1, count) if given[i] < bound]
        mass, left = sum([loads[i] for i in candidates]), rest
        for i in candidates:
            more = min(bound - given[i], max(1, left * loads[i] // mass), rest)
            given[i] = given[i] + more
            rest = rest - more
    return np.array(given)


def gaussian(key, shape, deviation, limit, cuts=(), held_as=jnp.bfloat16):
    factor_of = shard_levels(key, shape, cuts, -0.22, 0.18) if cuts else 1.0
    drawn = jax.random.normal(key, shape, jnp.float32) * deviation * factor_of
    return jnp.minimum(jnp.maximum(drawn, -limit), limit).astype(held_as)


def setup_inputs(seed: int = 0) -> dict:
    keys = jax.random.split(jax.random.key(seed), 13)
    air_state = gaussian(keys[0], (2, LEV, AX, AY), 1.0, 6.0, ((2, 8), (3, 4)), jnp.float32)
    coupling = jnp.clip(jnp.exp(math.log(10.0) - 5.2983174 * jax.random.uniform(keys[1], (LEV - 1, AX, AY), jnp.float32) ** shard_levels(keys[1], (LEV - 1, AX, AY), ((1, 8), (2, 4)), -0.2, 0.2)), 0.05, 10.0)
    forcing = gaussian(keys[2], (6, AX, AY), 1.0, 6.0, ((1, 8), (2, 4)), jnp.float32)
    surface_temp = gaussian(keys[3], (AX, AY), 1.0, 6.0, ((0, 8), (1, 4)), jnp.float32)
    remap_weight = gaussian(keys[4], (NZ_TOTAL, CELL, CELL), CELL ** -0.5, 0.5, ((0, 32),))
    block_owner_keys = jax.random.split(jax.random.fold_in(keys[5], 1), NZ_TOTAL // NZ_DEV)
    block_owner_turns = jax.random.permutation(jax.random.fold_in(keys[5], 3), NZ_TOTAL // NZ_DEV)
    block_owner = jax.vmap(lambda own, number: routed_block(jax.random.fold_in(keys[5], 2), own, number, NZ_DEV, DEVICES, 1, CAP, 2))(block_owner_keys, block_owner_turns).reshape((NZ_TOTAL, 1))
    block_row = set_ends(jax.random.randint(keys[6], (NZ_TOTAL,), 0, OB_DEV), jax.random.fold_in(keys[6], 1), 0, OB_DEV - 1).astype(jnp.int32)
    block_column = set_ends(jax.random.randint(keys[7], (NZ_TOTAL,), 0, AXD), jax.random.fold_in(keys[7], 1), 0, AXD - 1).astype(jnp.int32)
    land_mask = set_ends((jax.random.randint(keys[8], (OBLOCKS, CELL), 0, 4) < 3).astype(jnp.int32), jax.random.fold_in(keys[8], 1), 0, 1)
    ocean_temp = gaussian(keys[9], (OBLOCKS, CELL), 1.0, 6.0, ((0, 32),), jnp.float32)
    ocean_ice = jnp.clip(1.0 * jax.random.uniform(keys[10], (OBLOCKS, CELL), jnp.float32) ** shard_levels(keys[10], (OBLOCKS, CELL), ((0, 32),), -0.2, 0.2), 0.0, 1.0)
    layer_depth = jnp.clip(jnp.exp(math.log(4.0) - 2.0794415 * jax.random.uniform(keys[11], (OBLOCKS, CELL), jnp.float32) ** shard_levels(keys[11], (OBLOCKS, CELL), ((0, 32),), -0.2, 0.2)), 0.5, 4.0)
    return {"air_state": air_state, "coupling": coupling, "forcing": forcing, "surface_temp": surface_temp, "remap_weight": remap_weight, "block_owner": block_owner, "block_row": block_row, "block_column": block_column, "land_mask": land_mask, "ocean_temp": ocean_temp, "ocean_ice": ocean_ice, "layer_depth": layer_depth}


DIFFUSION = 0.2
SURFACE_STEP = 0.5

def stencil(padded):
    center = padded[:, :, 1:-1, 1:-1]
    beside_all = padded[:, :, 2:, 1:-1] + padded[:, :, :-2, 1:-1] + padded[:, :, 1:-1, 2:] + padded[:, :, 1:-1, :-2]
    return center + DIFFUSION * (beside_all - 4.0 * center)

def surface_fluxes(low_temp, low_humid, forcing, surface_temp):
    speed = jnp.sqrt(forcing[0] * forcing[0] + forcing[1] * forcing[1] + 1.0)
    return jnp.stack([speed * (surface_temp - low_temp), speed * (0.5 * surface_temp - low_humid), speed * forcing[0], speed * forcing[1], forcing[2], forcing[3] - 0.3 * surface_temp, forcing[4], forcing[5]])

def column_pass(state, coupling, source):
    levels = state.shape[1]
    pivots = []
    reduced = []
    for level in range(levels):
        right = state[:, level]
        if level == 0:
            right = right + SURFACE_STEP * source
        diagonal = jnp.ones_like(state[0, 0])
        if level > 0:
            diagonal = diagonal + coupling[level - 1]
        if level < levels - 1:
            diagonal = diagonal + coupling[level]
        if level > 0:
            pivot = diagonal - coupling[level - 1] * coupling[level - 1] / pivots[-1]
            value = (right + coupling[level - 1] * reduced[-1]) / pivot
        else:
            pivot = diagonal
            value = right / pivot
        pivots.append(pivot)
        reduced.append(value)
    solved = [reduced[-1]]
    for level in range(levels - 2, -1, -1):
        solved.append(reduced[level] + coupling[level] / pivots[level] * solved[-1])
    return jnp.stack(solved[::-1], axis=1)

def ocean_step(ocean_flux, land_mask, ocean_temp, ocean_ice, layer_depth):
    heat = ocean_flux[:, 0] + ocean_flux[:, 1] + ocean_flux[:, 4] + ocean_flux[:, 5]
    stress = ocean_flux[:, 2] * ocean_flux[:, 2] + ocean_flux[:, 3] * ocean_flux[:, 3]
    wet = land_mask.astype(jnp.float32)
    new_temp = ocean_temp + wet * (0.3 * heat / layer_depth - 0.01 * stress * ocean_temp)
    new_ice = jnp.clip(ocean_ice - wet * 0.05 * (heat + ocean_flux[:, 6] - ocean_flux[:, 7]), 0.0, 1.0)
    return (new_temp, new_ice)

def reference(air_state, coupling, forcing, surface_temp, remap_weight, block_owner, block_row, block_column, land_mask, ocean_temp, ocean_ice, layer_depth):
    all_devices = N_COMP * N_GX * N_GY
    mixed = air_state
    for substep in range(SUBSTEPS):
        mixed = stencil(jnp.pad(mixed, ((0, 0), (0, 0), (1, 1), (1, 1))))
    fluxes = surface_fluxes(mixed[0, 0], mixed[1, 0], forcing, surface_temp)
    air_new = column_pass(mixed, coupling, fluxes[:2])
    flux_blocks = fluxes.astype(jnp.bfloat16).reshape(NF, N_GX, AXD, N_COMP, N_GY, CELL)
    flux_blocks = flux_blocks.transpose(3, 1, 4, 2, 0, 5).reshape(all_devices, AXD, NF, CELL)
    weights = remap_weight.reshape(all_devices, NZ_DEV, CELL, CELL)
    columns = block_column.reshape(all_devices, NZ_DEV)

    def forward_device(inputs):
        dev_blocks, dev_weights, dev_columns = inputs
        picked = dev_blocks[dev_columns]
        return jnp.einsum('nfj,nij->nfi', picked.astype(jnp.float32), dev_weights.astype(jnp.float32))
    contribution = lax.map(forward_device, (flux_blocks, weights, columns)).reshape(all_devices * NZ_DEV, NF, CELL)
    target = (block_owner[:, 0] * OB_DEV + block_row).astype(jnp.int32)
    ocean_flux = jax.ops.segment_sum(contribution, target, num_segments=OBLOCKS)
    ocean_temp_new, ocean_ice_new = ocean_step(ocean_flux, land_mask, ocean_temp, ocean_ice, layer_depth)
    pair = jnp.stack([ocean_temp_new, ocean_ice_new], axis=1).astype(jnp.bfloat16)
    sent = pair[target].reshape(all_devices, NZ_DEV, 2, CELL)

    def back_device(inputs):
        dev_pair, dev_weights, dev_columns = inputs
        terms = jnp.einsum('nfi,nij->nfj', dev_pair.astype(jnp.float32), dev_weights.astype(jnp.float32))
        return jax.ops.segment_sum(terms, dev_columns, num_segments=AXD)
    seen = lax.map(back_device, (sent, weights, columns))
    surface_seen = seen.reshape(N_COMP, N_GX, N_GY, AXD, 2, CELL).transpose(4, 1, 3, 0, 2, 5).reshape(2, AX, AY)
    return (air_new, surface_seen, ocean_temp_new, ocean_ice_new)
```

```python
import functools

import jax
import jax.numpy as jnp
from jax import lax
from jax.experimental import pallas as pl
from jax.experimental.pallas import tpu as pltpu
from jax.sharding import PartitionSpec as P

F32 = jnp.float32
BF16 = jnp.bfloat16
ALL = ("comp", "gx", "gy")
NF = 8
SENT = 5
SURFACE_STEP = 0.5
MIX = 0.2
MIB = 1 << 20
BIG = 56 * MIB


def swaps(count, first):
    pairs = [(i, i + 1) for i in range(first, count - 1, 2)]
    return pairs + [(b, a) for a, b in pairs]


def grid_place():
    gx, n_gx = lax.axis_index("gx"), lax.axis_size("gx")
    c = lax.axis_index("comp") * lax.axis_size("gy") + lax.axis_index("gy")
    n_c = lax.axis_size("comp") * lax.axis_size("gy")
    there = lambda yes: jnp.where(yes, 1.0, 0.0).astype(F32)
    return gx % 2 == 0, c % 2 == 0, there(gx > 0), there(gx < n_gx - 1), there(c > 0), there(c < n_c - 1)


def rows_kernel(first, last, rows_a, rows_b):
    even_row = grid_place()[0]
    fields, levels, tile, lanes = first.shape
    for field in range(fields):
        at = slice(field * levels, (field + 1) * levels)
        for k in range(2):
            low, high = first[field, :, k, :], last[field, :, tile - 1 - k, :]
            to = slice(k * lanes, (k + 1) * lanes)
            rows_a[at, to] = jnp.where(even_row, high, low).astype(BF16)
            rows_b[at, to] = jnp.where(even_row, low, high).astype(BF16)


def pack_rows(air):
    fields, levels, rows, lanes = air.shape
    tile = 8
    out = jax.ShapeDtypeStruct((fields * levels, 2 * lanes), BF16)
    return pl.pallas_call(
        rows_kernel,
        grid=(1,),
        in_specs=[
            pl.BlockSpec((fields, levels, tile, lanes), lambda i: (0, 0, 0, 0)),
            pl.BlockSpec((fields, levels, tile, lanes), lambda i: (0, 0, rows // tile - 1, 0)),
        ],
        out_specs=[pl.BlockSpec(out.shape, lambda i: (0, 0))] * 2,
        out_shape=[out, out],
        compiler_params=pltpu.CompilerParams(vmem_limit_bytes=BIG),
        name="pack_rows",
    )(air, air)


def cols_kernel(air, own_left, own_right, left, right):
    step = pl.program_id(0)
    fields, chunk, rows, lanes = air.shape
    levels = chunk * pl.num_programs(0)
    pair = lax.broadcasted_iota(jnp.int32, (rows, lanes), 1) >> 1
    for field in range(fields):
        to_left, to_right = left[field], right[field]
        for sub in range(chunk):
            level = step * chunk + sub
            turned = pltpu.roll(air[field, sub], 2 * level, axis=1)
            to_left = jnp.where(pair == level, turned, to_left)
            to_right = jnp.where(pair == (level + levels - 1) % levels, turned, to_right)
        left[field] = to_left
        right[field] = to_right

    @pl.when(step == pl.num_programs(0) - 1)
    def _():
        for field in range(fields):
            own_left[field] = left[field]
            own_right[field] = pltpu.roll(right[field], 2, axis=1)


def pack_cols(air):
    fields, levels, rows, lanes = air.shape
    chunk = 8
    out = jax.ShapeDtypeStruct((fields, rows, lanes), F32)
    return pl.pallas_call(
        cols_kernel,
        grid=(levels // chunk,),
        in_specs=[pl.BlockSpec((fields, chunk, rows, lanes), lambda i: (0, i, 0, 0))],
        out_specs=[pl.BlockSpec(out.shape, lambda i: (0, 0, 0))] * 2,
        out_shape=[out, out],
        scratch_shapes=[pltpu.VMEM(out.shape, F32)] * 2,
        compiler_params=pltpu.CompilerParams(vmem_limit_bytes=BIG),
        cost_estimate=pl.CostEstimate(flops=4 * air.size, bytes_accessed=4 * air.size, transcendentals=0),
        name="pack_cols",
    )(air)


def with_row(strip, row, first):
    rows = strip.shape[0]
    index = lax.broadcasted_iota(jnp.int32, strip.shape, 0)
    if first:
        return jnp.where(index == 0, row, pltpu.roll(strip, 1, axis=0))
    return jnp.where(index == rows - 1, row, pltpu.roll(strip, rows - 1, axis=0))


def strips_kernel(got_a, got_b, own_left, own_right, to_g, to_x):
    even_col = grid_place()[1]
    fields, rows, lanes = own_left.shape
    top, _, low, _ = row_halo(got_a, got_b)
    levels = top.shape[0] // fields
    level = lax.broadcasted_iota(jnp.int32, (levels, lanes), 0)
    pair = lax.broadcasted_iota(jnp.int32, (levels, lanes), 1) >> 1
    spread = jnp.where(level == pair, 1.0, 0.0).astype(BF16)
    odd = (lax.broadcasted_iota(jnp.int32, (rows, lanes), 1) & 1) == 1
    for field in range(fields):
        at = slice(field * levels, (field + 1) * levels)
        above, below = [
            lax.dot_general(h[at].astype(BF16), spread, (((0,), (0,)), ((), ())), preferred_element_type=F32)
            for h in (top, low)
        ]
        left, right = own_left[field], own_right[field]
        edge = pltpu.roll(left, 1, axis=1)
        around = with_row(edge, 2.0 * above[0:1], True) + with_row(edge, 2.0 * below[0:1], False)
        west = jnp.where(odd, MIX * (edge + left + around), left)
        edge = pltpu.roll(right, lanes - 1, axis=1)
        around = with_row(edge, 2.0 * above[lanes - 1 :], True) + with_row(edge, 2.0 * below[lanes - 1 :], False)
        east = jnp.where(odd, right, MIX * (edge + right + around))
        to_g[field] = jnp.where(even_col, east, west).astype(BF16)
        to_x[field] = jnp.where(even_col, west, east).astype(BF16)


def make_strips(got_a, got_b, own_left, own_right):
    vmem = pl.BlockSpec(memory_space=pltpu.VMEM)
    out = jax.ShapeDtypeStruct(own_left.shape, BF16)
    return pl.pallas_call(
        strips_kernel,
        in_specs=[vmem] * 4,
        out_specs=[vmem] * 2,
        out_shape=[out, out],
        compiler_params=pltpu.CompilerParams(vmem_limit_bytes=BIG),
        name="strips",
    )(got_a, got_b, own_left, own_right)


def side_strips(field, got_g, got_x, own_left, own_right):
    _, even_col, _, _, has_left, has_right = grid_place()
    rows, lanes = got_g.shape[1], got_g.shape[2]
    from_g, from_x = got_g[field].astype(F32), got_x[field].astype(F32)
    west = jnp.where(even_col, from_x, from_g)
    east = jnp.where(even_col, from_g, from_x)
    next_west = pltpu.roll(west + MIX * own_left[field], 1, axis=1) * has_left
    next_east = pltpu.roll(east + MIX * own_right[field], lanes - 1, axis=1) * has_right
    odd = (lax.broadcasted_iota(jnp.int32, (rows, lanes), 1) & 1) == 1
    return jnp.where(odd, west, east), jnp.where(odd, next_west, next_east)


def row_halo(got_a, got_b):
    even_row = grid_place()[0]
    from_a, from_b = got_a[...].astype(F32), got_b[...].astype(F32)
    top = jnp.where(even_row, from_b, from_a)
    low = jnp.where(even_row, from_a, from_b)
    lanes = top.shape[1] // 2
    return top[:, :lanes], top[:, lanes:], low[:, :lanes], low[:, lanes:]


def sides_of_row(row):
    lanes = row.shape[1]
    lane = lax.broadcasted_iota(jnp.int32, row.shape, 1)
    from_left = jnp.where(lane == 0, 0.0, pltpu.roll(row, 1, axis=1))
    from_right = jnp.where(lane == lanes - 1, 0.0, pltpu.roll(row, lanes - 1, axis=1))
    return from_left + from_right


def substep(block, above, below, sides):
    lanes = block.shape[1]
    lane = lax.broadcasted_iota(jnp.int32, block.shape, 1)
    from_left = jnp.where(lane == 0, sides, pltpu.roll(block, 1, axis=1))
    from_right = jnp.where(lane == lanes - 1, sides, pltpu.roll(block, lanes - 1, axis=1))
    around = with_row(block, above, True) + with_row(block, below, False)
    return MIX * (block + around + (from_left + from_right))


def mixed_level(block, top1, top2, low1, low2, sides0, sides1):
    rows = block.shape[0]
    first, last = block[0:1], block[rows - 1 : rows]
    _, _, has_top, has_low, _, _ = grid_place()
    next_top = has_top * MIX * (top1 + top2 + first + sides_of_row(top1))
    next_low = has_low * MIX * (low1 + low2 + last + sides_of_row(low1))
    once = substep(block, top1, low1, sides0)
    return substep(once, next_top, next_low, sides1)


def forward_kernel(
    owner, block_row, block_column, air, forcing, surface_temp, got_a, got_b, got_g, got_x,
    own_left, own_right, weight, payload, slots, source,
    flux_rows, found, tags, counts, bound, levels, group,
):
    step = pl.program_id(0)
    blocks = weight.shape[0]
    rows, lanes = surface_temp.shape
    total = payload.shape[0] * payload.shape[1]

    @pl.when(step == 0)
    def _():
        halo = row_halo(got_a, got_b)
        lowest = []
        for field in range(2):
            sides0, sides1 = side_strips(field, got_g, got_x, own_left, own_right)
            at = field * levels
            lowest.append(
                mixed_level(
                    air[field, 0],
                    *[h[at : at + 1] for h in halo],
                    pltpu.roll(sides0, lanes - 1, axis=1),
                    pltpu.roll(sides1, lanes - 1, axis=1),
                )
            )
        u, v = forcing[0], forcing[1]
        ts = surface_temp[...]
        speed = jnp.sqrt(u * u + v * v + 1.0)
        fluxes = [
            speed * (ts - lowest[0]),
            speed * (0.5 * ts - lowest[1]),
            speed * u,
            speed * v,
            forcing[2],
            forcing[3] - 0.3 * ts,
            forcing[4],
            forcing[5],
        ]
        source[0] = fluxes[0]
        source[1] = fluxes[1]
        for field in range(NF):
            flux_rows[pl.ds(field, rows, stride=NF), :] = fluxes[field]
        tags[...] = jnp.full_like(tags, -1.0)
        if total > blocks * pl.num_programs(0):
            found[...] = jnp.zeros_like(found)

        def clear(i, _):
            counts[i] = 0
            return 0

        lax.fori_loop(0, payload.shape[0], clear, 0)

    def some(g, _):
        outs = []
        for k in range(group):
            n = g * group + k
            at = step * blocks + n
            picked = flux_rows[pl.ds(pl.multiple_of(block_column[at] * NF, NF), NF), :]
            out = lax.dot_general(
                picked.astype(BF16), weight[n], (((1,), (1,)), ((), ())), preferred_element_type=F32
            )
            outs.append((at, out))
        for at, out in outs:
            to = owner[at]
            rank = counts[to]
            counts[to] = rank + 1
            slot = to * bound + rank
            slots[at] = slot
            found[pl.ds(pl.multiple_of(slot * NF, NF), NF), :] = out
            tags[pl.ds(slot, 1), :] = jnp.full((1, lanes), block_row[at], jnp.int32).astype(F32)
        return 0

    lax.fori_loop(0, blocks // group, some, 0)

    @pl.when(step == pl.num_programs(0) - 1)
    def _():
        f = [found[pl.ds(k, total, stride=NF), :] for k in range(NF)]
        heat = (f[0] + f[1]) + (f[4] + f[5])
        heat_hi = heat.astype(BF16).astype(F32)
        lane = lax.broadcasted_iota(jnp.int32, (total, lanes), 1)
        heat_lo = jnp.where(lane == 0, tags[...], heat - heat_hi)
        shape = payload.shape[:2] + (lanes,)
        for k, part in enumerate((heat_hi, heat_lo, f[2], f[3], f[6] - f[7])):
            payload[:, :, k * lanes : (k + 1) * lanes] = part.reshape(shape).astype(BF16)


def forward(owner, block_row, block_column, air, forcing, surface_temp, halo, own, weight, devices, bound):
    got_a, got_b, got_g, got_x = halo
    _, levels, rows, lanes = air.shape
    nonzeros = weight.shape[0]
    chunk = 32
    whole = lambda x: pl.BlockSpec(x.shape, lambda i: (0,) * x.ndim)
    smem = pl.BlockSpec(memory_space=pltpu.SMEM)
    args = (forcing, surface_temp, got_a, got_b, got_g, got_x, *own)
    total = devices * bound
    return pl.pallas_call(
        functools.partial(forward_kernel, bound=bound, levels=levels, group=8),
        grid=(nonzeros // chunk,),
        in_specs=[smem, smem, smem]
        + [pl.BlockSpec((2, 1, rows, lanes), lambda i: (0, 0, 0, 0))]
        + [whole(x) for x in args]
        + [pl.BlockSpec((chunk, lanes, lanes), lambda i: (i, 0, 0))],
        out_specs=[
            pl.BlockSpec((devices, bound, SENT * lanes), lambda i: (0, 0, 0)),
            smem,
            pl.BlockSpec((2, rows, lanes), lambda i: (0, 0, 0)),
        ],
        out_shape=[
            jax.ShapeDtypeStruct((devices, bound, SENT * lanes), BF16),
            jax.ShapeDtypeStruct((nonzeros,), jnp.int32),
            jax.ShapeDtypeStruct((2, rows, lanes), F32),
        ],
        scratch_shapes=[
            pltpu.VMEM((rows * NF, lanes), F32),
            pltpu.VMEM((total * NF, lanes), F32),
            pltpu.VMEM((total, lanes), F32),
            pltpu.SMEM((devices,), jnp.int32),
        ],
        compiler_params=pltpu.CompilerParams(vmem_limit_bytes=BIG),
        name="forward_blocks",
    )(owner, block_row, block_column, air, *args, weight)


def column_kernel(
    air, coupling, got_a, got_b, got_g, got_x, own_left, own_right,
    source, air_new, ratio, halo_rows, strips,
):
    _, levels, rows, lanes = air.shape
    for k, h in enumerate(row_halo(got_a, got_b)):
        halo_rows[k] = h
    for field in range(2):
        sides0, sides1 = side_strips(field, got_g, got_x, own_left, own_right)
        strips[field, 0] = sides0
        strips[field, 1] = sides1

    def mixed(field, level):
        at = pl.ds(field * levels + level, 1)
        shift = (2 * lanes - 1 - 2 * level) % lanes
        return mixed_level(
            air[field, level],
            *[halo_rows[k, at, :] for k in range(4)],
            pltpu.roll(strips[field, 0], shift, axis=1),
            pltpu.roll(strips[field, 1], shift, axis=1),
        )

    above = coupling[0]
    inverse = 1.0 / (1.0 + above)
    ratio[0] = above * inverse
    for field in range(2):
        air_new[field, 0] = (mixed(field, 0) + SURFACE_STEP * source[field]) * inverse

    def up(level, carry, top=False):
        below = coupling[level - 1]
        diagonal = 1.0 + below
        if not top:
            above = coupling[level]
            diagonal = diagonal + above
        inverse = 1.0 / (diagonal - below * ratio[level - 1])
        if not top:
            ratio[level] = above * inverse
        for field in range(2):
            air_new[field, level] = (mixed(field, level) + below * air_new[field, level - 1]) * inverse
        return carry

    lax.fori_loop(1, levels - 1, up, 0)
    up(levels - 1, 0, True)

    def down(i, carry):
        level = levels - 2 - i
        for field in range(2):
            air_new[field, level] = air_new[field, level] + ratio[level] * air_new[field, level + 1]
        return carry

    lax.fori_loop(0, levels - 1, down, 0)


def columns(air, coupling, halo, own, source):
    got_a, got_b, got_g, got_x = halo
    fields, levels, rows, lanes = air.shape
    args = (air, coupling, got_a, got_b, got_g, got_x, *own, source)
    vmem = pl.BlockSpec(memory_space=pltpu.VMEM)
    return pl.pallas_call(
        column_kernel,
        in_specs=[vmem] * len(args),
        out_specs=vmem,
        out_shape=jax.ShapeDtypeStruct(air.shape, F32),
        scratch_shapes=[
            pltpu.VMEM((levels - 1, rows, lanes), F32),
            pltpu.VMEM((4, fields * levels, lanes), F32),
            pltpu.VMEM((fields, 2, rows, lanes), F32),
        ],
        compiler_params=pltpu.CompilerParams(vmem_limit_bytes=BIG),
        cost_estimate=pl.CostEstimate(flops=40 * air.size, bytes_accessed=11 * air.size, transcendentals=0),
        name="columns",
    )(*args)


def ocean_kernel(arrived, land_mask, ocean_temp, ocean_ice, layer_depth, temp_new, ice_new, replies):
    blocks, lanes = ocean_temp.shape
    total = arrived.shape[0] * arrived.shape[1]
    parts = [
        arrived[:, :, k * lanes : (k + 1) * lanes].astype(F32).reshape(total, lanes) for k in range(SENT)
    ]
    lane = lax.broadcasted_iota(jnp.int32, (total, lanes), 1)
    tag = parts[1][:, 0:1].astype(jnp.int32)
    parts[1] = jnp.where(lane == 0, 0.0, parts[1])
    slot_of = (tag == lax.broadcasted_iota(jnp.int32, (total, blocks), 1)).astype(F32).astype(BF16)
    sums = [
        lax.dot_general(slot_of, p.astype(BF16), (((0,), (0,)), ((), ())), preferred_element_type=F32)
        for p in parts
    ]
    heat = sums[0] + sums[1]
    stress = sums[2] * sums[2] + sums[3] * sums[3]
    wet = land_mask[...].astype(F32)
    temp = ocean_temp[...]
    temp = temp + wet * (0.3 * heat / layer_depth[...] - 0.01 * stress * temp)
    ice = jnp.clip(ocean_ice[...] - wet * 0.05 * (heat + sums[4]), 0.0, 1.0)
    temp_new[...] = temp
    ice_new[...] = ice
    shape = replies.shape[:2] + (lanes,)
    for k, field in enumerate((temp, ice)):
        answer = jnp.dot(slot_of, field.astype(BF16), preferred_element_type=F32)
        replies[:, :, k * lanes : (k + 1) * lanes] = answer.reshape(shape).astype(BF16)


def ocean(arrived, land_mask, ocean_temp, ocean_ice, layer_depth):
    devices, bound, _ = arrived.shape
    blocks, lanes = ocean_temp.shape
    vmem = pl.BlockSpec(memory_space=pltpu.VMEM)
    return pl.pallas_call(
        ocean_kernel,
        in_specs=[vmem] * 5,
        out_specs=[vmem] * 3,
        out_shape=[
            jax.ShapeDtypeStruct((blocks, lanes), F32),
            jax.ShapeDtypeStruct((blocks, lanes), F32),
            jax.ShapeDtypeStruct((devices, bound, 2 * lanes), BF16),
        ],
        compiler_params=pltpu.CompilerParams(vmem_limit_bytes=BIG),
        name="ocean",
    )(arrived, land_mask, ocean_temp, ocean_ice, layer_depth)


def backward_kernel(slots, block_column, returned, weight, seen, pairs, sums, group):
    step = pl.program_id(0)
    blocks, lanes = weight.shape[0], weight.shape[1]
    total = returned.shape[0] * returned.shape[1]
    rows = seen.shape[1]

    @pl.when(step == 0)
    def _():
        pairs[...] = jnp.zeros_like(pairs)
        sums[...] = jnp.zeros_like(sums)
        for k in range(2):
            part = returned[:, :, k * lanes : (k + 1) * lanes].astype(F32).reshape(total, lanes)
            pairs[pl.ds(k, total, stride=8), :] = part

    def some(g, _):
        outs = []
        for k in range(group):
            n = g * group + k
            at = step * blocks + n
            pair = pairs[pl.ds(pl.multiple_of(slots[at] * 8, 8), 8), :]
            outs.append((at, jnp.dot(pair.astype(BF16), weight[n], preferred_element_type=F32)))
        for at, out in outs:
            place = pl.ds(pl.multiple_of(block_column[at] * 8, 8), 8)
            sums[place, :] += out
        return 0

    lax.fori_loop(0, blocks // group, some, 0)

    @pl.when(step == pl.num_programs(0) - 1)
    def _():
        for k in range(2):
            seen[k] = sums[pl.ds(k, rows, stride=8), :]


def backward(slots, block_column, returned, weight, rows):
    devices, bound, _ = returned.shape
    nonzeros, lanes, _ = weight.shape
    chunk = 32
    smem = pl.BlockSpec(memory_space=pltpu.SMEM)
    return pl.pallas_call(
        functools.partial(backward_kernel, group=8),
        grid=(nonzeros // chunk,),
        in_specs=[
            smem,
            smem,
            pl.BlockSpec((devices, bound, 2 * lanes), lambda i: (0, 0, 0)),
            pl.BlockSpec((chunk, lanes, lanes), lambda i: (i, 0, 0)),
        ],
        out_specs=pl.BlockSpec((2, rows, lanes), lambda i: (0, 0, 0)),
        out_shape=jax.ShapeDtypeStruct((2, rows, lanes), F32),
        scratch_shapes=[
            pltpu.VMEM((devices * bound * 8, lanes), F32),
            pltpu.VMEM((rows * 8, lanes), F32),
        ],
        compiler_params=pltpu.CompilerParams(vmem_limit_bytes=BIG),
        name="backward_blocks",
    )(slots, block_column, returned, weight)


def local(
    air_state,
    coupling,
    forcing,
    surface_temp,
    remap_weight,
    block_owner,
    block_row,
    block_column,
    land_mask,
    ocean_temp,
    ocean_ice,
    layer_depth,
):
    devices = lax.axis_size("comp") * lax.axis_size("gx") * lax.axis_size("gy")
    nonzeros = remap_weight.shape[0]
    bound = max(4, (nonzeros + devices - 1) // devices)
    n_gx = lax.axis_size("gx")
    n_c = lax.axis_size("comp") * lax.axis_size("gy")
    rows_a, rows_b = pack_rows(air_state)
    got_a = lax.ppermute(rows_a, "gx", swaps(n_gx, 0))
    got_b = lax.ppermute(rows_b, "gx", swaps(n_gx, 1))
    own = pack_cols(air_state)
    to_g, to_x = make_strips(got_a, got_b, *own)
    got_x = lax.ppermute(to_x, ("comp", "gy"), swaps(n_c, 1))
    got_g = lax.ppermute(to_g, ("comp", "gy"), swaps(n_c, 0))
    halo = (got_a, got_b, got_g, got_x)
    payload, slots, source = forward(
        block_owner[:, 0], block_row, block_column, air_state, forcing, surface_temp, halo, own,
        remap_weight, devices, bound,
    )
    arrived = lax.all_to_all(payload, ALL, split_axis=0, concat_axis=0, tiled=True)
    air_new = columns(air_state, coupling, halo, own, source)
    ocean_temp_new, ocean_ice_new, replies = ocean(
        arrived, land_mask, ocean_temp, ocean_ice, layer_depth
    )
    returned = lax.all_to_all(replies, ALL, split_axis=0, concat_axis=0, tiled=True)
    surface_seen = backward(slots, block_column, returned, remap_weight, surface_temp.shape[0])
    return (air_new, surface_seen, ocean_temp_new, ocean_ice_new)


def solution(mesh):
    in_specs = (
        P(None, None, "gx", ("comp", "gy")),
        P(None, "gx", ("comp", "gy")),
        P(None, "gx", ("comp", "gy")),
        P("gx", ("comp", "gy")),
        P(ALL, None, None),
        P(ALL, None),
        P(ALL),
        P(ALL),
        P(ALL, None),
        P(ALL, None),
        P(ALL, None),
        P(ALL, None),
    )
    out_specs = (
        P(None, None, "gx", ("comp", "gy")),
        P(None, "gx", ("comp", "gy")),
        P(ALL, None),
        P(ALL, None),
    )
    return jax.shard_map(local, mesh=mesh, in_specs=in_specs, out_specs=out_specs, check_vma=False)
```

```python
import functools

import jax
import jax.numpy as jnp
from jax import lax
from jax.experimental import pallas as pl
from jax.experimental.pallas import tpu as pltpu
from jax.sharding import PartitionSpec as P

F32 = jnp.float32
BF16 = jnp.bfloat16
ALL = ("comp", "gx", "gy")
NF = 8
SENT = 5
SURFACE_STEP = 0.5
MIX = 0.2
MIB = 1 << 20
BIG = 56 * MIB
PARTS = 8
STEP = 8
GROUP = 4


def row_swaps(first):
    n_gx, n_gy = lax.axis_size("gx"), lax.axis_size("gy")
    pairs = []
    for comp in range(lax.axis_size("comp")):
        for gx in range(n_gx):
            for gy in range(n_gy):
                other = gx + 1 if (gx - first) % 2 == 0 else gx - 1
                to, core = (other, gy) if 0 <= other < n_gx else (gx, gy ^ 1)
                pairs.append(((comp * n_gx + gx) * n_gy + gy, (comp * n_gx + to) * n_gy + core))
    return pairs


def col_swaps(first):
    count = lax.axis_size("comp") * lax.axis_size("gy")
    return [(i, (i + 1 if (i - first) % 2 == 0 else i - 1) % count) for i in range(count)]


def grid_place():
    gx, n_gx = lax.axis_index("gx"), lax.axis_size("gx")
    c = lax.axis_index("comp") * lax.axis_size("gy") + lax.axis_index("gy")
    n_c = lax.axis_size("comp") * lax.axis_size("gy")
    there = lambda yes: jnp.where(yes, 1.0, 0.0).astype(F32)
    return gx % 2 == 0, c % 2 == 0, there(gx > 0), there(gx < n_gx - 1), there(c > 0), there(c < n_c - 1)


def rows_kernel(air, rows_a, rows_b, first, last, sem):
    even_row = grid_place()[0]
    count, tile, lanes = first.shape
    rows = air.shape[1]
    copies = [
        pltpu.make_async_copy(air.at[:, pl.ds(0, tile)], first, sem.at[0]),
        pltpu.make_async_copy(air.at[:, pl.ds(rows - tile, tile)], last, sem.at[1]),
    ]
    for c in copies:
        c.start()
    for c in copies:
        c.wait()
    first, last = [x.reshape(count * tile, lanes) for x in (first, last)]
    for k in range(2):
        low, high = first[pl.ds(k, count, stride=tile), :], last[pl.ds(tile - 1 - k, count, stride=tile), :]
        to = slice(k * lanes, (k + 1) * lanes)
        rows_a[:, to] = jnp.where(even_row, high, low).astype(BF16)
        rows_b[:, to] = jnp.where(even_row, low, high).astype(BF16)


def pack_rows(air):
    fields, levels, rows, lanes = air.shape
    out = jax.ShapeDtypeStruct((fields * levels, 2 * lanes), BF16)
    edge = pltpu.VMEM((fields * levels, 8, lanes), F32)
    return pl.pallas_call(
        rows_kernel,
        in_specs=[pl.BlockSpec(memory_space=pl.ANY)],
        out_specs=[pl.BlockSpec(memory_space=pltpu.VMEM)] * 2,
        out_shape=[out, out],
        scratch_shapes=[edge, edge, pltpu.SemaphoreType.DMA((2,))],
        compiler_params=pltpu.CompilerParams(vmem_limit_bytes=BIG),
        name="pack_rows",
    )(air.reshape(fields * levels, rows, lanes))


def cols_kernel(air, own_left, own_right, held, sem, chunk):
    fields, levels, rows, lanes = air.shape
    copies = []
    for i in range(levels // chunk):
        part = pl.ds(i * chunk, chunk)
        copies.append(pltpu.make_async_copy(air.at[:, part], held.at[:, part], sem.at[i]))
        copies[i].start()
    pair = lax.broadcasted_iota(jnp.int32, (rows, lanes), 1) >> 1
    for i in range(levels // chunk):
        copies[i].wait()

        def some(g, carry):
            out = []
            for field in range(fields):
                left, right = carry[2 * field : 2 * field + 2]
                for k in range(4):
                    level = i * chunk + g * 4 + k
                    turned = pltpu.roll(held[field, level], 2 * level, axis=1)
                    left = jnp.where(pair == level, turned, left)
                    right = jnp.where(pair == (level + levels - 1) % levels, turned, right)
                out += [left, right]
            return tuple(out)

        if i == 0:
            carry = (jnp.zeros((rows, lanes), F32),) * (2 * fields)
        carry = lax.fori_loop(0, chunk // 4, some, carry)
    for field in range(fields):
        own_left[field] = carry[2 * field]
        own_right[field] = pltpu.roll(carry[2 * field + 1], 2, axis=1)


def pack_cols(air):
    fields, levels, rows, lanes = air.shape
    chunk = 8
    out = jax.ShapeDtypeStruct((fields, rows, lanes), F32)
    return pl.pallas_call(
        functools.partial(cols_kernel, chunk=chunk),
        in_specs=[pl.BlockSpec(memory_space=pl.ANY)],
        out_specs=[pl.BlockSpec(memory_space=pltpu.VMEM)] * 2,
        out_shape=[out, out],
        scratch_shapes=[pltpu.VMEM(air.shape, F32), pltpu.SemaphoreType.DMA((levels // chunk,))],
        compiler_params=pltpu.CompilerParams(vmem_limit_bytes=BIG),
        cost_estimate=pl.CostEstimate(flops=4 * air.size, bytes_accessed=4 * air.size, transcendentals=0),
        name="pack_cols",
    )(air)


def with_row(strip, row, first):
    rows = strip.shape[0]
    index = lax.broadcasted_iota(jnp.int32, strip.shape, 0)
    if first:
        return jnp.where(index == 0, row, pltpu.roll(strip, 1, axis=0))
    return jnp.where(index == rows - 1, row, pltpu.roll(strip, rows - 1, axis=0))


def strips_kernel(got_a, got_b, own_left, own_right, to_g, to_x):
    even_col = grid_place()[1]
    fields, rows, lanes = own_left.shape
    top, _, low, _ = row_halo(got_a, got_b)
    levels = top.shape[0] // fields
    level = lax.broadcasted_iota(jnp.int32, (levels, lanes), 0)
    pair = lax.broadcasted_iota(jnp.int32, (levels, lanes), 1) >> 1
    spread = jnp.where(level == pair, 1.0, 0.0).astype(BF16)
    odd = (lax.broadcasted_iota(jnp.int32, (rows, lanes), 1) & 1) == 1
    for field in range(fields):
        at = slice(field * levels, (field + 1) * levels)
        above, below = [
            lax.dot_general(h[at].astype(BF16), spread, (((0,), (0,)), ((), ())), preferred_element_type=F32)
            for h in (top, low)
        ]
        left, right = own_left[field], own_right[field]
        edge = pltpu.roll(left, 1, axis=1)
        around = with_row(edge, 2.0 * above[0:1], True) + with_row(edge, 2.0 * below[0:1], False)
        west = jnp.where(odd, MIX * (edge + left + around), left)
        edge = pltpu.roll(right, lanes - 1, axis=1)
        around = with_row(edge, 2.0 * above[lanes - 1 :], True) + with_row(edge, 2.0 * below[lanes - 1 :], False)
        east = jnp.where(odd, right, MIX * (edge + right + around))
        to_g[field] = jnp.where(even_col, east, west).astype(BF16)
        to_x[field] = jnp.where(even_col, west, east).astype(BF16)


def make_strips(got_a, got_b, own_left, own_right):
    vmem = pl.BlockSpec(memory_space=pltpu.VMEM)
    out = jax.ShapeDtypeStruct(own_left.shape, BF16)
    return pl.pallas_call(
        strips_kernel,
        in_specs=[vmem] * 4,
        out_specs=[vmem] * 2,
        out_shape=[out, out],
        compiler_params=pltpu.CompilerParams(vmem_limit_bytes=BIG),
        name="strips",
    )(got_a, got_b, own_left, own_right)


def side_strips(field, got_g, got_x, own_left, own_right):
    _, even_col, _, _, has_left, has_right = grid_place()
    rows, lanes = got_g.shape[1], got_g.shape[2]
    from_g, from_x = got_g[field].astype(F32), got_x[field].astype(F32)
    west = jnp.where(even_col, from_x, from_g) * has_left
    east = jnp.where(even_col, from_g, from_x) * has_right
    next_west = pltpu.roll(west + MIX * own_left[field], 1, axis=1) * has_left
    next_east = pltpu.roll(east + MIX * own_right[field], lanes - 1, axis=1) * has_right
    odd = (lax.broadcasted_iota(jnp.int32, (rows, lanes), 1) & 1) == 1
    return jnp.where(odd, west, east), jnp.where(odd, next_west, next_east)


def row_halo(got_a, got_b):
    even_row, _, has_top, has_low, _, _ = grid_place()
    from_a, from_b = got_a[...].astype(F32), got_b[...].astype(F32)
    top = jnp.where(even_row, from_b, from_a) * has_top
    low = jnp.where(even_row, from_a, from_b) * has_low
    lanes = top.shape[1] // 2
    return top[:, :lanes], top[:, lanes:], low[:, :lanes], low[:, lanes:]


def sides_of_row(row):
    lanes = row.shape[1]
    lane = lax.broadcasted_iota(jnp.int32, row.shape, 1)
    from_left = jnp.where(lane == 0, 0.0, pltpu.roll(row, 1, axis=1))
    from_right = jnp.where(lane == lanes - 1, 0.0, pltpu.roll(row, lanes - 1, axis=1))
    return from_left + from_right


def substep(block, above, below, sides):
    lanes = block.shape[1]
    lane = lax.broadcasted_iota(jnp.int32, block.shape, 1)
    from_left = jnp.where(lane == 0, sides, pltpu.roll(block, 1, axis=1))
    from_right = jnp.where(lane == lanes - 1, sides, pltpu.roll(block, lanes - 1, axis=1))
    around = with_row(block, above, True) + with_row(block, below, False)
    return MIX * (block + around + (from_left + from_right))


def next_rows(top1, top2, low1, low2):
    return MIX * (top1 + top2 + sides_of_row(top1)), MIX * (low1 + low2 + sides_of_row(low1))


def mixed_level(block, top, next_top, low, next_low, sides0, sides1):
    rows = block.shape[0]
    _, _, has_top, has_low, _, _ = grid_place()
    once = substep(block, top, low, sides0)
    next_top = next_top + has_top * MIX * block[0:1]
    next_low = next_low + has_low * MIX * block[rows - 1 : rows]
    return substep(once, next_top, next_low, sides1)


def forward_kernel(
    owner, block_row, block_column, air, forcing, surface_temp, got_a, got_b, got_g, got_x,
    own_left, own_right, weight, payload, slots, source, held, sem, flux_rows, found, tags, counts,
    bound, levels, group,
):
    blocks = weight.shape[0]
    rows, lanes = surface_temp.shape
    devices = payload.shape[0]
    total = devices * bound
    copies = fetch(weight, held, sem)
    top1, top2, low1, low2 = [jnp.concatenate([h[0:1], h[levels : levels + 1]]) for h in row_halo(got_a, got_b)]
    next_top, next_low = next_rows(top1, top2, low1, low2)
    lowest = []
    for field in range(2):
        sides0, sides1 = side_strips(field, got_g, got_x, own_left, own_right)
        lowest.append(
            mixed_level(
                air[field, 0],
                *[h[field : field + 1] for h in (top1, next_top, low1, next_low)],
                pltpu.roll(sides0, lanes - 1, axis=1),
                pltpu.roll(sides1, lanes - 1, axis=1),
            )
        )
    u, v = forcing[0], forcing[1]
    ts = surface_temp[...]
    speed = jnp.sqrt(u * u + v * v + 1.0)
    fluxes = [
        speed * (ts - lowest[0]),
        speed * (0.5 * ts - lowest[1]),
        speed * u,
        speed * v,
        forcing[2],
        forcing[3] - 0.3 * ts,
        forcing[4],
        forcing[5],
    ]
    source[0] = fluxes[0]
    source[1] = fluxes[1]
    for field in range(NF):
        flux_rows[pl.ds(field, rows, stride=NF), :] = fluxes[field]
    if total > blocks:
        tags[...] = jnp.full_like(tags, -1.0)
        found[...] = jnp.zeros_like(found)

    def clear(i, _):
        counts[i] = 0
        return 0

    lax.fori_loop(0, devices, clear, 0)

    def some(first):
        outs = []
        for k in range(0, group, 2):
            at = first + k
            picked = [
                flux_rows[pl.ds(pl.multiple_of(block_column[n] * NF, NF), NF), :] for n in (at, at + 1)
            ]
            out = lax.dot_general(
                jnp.concatenate(picked).astype(BF16),
                held[pl.ds(at, 2)].reshape(2 * lanes, lanes),
                (((1,), (1,)), ((), ())),
                preferred_element_type=F32,
            )
            outs += [out[:NF, :lanes], out[NF:, lanes:]]
        for k, out in enumerate(outs):
            at = first + k
            to = owner[at]
            rank = counts[to]
            counts[to] = rank + 1
            slot = to * bound + rank
            slots[at] = slot
            found[pl.ds(pl.multiple_of(slot * NF, NF), NF), :] = out
            tags[pl.ds(slot, 1), :] = jnp.full((1, lanes), block_row[at], jnp.int32).astype(F32)

    per_chunk(copies, blocks, group, some)
    f = [found[pl.ds(k, total, stride=NF), :] for k in range(NF)]
    heat = (f[0] + f[1]) + (f[4] + f[5])
    heat_hi = heat.astype(BF16).astype(F32)
    lane = lax.broadcasted_iota(jnp.int32, (total, lanes), 1)
    heat_lo = jnp.where(lane == 0, tags[...], heat - heat_hi)
    shape = payload.shape[:2] + (lanes,)
    for k, part in enumerate((heat_hi, heat_lo, f[2], f[3], f[6] - f[7])):
        payload[:, :, k * lanes : (k + 1) * lanes] = part.reshape(shape).astype(BF16)


def fetch(source, held, sem):
    parts = sem.shape[0]
    size = source.shape[0] // parts
    copies = []
    for i in range(parts):
        at = pl.ds(i * size, size)
        copies.append(pltpu.make_async_copy(source.at[at], held.at[at], sem.at[i]))
        copies[i].start()
    return copies


def per_chunk(copies, blocks, group, some):
    size = blocks // len(copies)
    for i, copy in enumerate(copies):
        copy.wait()

        def body(g, carry, start=i * size):
            some(start + g * group)
            return carry

        lax.fori_loop(0, size // group, body, 0)


def forward(owner, block_row, block_column, air, forcing, surface_temp, halo, own, weight, devices, bound):
    _, levels, rows, lanes = air.shape
    nonzeros = weight.shape[0]
    smem = pl.BlockSpec(memory_space=pltpu.SMEM)
    vmem = pl.BlockSpec(memory_space=pltpu.VMEM)
    args = (forcing, surface_temp, *halo, *own)
    total = devices * bound
    return pl.pallas_call(
        functools.partial(forward_kernel, bound=bound, levels=levels, group=32),
        grid=(1,),
        in_specs=[smem, smem, smem]
        + [pl.BlockSpec((2, 1, rows, lanes), lambda i: (0, 0, 0, 0))]
        + [vmem for x in args]
        + [pl.BlockSpec(memory_space=pl.ANY)],
        out_specs=[vmem, smem, vmem],
        out_shape=[
            jax.ShapeDtypeStruct((devices, bound, SENT * lanes), BF16),
            jax.ShapeDtypeStruct((nonzeros,), jnp.int32),
            jax.ShapeDtypeStruct((2, rows, lanes), F32),
        ],
        scratch_shapes=[
            pltpu.VMEM(weight.shape, BF16),
            pltpu.SemaphoreType.DMA((PARTS,)),
            pltpu.VMEM((rows * NF, lanes), F32),
            pltpu.VMEM((total * NF, lanes), F32),
            pltpu.VMEM((total, lanes), F32),
            pltpu.SMEM((devices,), jnp.int32),
        ],
        compiler_params=pltpu.CompilerParams(vmem_limit_bytes=BIG),
        name="forward_blocks",
    )(owner, block_row, block_column, air, *args, weight)


def pivot_kernel(coupling, inverse, held, sem):
    levels = inverse.shape[0]
    copies = fetch_levels([(coupling, held)], sem, levels - 1)

    def one(level, ratio, last=False):
        below = held[level - 1]
        diagonal = 1.0 + below
        if not last:
            diagonal = diagonal + held[level]
        inv = 1.0 / (diagonal - below * ratio)
        inverse[level] = inv
        return inv if last else held[level] * inv

    for i, part in enumerate(copies):
        for c in part:
            c.wait()
        if i == 0:
            inv = 1.0 / (1.0 + held[0])
            inverse[0] = inv
            ratio = held[0] * inv
        start = max(1, i * STEP)
        stop = min((i + 1) * STEP, levels - 1)
        ratio = lax.fori_loop(start, stop, one, ratio)
    one(levels - 1, ratio, True)


def fetch_levels(pairs, sem, levels, order=1):
    copies = []
    starts = list(range(0, levels, STEP))[::order]
    for i, start in enumerate(starts):
        part = []
        for k, (source, held) in enumerate(pairs):
            at = pl.ds(start, min(STEP, source.shape[-3] - start))
            if len(source.shape) == 4:
                part.append(pltpu.make_async_copy(source.at[:, at], held.at[:, at], sem.at[k * len(starts) + i]))
            else:
                part.append(pltpu.make_async_copy(source.at[at], held.at[at], sem.at[k * len(starts) + i]))
        for c in part:
            c.start()
        copies.append(part)
    return copies


def pivots(coupling):
    levels, rows, lanes = coupling.shape
    shape = (levels + 1, rows, lanes)
    return pl.pallas_call(
        pivot_kernel,
        in_specs=[pl.BlockSpec(memory_space=pl.ANY)],
        out_specs=pl.BlockSpec(memory_space=pltpu.VMEM),
        out_shape=jax.ShapeDtypeStruct(shape, F32),
        scratch_shapes=[pltpu.VMEM(coupling.shape, F32), pltpu.SemaphoreType.DMA(((levels + STEP) // STEP,))],
        compiler_params=pltpu.CompilerParams(vmem_limit_bytes=BIG),
        cost_estimate=pl.CostEstimate(flops=8 * coupling.size, bytes_accessed=8 * coupling.size, transcendentals=0),
        name="pivots",
    )(coupling)


def beside(block, shifts):
    high = block.astype(BF16)
    low = (block - high.astype(F32)).astype(BF16)
    return jnp.dot(jnp.concatenate([high, low], axis=1), shifts, preferred_element_type=F32)


def stepped(block, above, below, inside, sides, edge):
    around = with_row(block, above, True) + with_row(block, below, False)
    return MIX * (block + around + (inside + jnp.where(edge, sides, 0.0)))


def up_kernel(
    air, coupling, inverse, got_a, got_b, got_g, got_x, own_left, own_right, source, reduced,
    held, held_c, held_i, done, halo_rows, strips, shifts, inside, once, sem, out_sem,
):
    fields, levels, rows, lanes = air.shape
    copies = fetch_levels([(air, held), (inverse, held_i), (coupling, held_c)], sem, levels)
    _, _, has_top, has_low, _, _ = grid_place()
    halo = row_halo(got_a, got_b)
    for k, h in enumerate((halo[0], halo[2], *next_rows(*halo))):
        halo_rows[k] = h
    for field in range(fields):
        sides0, sides1 = side_strips(field, got_g, got_x, own_left, own_right)
        strips[field, 0] = sides0
        strips[field, 1] = sides1
    row = lax.broadcasted_iota(jnp.int32, (2 * lanes, lanes), 0) % lanes
    column = lax.broadcasted_iota(jnp.int32, (2 * lanes, lanes), 1)
    shifts[...] = jnp.where(jnp.abs(row - column) == 1, 1.0, 0.0).astype(BF16)
    lane = lax.broadcasted_iota(jnp.int32, (rows, lanes), 1)
    edge = (lane == 0) | (lane == lanes - 1)
    groups = levels // GROUP
    members = [(field, k) for k in range(GROUP) for field in range(fields)]

    def place(k, field):
        return slice((k * fields + field) * rows, (k * fields + field + 1) * rows)

    def first_inside(g):
        block = jnp.concatenate([held[field, g * GROUP + k] for field, k in members])
        inside[0, g % 2] = beside(block, shifts[...])

    def first_step(g):
        for field, k in members:
            level = g * GROUP + k
            at = field * levels + level
            sides = pltpu.roll(strips[field, 0], (2 * lanes - 1 - 2 * level) % lanes, axis=1)
            once[g % 2, place(k, field)] = stepped(
                held[field, level], halo_rows[0, at : at + 1], halo_rows[1, at : at + 1],
                inside[0, g % 2, place(k, field)], sides, edge,
            )
        inside[1, g % 2] = beside(once[g % 2], shifts[...])

    def second_step(g):
        for field, k in members:
            level = g * GROUP + k
            at = field * levels + level
            sides = pltpu.roll(strips[field, 1], (2 * lanes - 1 - 2 * level) % lanes, axis=1)
            top = halo_rows[2, at : at + 1] + has_top * MIX * held[field, level, 0:1]
            low = halo_rows[3, at : at + 1] + has_low * MIX * held[field, level, rows - 1 : rows]
            right = stepped(
                once[g % 2, place(k, field)], top, low, inside[1, g % 2, place(k, field)], sides, edge
            )
            if level == 0:
                right = right + SURFACE_STEP * source[field]
            else:
                right = right + held_c[level - 1] * done[field, level - 1]
            done[field, level] = right * held_i[level]

    outs = []
    for g in range(groups + 2):
        if g < groups:
            if g * GROUP % STEP == 0:
                for c in copies[g * GROUP // STEP]:
                    c.wait()
            first_inside(g)
        if 0 <= g - 1 < groups:
            first_step(g - 1)
        if g >= 2:
            second_step(g - 2)
            end = (g - 1) * GROUP
            if end % STEP == 0:
                at = pl.ds(end - STEP, STEP)
                outs.append(pltpu.make_async_copy(done.at[:, at], reduced.at[:, at], out_sem.at[end // STEP - 1]))
                outs[-1].start()
    for c in outs:
        c.wait()


def columns_up(air, coupling, inverse, halo, own, source):
    fields, levels, rows, lanes = air.shape
    args = (air, coupling, inverse, *halo, *own, source)
    hbm = pl.BlockSpec(memory_space=pl.ANY)
    parts = levels // STEP
    return pl.pallas_call(
        up_kernel,
        in_specs=[hbm] * 3 + [pl.BlockSpec(memory_space=pltpu.VMEM)] * (len(args) - 3),
        out_specs=hbm,
        out_shape=jax.ShapeDtypeStruct(air.shape, F32),
        scratch_shapes=[
            pltpu.VMEM(air.shape, F32),
            pltpu.VMEM(coupling.shape, F32),
            pltpu.VMEM(inverse.shape, F32),
            pltpu.VMEM(air.shape, F32),
            pltpu.VMEM((4, fields * levels, lanes), F32),
            pltpu.VMEM((fields, 2, rows, lanes), F32),
            pltpu.VMEM((2 * lanes, lanes), BF16),
            pltpu.VMEM((2, 2, GROUP * fields * rows, lanes), F32),
            pltpu.VMEM((2, GROUP * fields * rows, lanes), F32),
            pltpu.SemaphoreType.DMA((3 * parts,)),
            pltpu.SemaphoreType.DMA((parts,)),
        ],
        compiler_params=pltpu.CompilerParams(vmem_limit_bytes=BIG),
        cost_estimate=pl.CostEstimate(flops=40 * air.size, bytes_accessed=12 * air.size, transcendentals=0),
        name="columns_up",
    )(*args)


def down_kernel(reduced, coupling, inverse, air_new, held, held_c, held_i, sem, out_sem):
    _, levels, rows, lanes = reduced.shape
    copies = fetch_levels([(reduced, held), (inverse, held_i), (coupling, held_c)], sem, levels, -1)
    outs = []
    for i, part in enumerate(copies):
        for c in part:
            c.wait()
        top = levels - 1 - i * STEP

        def one(k, _, top=top):
            level = top - k
            ratio = held_c[level] * held_i[level]
            for field in range(2):
                held[field, level] = held[field, level] + ratio * held[field, level + 1]
            return 0

        lax.fori_loop(1 if i == 0 else 0, STEP, one, 0)
        at = pl.ds(levels - (i + 1) * STEP, STEP)
        outs.append(pltpu.make_async_copy(held.at[:, at], air_new.at[:, at], out_sem.at[i]))
        outs[i].start()
    for c in outs:
        c.wait()


def columns_down(reduced, coupling, inverse):
    levels = reduced.shape[1]
    hbm = pl.BlockSpec(memory_space=pl.ANY)
    parts = levels // STEP
    return pl.pallas_call(
        down_kernel,
        in_specs=[hbm] * 3,
        out_specs=hbm,
        out_shape=jax.ShapeDtypeStruct(reduced.shape, F32),
        scratch_shapes=[
            pltpu.VMEM(reduced.shape, F32),
            pltpu.VMEM(coupling.shape, F32),
            pltpu.VMEM(inverse.shape, F32),
            pltpu.SemaphoreType.DMA((3 * parts,)),
            pltpu.SemaphoreType.DMA((parts,)),
        ],
        compiler_params=pltpu.CompilerParams(vmem_limit_bytes=BIG),
        cost_estimate=pl.CostEstimate(flops=8 * reduced.size, bytes_accessed=12 * reduced.size, transcendentals=0),
        name="columns_down",
    )(reduced, coupling, inverse)


def ocean_kernel(arrived, land_mask, ocean_temp, ocean_ice, layer_depth, temp_new, ice_new, replies):
    blocks, lanes = ocean_temp.shape
    total = arrived.shape[0] * arrived.shape[1]
    wide = arrived.shape[2]
    block = arrived[...].astype(F32).reshape(total, wide)
    lane = lax.broadcasted_iota(jnp.int32, (total, wide), 1)
    tag = block[:, lanes : lanes + 1].astype(jnp.int32)
    block = jnp.where(lane == lanes, 0.0, block).astype(BF16)
    slot_of = (tag == lax.broadcasted_iota(jnp.int32, (total, blocks), 1)).astype(F32).astype(BF16)
    sums = lax.dot_general(slot_of, block, (((0,), (0,)), ((), ())), preferred_element_type=F32)
    sums = [sums[:, k * lanes : (k + 1) * lanes] for k in range(SENT)]
    heat = sums[0] + sums[1]
    stress = sums[2] * sums[2] + sums[3] * sums[3]
    wet = land_mask[...].astype(F32)
    temp = ocean_temp[...]
    temp = temp + wet * (0.3 * heat / layer_depth[...] - 0.01 * stress * temp)
    ice = jnp.clip(ocean_ice[...] - wet * 0.05 * (heat + sums[4]), 0.0, 1.0)
    temp_new[...] = temp
    ice_new[...] = ice
    pair = jnp.concatenate([temp, ice], axis=1).astype(BF16)
    answer = jnp.dot(slot_of, pair, preferred_element_type=F32)
    replies[...] = answer.reshape(replies.shape).astype(BF16)


def ocean(arrived, land_mask, ocean_temp, ocean_ice, layer_depth):
    devices, bound, _ = arrived.shape
    blocks, lanes = ocean_temp.shape
    vmem = pl.BlockSpec(memory_space=pltpu.VMEM)
    return pl.pallas_call(
        ocean_kernel,
        in_specs=[vmem] * 5,
        out_specs=[vmem] * 3,
        out_shape=[
            jax.ShapeDtypeStruct((blocks, lanes), F32),
            jax.ShapeDtypeStruct((blocks, lanes), F32),
            jax.ShapeDtypeStruct((devices, bound, 2 * lanes), BF16),
        ],
        compiler_params=pltpu.CompilerParams(vmem_limit_bytes=BIG),
        name="ocean",
    )(arrived, land_mask, ocean_temp, ocean_ice, layer_depth)


def backward_kernel(slots, block_column, returned, weight, seen, held, sem, pairs, sums, group):
    blocks, lanes = weight.shape[0], weight.shape[1]
    total = returned.shape[0] * returned.shape[1]
    rows = seen.shape[1]
    copies = fetch(weight, held, sem)
    pairs[...] = jnp.zeros_like(pairs)
    sums[...] = jnp.zeros_like(sums)
    for k in range(2):
        part = returned[:, :, k * lanes : (k + 1) * lanes].astype(F32).reshape(total, lanes)
        pairs[pl.ds(k, total, stride=8), :] = part

    def some(first):
        outs = []
        for k in range(0, group, 2):
            at = first + k
            picked = [pairs[pl.ds(pl.multiple_of(slots[n] * 8, 8), 8), :] for n in (at, at + 1)]
            out = jnp.dot(
                jnp.concatenate(picked).astype(BF16),
                jnp.concatenate([held[at], held[at + 1]], axis=1),
                preferred_element_type=F32,
            )
            outs += [out[:8, :lanes], out[8:, lanes:]]
        for k, out in enumerate(outs):
            place = pl.ds(pl.multiple_of(block_column[first + k] * 8, 8), 8)
            sums[place, :] += out

    per_chunk(copies, blocks, group, some)
    for k in range(2):
        seen[k] = sums[pl.ds(k, rows, stride=8), :]


def backward(slots, block_column, returned, weight, rows):
    devices, bound, _ = returned.shape
    nonzeros, lanes, _ = weight.shape
    smem = pl.BlockSpec(memory_space=pltpu.SMEM)
    vmem = pl.BlockSpec(memory_space=pltpu.VMEM)
    return pl.pallas_call(
        functools.partial(backward_kernel, group=32),
        in_specs=[smem, smem, vmem, pl.BlockSpec(memory_space=pl.ANY)],
        out_specs=vmem,
        out_shape=jax.ShapeDtypeStruct((2, rows, lanes), F32),
        scratch_shapes=[
            pltpu.VMEM(weight.shape, BF16),
            pltpu.SemaphoreType.DMA((PARTS,)),
            pltpu.VMEM((devices * bound * 8, lanes), F32),
            pltpu.VMEM((rows * 8, lanes), F32),
        ],
        compiler_params=pltpu.CompilerParams(vmem_limit_bytes=BIG),
        name="backward_blocks",
    )(slots, block_column, returned, weight)


def local(
    air_state,
    coupling,
    forcing,
    surface_temp,
    remap_weight,
    block_owner,
    block_row,
    block_column,
    land_mask,
    ocean_temp,
    ocean_ice,
    layer_depth,
):
    devices = lax.axis_size("comp") * lax.axis_size("gx") * lax.axis_size("gy")
    nonzeros = remap_weight.shape[0]
    bound = max(4, (nonzeros + devices - 1) // devices)
    rows_a, rows_b = pack_rows(air_state)
    got_a = lax.ppermute(rows_a, ALL, row_swaps(0))
    got_b = lax.ppermute(rows_b, ALL, row_swaps(1))
    own = pack_cols(air_state)
    to_g, to_x = make_strips(got_a, got_b, *own)
    got_x = lax.ppermute(to_x, ("comp", "gy"), col_swaps(1))
    got_g = lax.ppermute(to_g, ("comp", "gy"), col_swaps(0))
    halo = (got_a, got_b, got_g, got_x)
    inverse = pivots(coupling)
    halo, inverse = lax.optimization_barrier((halo, inverse))
    payload, slots, source = forward(
        block_owner[:, 0], block_row, block_column, air_state, forcing, surface_temp, halo, own,
        remap_weight, devices, bound,
    )
    arrived = lax.all_to_all(payload, ALL, split_axis=0, concat_axis=0, tiled=True)
    reduced = columns_up(air_state, coupling, inverse, halo, own, source)
    arrived, reduced = lax.optimization_barrier((arrived, reduced))
    ocean_temp_new, ocean_ice_new, replies = ocean(
        arrived, land_mask, ocean_temp, ocean_ice, layer_depth
    )
    returned = lax.all_to_all(replies, ALL, split_axis=0, concat_axis=0, tiled=True)
    air_new = columns_down(reduced, coupling, inverse)
    returned, air_new = lax.optimization_barrier((returned, air_new))
    surface_seen = backward(slots, block_column, returned, remap_weight, surface_temp.shape[0])
    return (air_new, surface_seen, ocean_temp_new, ocean_ice_new)


def solution(mesh):
    in_specs = (
        P(None, None, "gx", ("comp", "gy")),
        P(None, "gx", ("comp", "gy")),
        P(None, "gx", ("comp", "gy")),
        P("gx", ("comp", "gy")),
        P(ALL, None, None),
        P(ALL, None),
        P(ALL),
        P(ALL),
        P(ALL, None),
        P(ALL, None),
        P(ALL, None),
        P(ALL, None),
    )
    out_specs = (
        P(None, None, "gx", ("comp", "gy")),
        P(None, "gx", ("comp", "gy")),
        P(ALL, None),
        P(ALL, None),
    )
    return jax.shard_map(local, mesh=mesh, in_specs=in_specs, out_specs=out_specs, check_vma=False)
```

```python
import functools

import jax
import jax.numpy as jnp
from jax import lax
from jax.experimental import pallas as pl
from jax.experimental.pallas import tpu as pltpu
from jax.sharding import PartitionSpec as P

F32 = jnp.float32
BF16 = jnp.bfloat16
ALL = ("comp", "gx", "gy")
NF = 8
SENT = 5
SURFACE_STEP = 0.5
MIX = 0.2
MIB = 1 << 20
PARTS = 8
STEP = 8
GROUP = 4


def in_vmem(*arrays):
    return [pltpu.with_memory_space_constraint(x, pltpu.VMEM) for x in arrays]


def in_hbm(*arrays):
    return [pltpu.with_memory_space_constraint(x, pltpu.HBM) for x in arrays]


def row_swaps(first):
    n_gx, n_gy = lax.axis_size("gx"), lax.axis_size("gy")
    pairs = []
    for comp in range(lax.axis_size("comp")):
        for gx in range(n_gx):
            for gy in range(n_gy):
                other = gx + 1 if (gx - first) % 2 == 0 else gx - 1
                to, core = (other, gy) if 0 <= other < n_gx else (gx, gy ^ 1)
                pairs.append(((comp * n_gx + gx) * n_gy + gy, (comp * n_gx + to) * n_gy + core))
    return pairs


def col_swaps(first):
    count = lax.axis_size("comp") * lax.axis_size("gy")
    return [(i, (i + 1 if (i - first) % 2 == 0 else i - 1) % count) for i in range(count)]


def grid_place():
    gx, n_gx = lax.axis_index("gx"), lax.axis_size("gx")
    c = lax.axis_index("comp") * lax.axis_size("gy") + lax.axis_index("gy")
    n_c = lax.axis_size("comp") * lax.axis_size("gy")
    there = lambda yes: jnp.where(yes, 1.0, 0.0).astype(F32)
    return gx % 2 == 0, c % 2 == 0, there(gx > 0), there(gx < n_gx - 1), there(c > 0), there(c < n_c - 1)


def rows_kernel(air, rows_a, rows_b, first, last, sem):
    even_row = grid_place()[0]
    count, tile, lanes = first.shape
    rows = air.shape[1]
    copies = [
        pltpu.make_async_copy(air.at[:, pl.ds(0, tile)], first, sem.at[0]),
        pltpu.make_async_copy(air.at[:, pl.ds(rows - tile, tile)], last, sem.at[1]),
    ]
    for c in copies:
        c.start()
    for c in copies:
        c.wait()
    first, last = [x.reshape(count * tile, lanes) for x in (first, last)]
    for k in range(2):
        low, high = first[pl.ds(k, count, stride=tile), :], last[pl.ds(tile - 1 - k, count, stride=tile), :]
        to = slice(k * lanes, (k + 1) * lanes)
        rows_a[:, to] = jnp.where(even_row, high, low).astype(BF16)
        rows_b[:, to] = jnp.where(even_row, low, high).astype(BF16)


def pack_rows(air):
    fields, levels, rows, lanes = air.shape
    out = jax.ShapeDtypeStruct((fields * levels, 2 * lanes), BF16)
    edge = pltpu.VMEM((fields * levels, 8, lanes), F32)
    return pl.pallas_call(
        rows_kernel,
        in_specs=[pl.BlockSpec(memory_space=pltpu.HBM)],
        out_specs=[pl.BlockSpec(memory_space=pltpu.VMEM)] * 2,
        out_shape=[out, out],
        scratch_shapes=[edge, edge, pltpu.SemaphoreType.DMA((2,))],
        compiler_params=pltpu.CompilerParams(vmem_limit_bytes=8 * MIB),
        name="pack_rows",
    )(*in_hbm(air.reshape(fields * levels, rows, lanes)))


def cols_kernel(air, weight, own_left, own_right, lowest, first_half, held, sem, sem_w, chunk):
    fields, levels, rows, lanes = air.shape
    copies = []
    for i in range(levels // chunk):
        part = pl.ds(i * chunk, chunk)
        copies.append(pltpu.make_async_copy(air.at[:, part], held.at[:, part], sem.at[i]))
        copies[i].start()
    weights = fetch(weight.at[pl.ds(0, first_half.shape[0])], first_half, sem_w)
    pair = lax.broadcasted_iota(jnp.int32, (rows, lanes), 1) >> 1
    left, right = [[jnp.zeros((rows, lanes), F32)] * fields for _ in range(2)]
    for i in range(levels // chunk):
        copies[i].wait()
        if i == 0:
            lowest[...] = held[:, 0]
        for level in range(i * chunk, (i + 1) * chunk):
            for field in range(fields):
                turned = pltpu.roll(held[field, level], 2 * level % lanes, axis=1)
                left[field] = jnp.where(pair == level, turned, left[field])
                right[field] = jnp.where(pair == (level - 1) % levels, turned, right[field])
    for field in range(fields):
        own_left[field] = left[field]
        own_right[field] = pltpu.roll(right[field], 2, axis=1)
    for c in weights:
        c.wait()


def pack_cols(air, weight):
    fields, levels, rows, lanes = air.shape
    chunk = 8
    vmem = pl.BlockSpec(memory_space=pltpu.VMEM)
    out = jax.ShapeDtypeStruct((fields, rows, lanes), F32)
    return pl.pallas_call(
        functools.partial(cols_kernel, chunk=chunk),
        in_specs=[pl.BlockSpec(memory_space=pltpu.HBM)] * 2,
        out_specs=[vmem] * 4,
        out_shape=[out, out, out, pltpu.VMEM((weight.shape[0] // 2, lanes, lanes), BF16)],
        scratch_shapes=[
            pltpu.VMEM(air.shape, F32),
            pltpu.SemaphoreType.DMA((levels // chunk,)),
            pltpu.SemaphoreType.DMA((PARTS,)),
        ],
        compiler_params=pltpu.CompilerParams(vmem_limit_bytes=12 * MIB),
        cost_estimate=pl.CostEstimate(flops=4 * air.size, bytes_accessed=4 * air.size, transcendentals=0),
        name="pack_cols",
    )(*in_hbm(air, weight))


def with_row(strip, row, first):
    rows = strip.shape[0]
    index = lax.broadcasted_iota(jnp.int32, strip.shape, 0)
    if first:
        return jnp.where(index == 0, row, pltpu.roll(strip, 1, axis=0))
    return jnp.where(index == rows - 1, row, pltpu.roll(strip, rows - 1, axis=0))


def strips_kernel(got_a, got_b, own_left, own_right, to_g, to_x):
    even_col = grid_place()[1]
    fields, rows, lanes = own_left.shape
    top, _, low, _ = row_halo(got_a, got_b)
    levels = top.shape[0] // fields
    level = lax.broadcasted_iota(jnp.int32, (levels, lanes), 0)
    pair = lax.broadcasted_iota(jnp.int32, (levels, lanes), 1) >> 1
    spread = jnp.where(level == pair, 1.0, 0.0).astype(BF16)
    odd = (lax.broadcasted_iota(jnp.int32, (rows, lanes), 1) & 1) == 1
    for field in range(fields):
        at = slice(field * levels, (field + 1) * levels)
        above, below = [
            lax.dot_general(h[at].astype(BF16), spread, (((0,), (0,)), ((), ())), preferred_element_type=F32)
            for h in (top, low)
        ]
        left, right = own_left[field], own_right[field]
        edge = pltpu.roll(left, 1, axis=1)
        around = with_row(edge, 2.0 * above[0:1], True) + with_row(edge, 2.0 * below[0:1], False)
        west = jnp.where(odd, MIX * (edge + left + around), left)
        edge = pltpu.roll(right, lanes - 1, axis=1)
        around = with_row(edge, 2.0 * above[lanes - 1 :], True) + with_row(edge, 2.0 * below[lanes - 1 :], False)
        east = jnp.where(odd, right, MIX * (edge + right + around))
        to_g[field] = jnp.where(even_col, east, west).astype(BF16)
        to_x[field] = jnp.where(even_col, west, east).astype(BF16)


def make_strips(got_a, got_b, own_left, own_right):
    vmem = pl.BlockSpec(memory_space=pltpu.VMEM)
    out = jax.ShapeDtypeStruct(own_left.shape, BF16)
    return pl.pallas_call(
        strips_kernel,
        in_specs=[vmem] * 4,
        out_specs=[vmem] * 2,
        out_shape=[out, out],
        compiler_params=pltpu.CompilerParams(vmem_limit_bytes=8 * MIB),
        name="strips",
    )(got_a, got_b, own_left, own_right)


def side_strips(field, got_g, got_x, own_left, own_right):
    _, even_col, _, _, has_left, has_right = grid_place()
    rows, lanes = got_g.shape[1], got_g.shape[2]
    from_g, from_x = got_g[field].astype(F32), got_x[field].astype(F32)
    west = jnp.where(even_col, from_x, from_g) * has_left
    east = jnp.where(even_col, from_g, from_x) * has_right
    next_west = pltpu.roll(west + MIX * own_left[field], 1, axis=1) * has_left
    next_east = pltpu.roll(east + MIX * own_right[field], lanes - 1, axis=1) * has_right
    odd = (lax.broadcasted_iota(jnp.int32, (rows, lanes), 1) & 1) == 1
    return jnp.where(odd, west, east), jnp.where(odd, next_west, next_east)


def row_halo(got_a, got_b):
    even_row, _, has_top, has_low, _, _ = grid_place()
    from_a, from_b = got_a[...].astype(F32), got_b[...].astype(F32)
    top = jnp.where(even_row, from_b, from_a) * has_top
    low = jnp.where(even_row, from_a, from_b) * has_low
    lanes = top.shape[1] // 2
    return top[:, :lanes], top[:, lanes:], low[:, :lanes], low[:, lanes:]


def sides_of_row(row):
    lanes = row.shape[1]
    lane = lax.broadcasted_iota(jnp.int32, row.shape, 1)
    from_left = jnp.where(lane == 0, 0.0, pltpu.roll(row, 1, axis=1))
    from_right = jnp.where(lane == lanes - 1, 0.0, pltpu.roll(row, lanes - 1, axis=1))
    return from_left + from_right


def substep(block, above, below, sides):
    lanes = block.shape[1]
    lane = lax.broadcasted_iota(jnp.int32, block.shape, 1)
    from_left = jnp.where(lane == 0, sides, pltpu.roll(block, 1, axis=1))
    from_right = jnp.where(lane == lanes - 1, sides, pltpu.roll(block, lanes - 1, axis=1))
    around = with_row(block, above, True) + with_row(block, below, False)
    return MIX * (block + around + (from_left + from_right))


def next_rows(top1, top2, low1, low2):
    return MIX * (top1 + top2 + sides_of_row(top1)), MIX * (low1 + low2 + sides_of_row(low1))


def mixed_level(block, top, next_top, low, next_low, sides0, sides1):
    rows = block.shape[0]
    _, _, has_top, has_low, _, _ = grid_place()
    once = substep(block, top, low, sides0)
    next_top = next_top + has_top * MIX * block[0:1]
    next_low = next_low + has_low * MIX * block[rows - 1 : rows]
    return substep(once, next_top, next_low, sides1)


def forward_kernel(
    owner, block_row, block_column, air, forcing, surface_temp, got_a, got_b, got_g, got_x,
    own_left, own_right, first_half, weight, payload, slots, source, held, sem, flux_rows, found, tags,
    counts,
    bound, levels, group,
):
    blocks = weight.shape[0]
    rows, lanes = surface_temp.shape
    devices = payload.shape[0]
    total = devices * bound
    half = held.shape[0]
    copies = fetch(weight.at[pl.ds(half, half)], held, sem)
    top1, top2, low1, low2 = [jnp.concatenate([h[0:1], h[levels : levels + 1]]) for h in row_halo(got_a, got_b)]
    next_top, next_low = next_rows(top1, top2, low1, low2)
    lowest = []
    for field in range(2):
        sides0, sides1 = side_strips(field, got_g, got_x, own_left, own_right)
        lowest.append(
            mixed_level(
                air[field],
                *[h[field : field + 1] for h in (top1, next_top, low1, next_low)],
                pltpu.roll(sides0, lanes - 1, axis=1),
                pltpu.roll(sides1, lanes - 1, axis=1),
            )
        )
    u, v = forcing[0], forcing[1]
    ts = surface_temp[...]
    speed = jnp.sqrt(u * u + v * v + 1.0)
    fluxes = [
        speed * (ts - lowest[0]),
        speed * (0.5 * ts - lowest[1]),
        speed * u,
        speed * v,
        forcing[2],
        forcing[3] - 0.3 * ts,
        forcing[4],
        forcing[5],
    ]
    source[0] = fluxes[0]
    source[1] = fluxes[1]
    for field in range(NF):
        flux_rows[pl.ds(field, rows, stride=NF), :] = fluxes[field]
    if total > blocks:
        tags[...] = jnp.full_like(tags, -1.0)
        found[...] = jnp.zeros_like(found)

    def clear(i, _):
        counts[i] = 0
        return 0

    lax.fori_loop(0, devices, clear, 0)

    def some(first, start, half):
        outs = []
        for k in range(0, group, 2):
            at = start + first + k
            picked = [
                flux_rows[pl.ds(pl.multiple_of(block_column[n] * NF, NF), NF), :] for n in (at, at + 1)
            ]
            out = lax.dot_general(
                jnp.concatenate(picked).astype(BF16),
                half[pl.ds(first + k, 2)].reshape(2 * lanes, lanes),
                (((1,), (1,)), ((), ())),
                preferred_element_type=F32,
            )
            outs += [out[:NF, :lanes], out[NF:, lanes:]]
        for k, out in enumerate(outs):
            at = start + first + k
            to = owner[at]
            rank = counts[to]
            counts[to] = rank + 1
            slot = to * bound + rank
            slots[at] = slot
            found[pl.ds(pl.multiple_of(slot * NF, NF), NF), :] = out
            tags[pl.ds(slot, 1), :] = jnp.full((1, lanes), block_row[at], jnp.int32).astype(F32)

    all_of(first_half, 0, group, some)
    for c in copies:
        c.wait()
    all_of(held, half, group, some)
    f = [found[pl.ds(k, total, stride=NF), :] for k in range(NF)]
    heat = (f[0] + f[1]) + (f[4] + f[5])
    heat_hi = heat.astype(BF16).astype(F32)
    lane = lax.broadcasted_iota(jnp.int32, (total, lanes), 1)
    heat_lo = jnp.where(lane == 0, tags[...], heat - heat_hi)
    shape = payload.shape[:2] + (lanes,)
    for k, part in enumerate((heat_hi, heat_lo, f[2], f[3], f[6] - f[7])):
        payload[:, :, k * lanes : (k + 1) * lanes] = part.reshape(shape).astype(BF16)


def fetch(source, held, sem):
    parts = sem.shape[0]
    size = source.shape[0] // parts
    copies = []
    for i in range(parts):
        at = pl.ds(i * size, size)
        copies.append(pltpu.make_async_copy(source.at[at], held.at[at], sem.at[i]))
        copies[i].start()
    return copies


def all_of(weight, start, group, some):
    def body(g, carry):
        some(g * group, start, weight)
        return carry

    lax.fori_loop(0, weight.shape[0] // group, body, 0)


def forward(
    owner, block_row, block_column, lowest, forcing, surface_temp, halo, own, first_half, weight, levels,
    devices, bound,
):
    _, rows, lanes = lowest.shape
    nonzeros = weight.shape[0]
    smem = pl.BlockSpec(memory_space=pltpu.SMEM)
    vmem = pl.BlockSpec(memory_space=pltpu.VMEM)
    args = (forcing, surface_temp, *halo, *own)
    total = devices * bound
    return pl.pallas_call(
        functools.partial(forward_kernel, bound=bound, levels=levels, group=32),
        in_specs=[smem, smem, smem]
        + [vmem] * (len(args) + 2)
        + [pl.BlockSpec(memory_space=pltpu.HBM)],
        out_specs=[vmem, smem, vmem],
        out_shape=[
            jax.ShapeDtypeStruct((devices, bound, SENT * lanes), BF16),
            jax.ShapeDtypeStruct((nonzeros,), jnp.int32),
            jax.ShapeDtypeStruct((2, rows, lanes), F32),
        ],
        scratch_shapes=[
            pltpu.VMEM(first_half.shape, BF16),
            pltpu.SemaphoreType.DMA((PARTS,)),
            pltpu.VMEM((rows * NF, lanes), F32),
            pltpu.VMEM((total * NF, lanes), F32),
            pltpu.VMEM((total, lanes), F32),
            pltpu.SMEM((devices,), jnp.int32),
        ],
        compiler_params=pltpu.CompilerParams(vmem_limit_bytes=20 * MIB),
        name="forward_blocks",
    )(owner, block_row, block_column, lowest, *args, *in_vmem(first_half), *in_hbm(weight))


def pivot_kernel(coupling, out, held, inverse, sem, out_sem):
    levels = inverse.shape[0]
    copies = fetch_levels([(coupling, held)], sem, levels - 1)

    def one(level, ratio, last=False):
        below = held[level - 1]
        diagonal = 1.0 + below
        if not last:
            diagonal = diagonal + held[level]
        inv = 1.0 / (diagonal - below * ratio)
        inverse[level] = inv
        return inv if last else held[level] * inv

    outs = []
    for i, part in enumerate(copies):
        for c in part:
            c.wait()
        if i == 0:
            inv = 1.0 / (1.0 + held[0])
            inverse[0] = inv
            ratio = held[0] * inv
        start = max(1, i * STEP)
        stop = min((i + 1) * STEP, levels - 1)
        ratio = lax.fori_loop(start, stop, one, ratio)
        if stop == levels - 1:
            one(levels - 1, ratio, True)
        at = pl.ds(i * STEP, STEP)
        outs.append(pltpu.make_async_copy(inverse.at[at], out.at[at], out_sem.at[i]))
        outs[i].start()
    for c in outs:
        c.wait()


def fetch_levels(pairs, sem, levels, order=1):
    copies = []
    starts = list(range(0, levels, STEP))[::order]
    for i, start in enumerate(starts):
        part = []
        for k, (source, held) in enumerate(pairs):
            at = pl.ds(start, min(STEP, source.shape[-3] - start))
            if len(source.shape) == 4:
                part.append(pltpu.make_async_copy(source.at[:, at], held.at[:, at], sem.at[k * len(starts) + i]))
            else:
                part.append(pltpu.make_async_copy(source.at[at], held.at[at], sem.at[k * len(starts) + i]))
        for c in part:
            c.start()
        copies.append(part)
    return copies


def pivots(coupling):
    levels, rows, lanes = coupling.shape
    shape = (levels + 1, rows, lanes)
    return pl.pallas_call(
        pivot_kernel,
        in_specs=[pl.BlockSpec(memory_space=pltpu.HBM)],
        out_specs=pl.BlockSpec(memory_space=pltpu.HBM),
        out_shape=pltpu.HBM(shape, F32),
        scratch_shapes=[
            pltpu.VMEM(coupling.shape, F32),
            pltpu.VMEM(shape, F32),
            pltpu.SemaphoreType.DMA(((levels + STEP) // STEP,)),
            pltpu.SemaphoreType.DMA(((levels + STEP) // STEP,)),
        ],
        compiler_params=pltpu.CompilerParams(vmem_limit_bytes=12 * MIB),
        cost_estimate=pl.CostEstimate(flops=8 * coupling.size, bytes_accessed=8 * coupling.size, transcendentals=0),
        name="pivots",
    )(*in_hbm(coupling))


def beside(block, shifts):
    high = block.astype(BF16)
    low = (block - high.astype(F32)).astype(BF16)
    return jnp.dot(jnp.concatenate([high, low], axis=1), shifts, preferred_element_type=F32)


def stepped(block, above, below, inside, sides, edge):
    around = with_row(block, above, True) + with_row(block, below, False)
    return MIX * (block + around + (inside + jnp.where(edge, sides, 0.0)))


def up_kernel(
    air, coupling, inverse, got_a, got_b, got_g, got_x, own_left, own_right, source, reduced,
    held, held_c, held_i, done, halo_rows, strips, shifts, inside, once, sem, out_sem,
):
    fields, levels, rows, lanes = air.shape
    copies = fetch_levels([(air, held), (inverse, held_i), (coupling, held_c)], sem, levels)
    _, _, has_top, has_low, _, _ = grid_place()
    halo = row_halo(got_a, got_b)
    for k, h in enumerate((halo[0], halo[2], *next_rows(*halo))):
        halo_rows[k] = h
    for field in range(fields):
        sides0, sides1 = side_strips(field, got_g, got_x, own_left, own_right)
        strips[field, 0] = sides0
        strips[field, 1] = sides1
    row = lax.broadcasted_iota(jnp.int32, (2 * lanes, lanes), 0) % lanes
    column = lax.broadcasted_iota(jnp.int32, (2 * lanes, lanes), 1)
    shifts[...] = jnp.where(jnp.abs(row - column) == 1, 1.0, 0.0).astype(BF16)
    lane = lax.broadcasted_iota(jnp.int32, (rows, lanes), 1)
    edge = (lane == 0) | (lane == lanes - 1)
    groups = levels // GROUP
    members = [(field, k) for k in range(GROUP) for field in range(fields)]

    def place(k, field):
        return slice((k * fields + field) * rows, (k * fields + field + 1) * rows)

    def first_inside(g):
        block = jnp.concatenate([held[field, g * GROUP + k] for field, k in members])
        inside[0, g % 2] = beside(block, shifts[...])

    def first_step(g):
        for field, k in members:
            level = g * GROUP + k
            at = field * levels + level
            sides = pltpu.roll(strips[field, 0], (2 * lanes - 1 - 2 * level) % lanes, axis=1)
            once[g % 2, place(k, field)] = stepped(
                held[field, level], halo_rows[0, at : at + 1], halo_rows[1, at : at + 1],
                inside[0, g % 2, place(k, field)], sides, edge,
            )
        inside[1, g % 2] = beside(once[g % 2], shifts[...])

    def second_step(g):
        for field, k in members:
            level = g * GROUP + k
            at = field * levels + level
            sides = pltpu.roll(strips[field, 1], (2 * lanes - 1 - 2 * level) % lanes, axis=1)
            top = halo_rows[2, at : at + 1] + has_top * MIX * held[field, level, 0:1]
            low = halo_rows[3, at : at + 1] + has_low * MIX * held[field, level, rows - 1 : rows]
            right = stepped(
                once[g % 2, place(k, field)], top, low, inside[1, g % 2, place(k, field)], sides, edge
            )
            if level == 0:
                right = right + SURFACE_STEP * source[field]
            else:
                right = right + held_c[level - 1] * done[field, level - 1]
            done[field, level] = right * held_i[level]

    outs = []
    for g in range(groups + 2):
        if g < groups:
            if g * GROUP % STEP == 0:
                for c in copies[g * GROUP // STEP]:
                    c.wait()
            first_inside(g)
        if 0 <= g - 1 < groups:
            first_step(g - 1)
        if g >= 2:
            second_step(g - 2)
            end = (g - 1) * GROUP
            if end % STEP == 0:
                at = pl.ds(end - STEP, STEP)
                outs.append(pltpu.make_async_copy(done.at[:, at], reduced.at[:, at], out_sem.at[end // STEP - 1]))
                outs[-1].start()
    for c in outs:
        c.wait()


def columns_up(air, coupling, inverse, halo, own, source):
    fields, levels, rows, lanes = air.shape
    args = (air, coupling, inverse, *halo, *own, source)
    hbm = pl.BlockSpec(memory_space=pltpu.HBM)
    parts = levels // STEP
    return pl.pallas_call(
        up_kernel,
        in_specs=[hbm] * 3 + [pl.BlockSpec(memory_space=pltpu.VMEM)] * (len(args) - 3),
        out_specs=hbm,
        out_shape=pltpu.HBM(air.shape, F32),
        scratch_shapes=[
            pltpu.VMEM(air.shape, F32),
            pltpu.VMEM(coupling.shape, F32),
            pltpu.VMEM(inverse.shape, F32),
            pltpu.VMEM(air.shape, F32),
            pltpu.VMEM((4, fields * levels, lanes), F32),
            pltpu.VMEM((fields, 2, rows, lanes), F32),
            pltpu.VMEM((2 * lanes, lanes), BF16),
            pltpu.VMEM((2, 2, GROUP * fields * rows, lanes), F32),
            pltpu.VMEM((2, GROUP * fields * rows, lanes), F32),
            pltpu.SemaphoreType.DMA((3 * parts,)),
            pltpu.SemaphoreType.DMA((parts,)),
        ],
        compiler_params=pltpu.CompilerParams(vmem_limit_bytes=24 * MIB),
        cost_estimate=pl.CostEstimate(flops=40 * air.size, bytes_accessed=12 * air.size, transcendentals=0),
        name="columns_up",
    )(*in_hbm(*args[:3]), *args[3:])


def down_kernel(reduced, coupling, inverse, air_new, held, held_c, held_i, sem, out_sem):
    _, levels, rows, lanes = reduced.shape
    copies = fetch_levels([(reduced, held), (inverse, held_i), (coupling, held_c)], sem, levels, -1)
    outs = []
    for i, part in enumerate(copies):
        for c in part:
            c.wait()
        top = levels - 1 - i * STEP

        def one(k, _, top=top):
            level = top - k
            ratio = held_c[level] * held_i[level]
            for field in range(2):
                held[field, level] = held[field, level] + ratio * held[field, level + 1]
            return 0

        lax.fori_loop(1 if i == 0 else 0, STEP, one, 0)
        at = pl.ds(levels - (i + 1) * STEP, STEP)
        outs.append(pltpu.make_async_copy(held.at[:, at], air_new.at[:, at], out_sem.at[i]))
        outs[i].start()
    for c in outs:
        c.wait()


def columns_down(reduced, coupling, inverse):
    levels = reduced.shape[1]
    hbm = pl.BlockSpec(memory_space=pltpu.HBM)
    parts = levels // STEP
    return pl.pallas_call(
        down_kernel,
        in_specs=[hbm] * 3,
        out_specs=hbm,
        out_shape=pltpu.HBM(reduced.shape, F32),
        scratch_shapes=[
            pltpu.VMEM(reduced.shape, F32),
            pltpu.VMEM(coupling.shape, F32),
            pltpu.VMEM(inverse.shape, F32),
            pltpu.SemaphoreType.DMA((3 * parts,)),
            pltpu.SemaphoreType.DMA((parts,)),
        ],
        compiler_params=pltpu.CompilerParams(vmem_limit_bytes=16 * MIB),
        cost_estimate=pl.CostEstimate(flops=8 * reduced.size, bytes_accessed=12 * reduced.size, transcendentals=0),
        name="columns_down",
    )(*in_hbm(reduced, coupling, inverse))


def ocean_kernel(arrived, land_mask, ocean_temp, ocean_ice, layer_depth, temp_new, ice_new, replies):
    blocks, lanes = ocean_temp.shape
    total = arrived.shape[0] * arrived.shape[1]
    wide = arrived.shape[2]
    block = arrived[...].astype(F32).reshape(total, wide)
    lane = lax.broadcasted_iota(jnp.int32, (total, wide), 1)
    tag = block[:, lanes : lanes + 1].astype(jnp.int32)
    block = jnp.where(lane == lanes, 0.0, block).astype(BF16)
    slot_of = (tag == lax.broadcasted_iota(jnp.int32, (total, blocks), 1)).astype(F32).astype(BF16)
    sums = lax.dot_general(slot_of, block, (((0,), (0,)), ((), ())), preferred_element_type=F32)
    sums = [sums[:, k * lanes : (k + 1) * lanes] for k in range(SENT)]
    heat = sums[0] + sums[1]
    stress = sums[2] * sums[2] + sums[3] * sums[3]
    wet = land_mask[...].astype(F32)
    temp = ocean_temp[...]
    temp = temp + wet * (0.3 * heat / layer_depth[...] - 0.01 * stress * temp)
    ice = jnp.clip(ocean_ice[...] - wet * 0.05 * (heat + sums[4]), 0.0, 1.0)
    temp_new[...] = temp
    ice_new[...] = ice
    pair = jnp.concatenate([temp, ice], axis=1).astype(BF16)
    answer = jnp.dot(slot_of, pair, preferred_element_type=F32)
    replies[...] = answer.reshape(replies.shape).astype(BF16)


def ocean(arrived, land_mask, ocean_temp, ocean_ice, layer_depth):
    devices, bound, _ = arrived.shape
    blocks, lanes = ocean_temp.shape
    vmem = pl.BlockSpec(memory_space=pltpu.VMEM)
    return pl.pallas_call(
        ocean_kernel,
        in_specs=[vmem] * 5,
        out_specs=[vmem] * 3,
        out_shape=[
            jax.ShapeDtypeStruct((blocks, lanes), F32),
            jax.ShapeDtypeStruct((blocks, lanes), F32),
            jax.ShapeDtypeStruct((devices, bound, 2 * lanes), BF16),
        ],
        compiler_params=pltpu.CompilerParams(vmem_limit_bytes=16 * MIB),
        name="ocean",
    )(arrived, land_mask, ocean_temp, ocean_ice, layer_depth)


def backward_kernel(slots, block_column, returned, weight, seen, held, sem, pairs, sums, group):
    lanes = weight.shape[1]
    total = returned.shape[0] * returned.shape[1]
    rows = seen.shape[1]
    copies = fetch(weight, held, sem)
    pairs[...] = jnp.zeros_like(pairs)
    sums[...] = jnp.zeros_like(sums)
    for k in range(2):
        part = returned[:, :, k * lanes : (k + 1) * lanes].astype(F32).reshape(total, lanes)
        pairs[pl.ds(k, total, stride=8), :] = part

    def some(first):
        outs = []
        for k in range(0, group, 2):
            at = first + k
            picked = [pairs[pl.ds(pl.multiple_of(slots[n] * 8, 8), 8), :] for n in (at, at + 1)]
            out = jnp.dot(
                jnp.concatenate(picked).astype(BF16),
                jnp.concatenate([held[at], held[at + 1]], axis=1),
                preferred_element_type=F32,
            )
            outs += [out[:8, :lanes], out[8:, lanes:]]
        for k, out in enumerate(outs):
            place = pl.ds(pl.multiple_of(block_column[first + k] * 8, 8), 8)
            sums[place, :] += out

    size = weight.shape[0] // PARTS
    for i, copy in enumerate(copies):
        copy.wait()

        def body(g, carry, start=i * size):
            some(start + g * group)
            return carry

        lax.fori_loop(0, size // group, body, 0)
    for k in range(2):
        seen[k] = sums[pl.ds(k, rows, stride=8), :]


def backward(slots, block_column, returned, weight, rows):
    devices, bound, _ = returned.shape
    nonzeros, lanes, _ = weight.shape
    smem = pl.BlockSpec(memory_space=pltpu.SMEM)
    vmem = pl.BlockSpec(memory_space=pltpu.VMEM)
    return pl.pallas_call(
        functools.partial(backward_kernel, group=32),
        in_specs=[smem, smem, vmem, pl.BlockSpec(memory_space=pltpu.HBM)],
        out_specs=vmem,
        out_shape=jax.ShapeDtypeStruct((2, rows, lanes), F32),
        scratch_shapes=[
            pltpu.VMEM(weight.shape, BF16),
            pltpu.SemaphoreType.DMA((PARTS,)),
            pltpu.VMEM((devices * bound * 8, lanes), F32),
            pltpu.VMEM((rows * 8, lanes), F32),
        ],
        compiler_params=pltpu.CompilerParams(vmem_limit_bytes=16 * MIB),
        name="backward_blocks",
    )(slots, block_column, returned, *in_hbm(weight))


def local(
    air_state,
    coupling,
    forcing,
    surface_temp,
    remap_weight,
    block_owner,
    block_row,
    block_column,
    land_mask,
    ocean_temp,
    ocean_ice,
    layer_depth,
):
    devices = lax.axis_size("comp") * lax.axis_size("gx") * lax.axis_size("gy")
    nonzeros = remap_weight.shape[0]
    bound = max(4, (nonzeros + devices - 1) // devices)
    rows_a, rows_b = pack_rows(air_state)
    got_a = lax.ppermute(rows_a, ALL, row_swaps(0))
    got_b = lax.ppermute(rows_b, ALL, row_swaps(1))
    *own, lowest, first_half = pack_cols(air_state, remap_weight)
    to_g, to_x = make_strips(got_a, got_b, *own)
    got_x = lax.ppermute(to_x, ("comp", "gy"), col_swaps(1))
    got_g = lax.ppermute(to_g, ("comp", "gy"), col_swaps(0))
    halo = (got_a, got_b, got_g, got_x)
    inverse = pivots(coupling)
    halo, inverse = lax.optimization_barrier((halo, inverse))
    payload, slots, source = forward(
        block_owner[:, 0], block_row, block_column, lowest, forcing, surface_temp, halo, own,
        first_half, remap_weight, air_state.shape[1], devices, bound,
    )
    arrived = lax.all_to_all(payload, ALL, split_axis=0, concat_axis=0, tiled=True)
    reduced = columns_up(air_state, coupling, inverse, halo, own, source)
    arrived, reduced = lax.optimization_barrier((arrived, reduced))
    ocean_temp_new, ocean_ice_new, replies = ocean(
        arrived, land_mask, ocean_temp, ocean_ice, layer_depth
    )
    returned = lax.all_to_all(replies, ALL, split_axis=0, concat_axis=0, tiled=True)
    air_new = columns_down(reduced, coupling, inverse)
    returned, air_new = lax.optimization_barrier((returned, air_new))
    surface_seen = backward(slots, block_column, returned, remap_weight, surface_temp.shape[0])
    return (air_new, surface_seen, ocean_temp_new, ocean_ice_new)


def solution(mesh):
    in_specs = (
        P(None, None, "gx", ("comp", "gy")),
        P(None, "gx", ("comp", "gy")),
        P(None, "gx", ("comp", "gy")),
        P("gx", ("comp", "gy")),
        P(ALL, None, None),
        P(ALL, None),
        P(ALL),
        P(ALL),
        P(ALL, None),
        P(ALL, None),
        P(ALL, None),
        P(ALL, None),
    )
    out_specs = (
        P(None, None, "gx", ("comp", "gy")),
        P(None, "gx", ("comp", "gy")),
        P(ALL, None),
        P(ALL, None),
    )
    return jax.shard_map(local, mesh=mesh, in_specs=in_specs, out_specs=out_specs, check_vma=False)
```

```python
import functools

import jax
import jax.numpy as jnp
from jax import lax
from jax.experimental import pallas as pl
from jax.experimental.pallas import tpu as pltpu
from jax.sharding import PartitionSpec as P

F32 = jnp.float32
BF16 = jnp.bfloat16
ALL = ("comp", "gx", "gy")
NF = 8
SENT = 5
SURFACE_STEP = 0.5
MIX = 0.2
MIB = 1 << 20
PARTS = 8
STEP = 8
GROUP = 4
LAG = 8


def in_vmem(*arrays):
    return [pltpu.with_memory_space_constraint(x, pltpu.VMEM) for x in arrays]


def in_hbm(*arrays):
    return [pltpu.with_memory_space_constraint(x, pltpu.HBM) for x in arrays]


def row_swaps(first):
    n_gx, n_gy = lax.axis_size("gx"), lax.axis_size("gy")
    pairs = []
    for comp in range(lax.axis_size("comp")):
        for gx in range(n_gx):
            for gy in range(n_gy):
                other = gx + 1 if (gx - first) % 2 == 0 else gx - 1
                to, core = (other, gy) if 0 <= other < n_gx else (gx, gy ^ 1)
                pairs.append(((comp * n_gx + gx) * n_gy + gy, (comp * n_gx + to) * n_gy + core))
    return pairs


def col_swaps(first):
    count = lax.axis_size("comp") * lax.axis_size("gy")
    return [(i, (i + 1 if (i - first) % 2 == 0 else i - 1) % count) for i in range(count)]


def grid_place():
    gx, n_gx = lax.axis_index("gx"), lax.axis_size("gx")
    c = lax.axis_index("comp") * lax.axis_size("gy") + lax.axis_index("gy")
    n_c = lax.axis_size("comp") * lax.axis_size("gy")
    there = lambda yes: jnp.where(yes, 1.0, 0.0).astype(F32)
    return gx % 2 == 0, c % 2 == 0, there(gx > 0), there(gx < n_gx - 1), there(c > 0), there(c < n_c - 1)


def rows_kernel(air, rows_a, rows_b, first, last, sem):
    even_row = grid_place()[0]
    count, tile, lanes = first.shape
    rows = air.shape[1]
    copies = [
        pltpu.make_async_copy(air.at[:, pl.ds(0, tile)], first, sem.at[0]),
        pltpu.make_async_copy(air.at[:, pl.ds(rows - tile, tile)], last, sem.at[1]),
    ]
    for c in copies:
        c.start()
    for c in copies:
        c.wait()
    first, last = [x.reshape(count * tile, lanes) for x in (first, last)]
    for k in range(2):
        low, high = first[pl.ds(k, count, stride=tile), :], last[pl.ds(tile - 1 - k, count, stride=tile), :]
        to = slice(k * lanes, (k + 1) * lanes)
        rows_a[:, to] = jnp.where(even_row, high, low).astype(BF16)
        rows_b[:, to] = jnp.where(even_row, low, high).astype(BF16)


def pack_rows(air):
    fields, levels, rows, lanes = air.shape
    out = jax.ShapeDtypeStruct((fields * levels, 2 * lanes), BF16)
    edge = pltpu.VMEM((fields * levels, 8, lanes), F32)
    return pl.pallas_call(
        rows_kernel,
        in_specs=[pl.BlockSpec(memory_space=pltpu.HBM)],
        out_specs=[pl.BlockSpec(memory_space=pltpu.VMEM)] * 2,
        out_shape=[out, out],
        scratch_shapes=[edge, edge, pltpu.SemaphoreType.DMA((2,))],
        compiler_params=pltpu.CompilerParams(vmem_limit_bytes=8 * MIB),
        name="pack_rows",
    )(*in_hbm(air.reshape(fields * levels, rows, lanes)))


def cols_kernel(air, weight, own_left, own_right, lowest, first_half, held, sem, sem_w, chunk):
    fields, levels, rows, lanes = air.shape
    copies = []
    for i in range(levels // chunk):
        part = pl.ds(i * chunk, chunk)
        copies.append(pltpu.make_async_copy(air.at[:, part], held.at[:, part], sem.at[i]))
        copies[i].start()
    weights = fetch(weight.at[pl.ds(0, first_half.shape[0])], first_half, sem_w)
    pair = lax.broadcasted_iota(jnp.int32, (rows, lanes), 1) >> 1
    left, right = [[jnp.zeros((rows, lanes), F32)] * fields for _ in range(2)]
    for i in range(levels // chunk):
        copies[i].wait()
        if i == 0:
            lowest[...] = held[:, 0]
        for level in range(i * chunk, (i + 1) * chunk):
            for field in range(fields):
                turned = pltpu.roll(held[field, level], 2 * level % lanes, axis=1)
                left[field] = jnp.where(pair == level, turned, left[field])
                right[field] = jnp.where(pair == (level - 1) % levels, turned, right[field])
    for field in range(fields):
        own_left[field] = left[field]
        own_right[field] = pltpu.roll(right[field], 2, axis=1)
    for c in weights:
        c.wait()


def pack_cols(air, weight):
    fields, levels, rows, lanes = air.shape
    chunk = 8
    vmem = pl.BlockSpec(memory_space=pltpu.VMEM)
    out = jax.ShapeDtypeStruct((fields, rows, lanes), F32)
    return pl.pallas_call(
        functools.partial(cols_kernel, chunk=chunk),
        in_specs=[pl.BlockSpec(memory_space=pltpu.HBM)] * 2,
        out_specs=[vmem] * 4,
        out_shape=[out, out, out, pltpu.VMEM((weight.shape[0] // 2, lanes, lanes), BF16)],
        scratch_shapes=[
            pltpu.VMEM(air.shape, F32),
            pltpu.SemaphoreType.DMA((levels // chunk,)),
            pltpu.SemaphoreType.DMA((PARTS,)),
        ],
        compiler_params=pltpu.CompilerParams(vmem_limit_bytes=12 * MIB),
        cost_estimate=pl.CostEstimate(flops=4 * air.size, bytes_accessed=4 * air.size, transcendentals=0),
        name="pack_cols",
    )(*in_hbm(air, weight))


def with_row(strip, row, first):
    rows = strip.shape[0]
    index = lax.broadcasted_iota(jnp.int32, strip.shape, 0)
    if first:
        return jnp.where(index == 0, row, pltpu.roll(strip, 1, axis=0))
    return jnp.where(index == rows - 1, row, pltpu.roll(strip, rows - 1, axis=0))


def strips_kernel(got_a, got_b, own_left, own_right, to_g, to_x):
    even_col = grid_place()[1]
    fields, rows, lanes = own_left.shape
    top, _, low, _ = row_halo(got_a, got_b)
    levels = top.shape[0] // fields
    level = lax.broadcasted_iota(jnp.int32, (levels, lanes), 0)
    pair = lax.broadcasted_iota(jnp.int32, (levels, lanes), 1) >> 1
    spread = jnp.where(level == pair, 1.0, 0.0).astype(BF16)
    odd = (lax.broadcasted_iota(jnp.int32, (rows, lanes), 1) & 1) == 1
    for field in range(fields):
        at = slice(field * levels, (field + 1) * levels)
        above, below = [
            lax.dot_general(h[at].astype(BF16), spread, (((0,), (0,)), ((), ())), preferred_element_type=F32)
            for h in (top, low)
        ]
        left, right = own_left[field], own_right[field]
        edge = pltpu.roll(left, 1, axis=1)
        around = with_row(edge, 2.0 * above[0:1], True) + with_row(edge, 2.0 * below[0:1], False)
        west = jnp.where(odd, MIX * (edge + left + around), left)
        edge = pltpu.roll(right, lanes - 1, axis=1)
        around = with_row(edge, 2.0 * above[lanes - 1 :], True) + with_row(edge, 2.0 * below[lanes - 1 :], False)
        east = jnp.where(odd, right, MIX * (edge + right + around))
        to_g[field] = jnp.where(even_col, east, west).astype(BF16)
        to_x[field] = jnp.where(even_col, west, east).astype(BF16)


def make_strips(got_a, got_b, own_left, own_right):
    vmem = pl.BlockSpec(memory_space=pltpu.VMEM)
    out = jax.ShapeDtypeStruct(own_left.shape, BF16)
    return pl.pallas_call(
        strips_kernel,
        in_specs=[vmem] * 4,
        out_specs=[vmem] * 2,
        out_shape=[out, out],
        compiler_params=pltpu.CompilerParams(vmem_limit_bytes=8 * MIB),
        name="strips",
    )(got_a, got_b, own_left, own_right)


def side_strips(field, got_g, got_x, own_left, own_right):
    _, even_col, _, _, has_left, has_right = grid_place()
    rows, lanes = got_g.shape[1], got_g.shape[2]
    from_g, from_x = got_g[field].astype(F32), got_x[field].astype(F32)
    west = jnp.where(even_col, from_x, from_g) * has_left
    east = jnp.where(even_col, from_g, from_x) * has_right
    next_west = pltpu.roll(west + MIX * own_left[field], 1, axis=1) * has_left
    next_east = pltpu.roll(east + MIX * own_right[field], lanes - 1, axis=1) * has_right
    odd = (lax.broadcasted_iota(jnp.int32, (rows, lanes), 1) & 1) == 1
    return jnp.where(odd, west, east), jnp.where(odd, next_west, next_east)


def row_halo(got_a, got_b):
    even_row, _, has_top, has_low, _, _ = grid_place()
    from_a, from_b = got_a[...].astype(F32), got_b[...].astype(F32)
    top = jnp.where(even_row, from_b, from_a) * has_top
    low = jnp.where(even_row, from_a, from_b) * has_low
    lanes = top.shape[1] // 2
    return top[:, :lanes], top[:, lanes:], low[:, :lanes], low[:, lanes:]


def sides_of_row(row):
    lanes = row.shape[1]
    lane = lax.broadcasted_iota(jnp.int32, row.shape, 1)
    from_left = jnp.where(lane == 0, 0.0, pltpu.roll(row, 1, axis=1))
    from_right = jnp.where(lane == lanes - 1, 0.0, pltpu.roll(row, lanes - 1, axis=1))
    return from_left + from_right


def substep(block, above, below, sides):
    lanes = block.shape[1]
    lane = lax.broadcasted_iota(jnp.int32, block.shape, 1)
    from_left = jnp.where(lane == 0, sides, pltpu.roll(block, 1, axis=1))
    from_right = jnp.where(lane == lanes - 1, sides, pltpu.roll(block, lanes - 1, axis=1))
    around = with_row(block, above, True) + with_row(block, below, False)
    return MIX * (block + around + (from_left + from_right))


def next_rows(top1, top2, low1, low2):
    return MIX * (top1 + top2 + sides_of_row(top1)), MIX * (low1 + low2 + sides_of_row(low1))


def mixed_level(block, top, next_top, low, next_low, sides0, sides1):
    rows = block.shape[0]
    _, _, has_top, has_low, _, _ = grid_place()
    once = substep(block, top, low, sides0)
    next_top = next_top + has_top * MIX * block[0:1]
    next_low = next_low + has_low * MIX * block[rows - 1 : rows]
    return substep(once, next_top, next_low, sides1)


def forward_kernel(
    owner_far, row_far, column_far, air, forcing, surface_temp, got_a, got_b, got_g, got_x,
    own_left, own_right, first_half, weight, payload, slots_far, source, held, sem, flux_rows, found, tags,
    counts, owner, block_row, block_column, slots, sem_i,
    bound, levels, group,
):
    blocks = weight.shape[0]
    rows, lanes = surface_temp.shape
    devices = payload.shape[0]
    total = devices * bound
    half = held.shape[0]
    copies = fetch(weight.at[pl.ds(half, half)], held, sem)
    indices = fetch_indices((owner_far, row_far, column_far), (owner, block_row, block_column), sem_i)
    top1, top2, low1, low2 = [jnp.concatenate([h[0:1], h[levels : levels + 1]]) for h in row_halo(got_a, got_b)]
    next_top, next_low = next_rows(top1, top2, low1, low2)
    lowest = []
    for field in range(2):
        sides0, sides1 = side_strips(field, got_g, got_x, own_left, own_right)
        lowest.append(
            mixed_level(
                air[field],
                *[h[field : field + 1] for h in (top1, next_top, low1, next_low)],
                pltpu.roll(sides0, lanes - 1, axis=1),
                pltpu.roll(sides1, lanes - 1, axis=1),
            )
        )
    u, v = forcing[0], forcing[1]
    ts = surface_temp[...]
    speed = jnp.sqrt(u * u + v * v + 1.0)
    fluxes = [
        speed * (ts - lowest[0]),
        speed * (0.5 * ts - lowest[1]),
        speed * u,
        speed * v,
        forcing[2],
        forcing[3] - 0.3 * ts,
        forcing[4],
        forcing[5],
    ]
    source[0] = fluxes[0]
    source[1] = fluxes[1]
    for field in range(NF):
        flux_rows[pl.ds(field, rows, stride=NF), :] = fluxes[field]
    if total > blocks:
        tags[...] = jnp.full_like(tags, -1.0)
        found[...] = jnp.zeros_like(found)

    def clear(i, _):
        counts[i] = 0
        return 0

    lax.fori_loop(0, devices, clear, 0)
    for c in indices:
        c.wait()

    def place(pair):
        for at, out in pair:
            to = owner[at]
            rank = counts[to]
            counts[to] = rank + 1
            slot = to * bound + rank
            slots[at] = slot
            found[pl.ds(pl.multiple_of(slot * NF, NF), NF), :] = out
            tags[pl.ds(slot, 1), :] = jnp.full((1, lanes), block_row[at], jnp.int32).astype(F32)

    def some(first, start, half):
        waiting = []
        for k in range(0, group, 2):
            at = start + first + k
            picked = [
                flux_rows[pl.ds(pl.multiple_of(block_column[n] * NF, NF), NF), :] for n in (at, at + 1)
            ]
            out = lax.dot_general(
                jnp.concatenate(picked).astype(BF16),
                half[pl.ds(first + k, 2)].reshape(2 * lanes, lanes),
                (((1,), (1,)), ((), ())),
                preferred_element_type=F32,
            )
            waiting.append(((at, out[:NF, :lanes]), (at + 1, out[NF:, lanes:])))
            if len(waiting) > LAG:
                place(waiting.pop(0))
        for pair in waiting:
            place(pair)

    all_of(first_half, 0, group, some)
    for c in copies:
        c.wait()
    all_of(held, half, group, some)
    (kept,) = fetch_indices((slots,), (slots_far,), sem_i)
    f = [found[pl.ds(k, total, stride=NF), :] for k in range(NF)]
    heat = (f[0] + f[1]) + (f[4] + f[5])
    heat_hi = heat.astype(BF16).astype(F32)
    lane = lax.broadcasted_iota(jnp.int32, (total, lanes), 1)
    heat_lo = jnp.where(lane == 0, tags[...], heat - heat_hi)
    shape = payload.shape[:2] + (lanes,)
    for k, part in enumerate((heat_hi, heat_lo, f[2], f[3], f[6] - f[7])):
        payload[:, :, k * lanes : (k + 1) * lanes] = part.reshape(shape).astype(BF16)
    kept.wait()


def fetch(source, held, sem):
    parts = sem.shape[0]
    size = source.shape[0] // parts
    copies = []
    for i in range(parts):
        at = pl.ds(i * size, size)
        copies.append(pltpu.make_async_copy(source.at[at], held.at[at], sem.at[i]))
        copies[i].start()
    return copies


def fetch_indices(sources, targets, sem):
    copies = [pltpu.make_async_copy(a, b, sem.at[i]) for i, (a, b) in enumerate(zip(sources, targets))]
    for c in copies:
        c.start()
    return copies


def all_of(weight, start, group, some):
    def body(g, carry):
        some(g * group, start, weight)
        return carry

    lax.fori_loop(0, weight.shape[0] // group, body, 0)


def forward(
    owner, block_row, block_column, lowest, forcing, surface_temp, halo, own, first_half, weight, levels,
    devices, bound,
):
    _, rows, lanes = lowest.shape
    nonzeros = weight.shape[0]
    hbm = pl.BlockSpec(memory_space=pltpu.HBM)
    vmem = pl.BlockSpec(memory_space=pltpu.VMEM)
    args = (forcing, surface_temp, *halo, *own)
    total = devices * bound
    return pl.pallas_call(
        functools.partial(forward_kernel, bound=bound, levels=levels, group=128),
        in_specs=[hbm, hbm, hbm]
        + [vmem] * (len(args) + 2)
        + [pl.BlockSpec(memory_space=pltpu.HBM)],
        out_specs=[vmem, hbm, vmem],
        out_shape=[
            jax.ShapeDtypeStruct((devices, bound, SENT * lanes), BF16),
            pltpu.HBM((nonzeros,), jnp.int32),
            jax.ShapeDtypeStruct((2, rows, lanes), F32),
        ],
        scratch_shapes=[
            pltpu.VMEM(first_half.shape, BF16),
            pltpu.SemaphoreType.DMA((PARTS,)),
            pltpu.VMEM((rows * NF, lanes), F32),
            pltpu.VMEM((total * NF, lanes), F32),
            pltpu.VMEM((total, lanes), F32),
            pltpu.SMEM((devices,), jnp.int32),
            pltpu.SMEM((nonzeros,), jnp.int32),
            pltpu.SMEM((nonzeros,), jnp.int32),
            pltpu.SMEM((nonzeros,), jnp.int32),
            pltpu.SMEM((nonzeros,), jnp.int32),
            pltpu.SemaphoreType.DMA((3,)),
        ],
        compiler_params=pltpu.CompilerParams(vmem_limit_bytes=20 * MIB),
        name="forward_blocks",
    )(*in_hbm(owner, block_row, block_column), lowest, *args, *in_vmem(first_half), *in_hbm(weight))


def pivot_kernel(coupling, out, held, inverse, sem, out_sem):
    levels = inverse.shape[0]
    copies = fetch_levels([(coupling, held)], sem, levels - 1)

    def one(level, ratio, last=False):
        below = held[level - 1]
        diagonal = 1.0 + below
        if not last:
            diagonal = diagonal + held[level]
        inv = 1.0 / (diagonal - below * ratio)
        inverse[level] = inv
        return inv if last else held[level] * inv

    outs = []
    for i, part in enumerate(copies):
        for c in part:
            c.wait()
        if i == 0:
            inv = 1.0 / (1.0 + held[0])
            inverse[0] = inv
            ratio = held[0] * inv
        start = max(1, i * STEP)
        stop = min((i + 1) * STEP, levels - 1)
        ratio = lax.fori_loop(start, stop, one, ratio)
        if stop == levels - 1:
            one(levels - 1, ratio, True)
        at = pl.ds(i * STEP, STEP)
        outs.append(pltpu.make_async_copy(inverse.at[at], out.at[at], out_sem.at[i]))
        outs[i].start()
    for c in outs:
        c.wait()


def fetch_levels(pairs, sem, levels, order=1):
    copies = []
    starts = list(range(0, levels, STEP))[::order]
    for i, start in enumerate(starts):
        part = []
        for k, (source, held) in enumerate(pairs):
            at = pl.ds(start, min(STEP, source.shape[-3] - start))
            if len(source.shape) == 4:
                part.append(pltpu.make_async_copy(source.at[:, at], held.at[:, at], sem.at[k * len(starts) + i]))
            else:
                part.append(pltpu.make_async_copy(source.at[at], held.at[at], sem.at[k * len(starts) + i]))
        for c in part:
            c.start()
        copies.append(part)
    return copies


def pivots(coupling):
    levels, rows, lanes = coupling.shape
    shape = (levels + 1, rows, lanes)
    return pl.pallas_call(
        pivot_kernel,
        in_specs=[pl.BlockSpec(memory_space=pltpu.HBM)],
        out_specs=pl.BlockSpec(memory_space=pltpu.HBM),
        out_shape=pltpu.HBM(shape, F32),
        scratch_shapes=[
            pltpu.VMEM(coupling.shape, F32),
            pltpu.VMEM(shape, F32),
            pltpu.SemaphoreType.DMA(((levels + STEP) // STEP,)),
            pltpu.SemaphoreType.DMA(((levels + STEP) // STEP,)),
        ],
        compiler_params=pltpu.CompilerParams(vmem_limit_bytes=12 * MIB),
        cost_estimate=pl.CostEstimate(flops=8 * coupling.size, bytes_accessed=8 * coupling.size, transcendentals=0),
        name="pivots",
    )(*in_hbm(coupling))


def beside(block, shifts):
    high = block.astype(BF16)
    low = (block - high.astype(F32)).astype(BF16)
    return jnp.dot(jnp.concatenate([high, low], axis=1), shifts, preferred_element_type=F32)


def stepped(block, above, below, inside, sides, edge):
    around = with_row(block, above, True) + with_row(block, below, False)
    return MIX * (block + around + (inside + jnp.where(edge, sides, 0.0)))


def up_kernel(
    air, coupling, inverse, got_a, got_b, got_g, got_x, own_left, own_right, source, reduced,
    held, held_c, held_i, done, halo_rows, strips, shifts, inside, once, sem, out_sem,
):
    fields, levels, rows, lanes = air.shape
    copies = fetch_levels([(air, held), (inverse, held_i), (coupling, held_c)], sem, levels)
    _, _, has_top, has_low, _, _ = grid_place()
    halo = row_halo(got_a, got_b)
    for k, h in enumerate((halo[0], halo[2], *next_rows(*halo))):
        halo_rows[k] = h
    for field in range(fields):
        sides0, sides1 = side_strips(field, got_g, got_x, own_left, own_right)
        strips[field, 0] = sides0
        strips[field, 1] = sides1
    row = lax.broadcasted_iota(jnp.int32, (2 * lanes, lanes), 0) % lanes
    column = lax.broadcasted_iota(jnp.int32, (2 * lanes, lanes), 1)
    shifts[...] = jnp.where(jnp.abs(row - column) == 1, 1.0, 0.0).astype(BF16)
    lane = lax.broadcasted_iota(jnp.int32, (rows, lanes), 1)
    edge = (lane == 0) | (lane == lanes - 1)
    groups = levels // GROUP
    members = [(field, k) for k in range(GROUP) for field in range(fields)]

    def place(k, field):
        return slice((k * fields + field) * rows, (k * fields + field + 1) * rows)

    def first_inside(g):
        block = jnp.concatenate([held[field, g * GROUP + k] for field, k in members])
        inside[0, g % 2] = beside(block, shifts[...])

    def first_step(g):
        for field, k in members:
            level = g * GROUP + k
            at = field * levels + level
            sides = pltpu.roll(strips[field, 0], (2 * lanes - 1 - 2 * level) % lanes, axis=1)
            once[g % 2, place(k, field)] = stepped(
                held[field, level], halo_rows[0, at : at + 1], halo_rows[1, at : at + 1],
                inside[0, g % 2, place(k, field)], sides, edge,
            )
        inside[1, g % 2] = beside(once[g % 2], shifts[...])

    def second_step(g):
        for field, k in members:
            level = g * GROUP + k
            at = field * levels + level
            sides = pltpu.roll(strips[field, 1], (2 * lanes - 1 - 2 * level) % lanes, axis=1)
            top = halo_rows[2, at : at + 1] + has_top * MIX * held[field, level, 0:1]
            low = halo_rows[3, at : at + 1] + has_low * MIX * held[field, level, rows - 1 : rows]
            right = stepped(
                once[g % 2, place(k, field)], top, low, inside[1, g % 2, place(k, field)], sides, edge
            )
            if level == 0:
                right = right + SURFACE_STEP * source[field]
            else:
                right = right + held_c[level - 1] * done[field, level - 1]
            done[field, level] = right * held_i[level]

    outs = []
    for g in range(groups + 2):
        if g < groups:
            if g * GROUP % STEP == 0:
                for c in copies[g * GROUP // STEP]:
                    c.wait()
            first_inside(g)
        if 0 <= g - 1 < groups:
            first_step(g - 1)
        if g >= 2:
            second_step(g - 2)
            end = (g - 1) * GROUP
            if end % STEP == 0:
                at = pl.ds(end - STEP, STEP)
                outs.append(pltpu.make_async_copy(done.at[:, at], reduced.at[:, at], out_sem.at[end // STEP - 1]))
                outs[-1].start()
    for c in outs:
        c.wait()


def columns_up(air, coupling, inverse, halo, own, source):
    fields, levels, rows, lanes = air.shape
    args = (air, coupling, inverse, *halo, *own, source)
    hbm = pl.BlockSpec(memory_space=pltpu.HBM)
    parts = levels // STEP
    return pl.pallas_call(
        up_kernel,
        in_specs=[hbm] * 3 + [pl.BlockSpec(memory_space=pltpu.VMEM)] * (len(args) - 3),
        out_specs=hbm,
        out_shape=pltpu.HBM(air.shape, F32),
        scratch_shapes=[
            pltpu.VMEM(air.shape, F32),
            pltpu.VMEM(coupling.shape, F32),
            pltpu.VMEM(inverse.shape, F32),
            pltpu.VMEM(air.shape, F32),
            pltpu.VMEM((4, fields * levels, lanes), F32),
            pltpu.VMEM((fields, 2, rows, lanes), F32),
            pltpu.VMEM((2 * lanes, lanes), BF16),
            pltpu.VMEM((2, 2, GROUP * fields * rows, lanes), F32),
            pltpu.VMEM((2, GROUP * fields * rows, lanes), F32),
            pltpu.SemaphoreType.DMA((3 * parts,)),
            pltpu.SemaphoreType.DMA((parts,)),
        ],
        compiler_params=pltpu.CompilerParams(vmem_limit_bytes=24 * MIB),
        cost_estimate=pl.CostEstimate(flops=40 * air.size, bytes_accessed=12 * air.size, transcendentals=0),
        name="columns_up",
    )(*in_hbm(*args[:3]), *args[3:])


def down_kernel(reduced, coupling, inverse, air_new, held, held_c, held_i, sem, out_sem):
    _, levels, rows, lanes = reduced.shape
    copies = fetch_levels([(reduced, held), (inverse, held_i), (coupling, held_c)], sem, levels, -1)
    outs = []
    for i, part in enumerate(copies):
        for c in part:
            c.wait()
        top = levels - 1 - i * STEP

        def one(k, _, top=top):
            level = top - k
            ratio = held_c[level] * held_i[level]
            for field in range(2):
                held[field, level] = held[field, level] + ratio * held[field, level + 1]
            return 0

        lax.fori_loop(1 if i == 0 else 0, STEP, one, 0)
        at = pl.ds(levels - (i + 1) * STEP, STEP)
        outs.append(pltpu.make_async_copy(held.at[:, at], air_new.at[:, at], out_sem.at[i]))
        outs[i].start()
    for c in outs:
        c.wait()


def columns_down(reduced, coupling, inverse):
    levels = reduced.shape[1]
    hbm = pl.BlockSpec(memory_space=pltpu.HBM)
    parts = levels // STEP
    return pl.pallas_call(
        down_kernel,
        in_specs=[hbm] * 3,
        out_specs=hbm,
        out_shape=pltpu.HBM(reduced.shape, F32),
        scratch_shapes=[
            pltpu.VMEM(reduced.shape, F32),
            pltpu.VMEM(coupling.shape, F32),
            pltpu.VMEM(inverse.shape, F32),
            pltpu.SemaphoreType.DMA((3 * parts,)),
            pltpu.SemaphoreType.DMA((parts,)),
        ],
        compiler_params=pltpu.CompilerParams(vmem_limit_bytes=16 * MIB),
        cost_estimate=pl.CostEstimate(flops=8 * reduced.size, bytes_accessed=12 * reduced.size, transcendentals=0),
        name="columns_down",
    )(*in_hbm(reduced, coupling, inverse))


def ocean_kernel(arrived, land_mask, ocean_temp, ocean_ice, layer_depth, temp_new, ice_new, replies):
    blocks, lanes = ocean_temp.shape
    total = arrived.shape[0] * arrived.shape[1]
    wide = arrived.shape[2]
    block = arrived[...].astype(F32).reshape(total, wide)
    lane = lax.broadcasted_iota(jnp.int32, (total, wide), 1)
    tag = block[:, lanes : lanes + 1].astype(jnp.int32)
    block = jnp.where(lane == lanes, 0.0, block).astype(BF16)
    slot_of = (tag == lax.broadcasted_iota(jnp.int32, (total, blocks), 1)).astype(F32).astype(BF16)
    sums = lax.dot_general(slot_of, block, (((0,), (0,)), ((), ())), preferred_element_type=F32)
    sums = [sums[:, k * lanes : (k + 1) * lanes] for k in range(SENT)]
    heat = sums[0] + sums[1]
    stress = sums[2] * sums[2] + sums[3] * sums[3]
    wet = land_mask[...].astype(F32)
    temp = ocean_temp[...]
    temp = temp + wet * (0.3 * heat / layer_depth[...] - 0.01 * stress * temp)
    ice = jnp.clip(ocean_ice[...] - wet * 0.05 * (heat + sums[4]), 0.0, 1.0)
    temp_new[...] = temp
    ice_new[...] = ice
    pair = jnp.concatenate([temp, ice], axis=1).astype(BF16)
    answer = jnp.dot(slot_of, pair, preferred_element_type=F32)
    replies[...] = answer.reshape(replies.shape).astype(BF16)


def ocean(arrived, land_mask, ocean_temp, ocean_ice, layer_depth):
    devices, bound, _ = arrived.shape
    blocks, lanes = ocean_temp.shape
    vmem = pl.BlockSpec(memory_space=pltpu.VMEM)
    return pl.pallas_call(
        ocean_kernel,
        in_specs=[vmem] * 5,
        out_specs=[vmem] * 3,
        out_shape=[
            jax.ShapeDtypeStruct((blocks, lanes), F32),
            jax.ShapeDtypeStruct((blocks, lanes), F32),
            jax.ShapeDtypeStruct((devices, bound, 2 * lanes), BF16),
        ],
        compiler_params=pltpu.CompilerParams(vmem_limit_bytes=16 * MIB),
        name="ocean",
    )(arrived, land_mask, ocean_temp, ocean_ice, layer_depth)


def backward_kernel(
    slots_far, column_far, returned, weight, seen, held, sem, pairs, sums, slots, block_column, sem_i
):
    lanes = weight.shape[1]
    total = returned.shape[0] * returned.shape[1]
    rows = seen.shape[1]
    copies = fetch(weight, held, sem)
    indices = fetch_indices((slots_far, column_far), (slots, block_column), sem_i)
    pairs[...] = jnp.zeros_like(pairs)
    sums[...] = jnp.zeros_like(sums)
    for k in range(2):
        part = returned[:, :, k * lanes : (k + 1) * lanes].astype(F32).reshape(total, lanes)
        pairs[pl.ds(k, total, stride=8), :] = part

    def place(pair):
        for at, out in pair:
            sums[pl.ds(pl.multiple_of(block_column[at] * 8, 8), 8), :] += out

    size = weight.shape[0] // PARTS
    for c in indices:
        c.wait()
    waiting = []
    for at in range(0, weight.shape[0], 2):
        if at % size == 0:
            copies[at // size].wait()
        picked = [pairs[pl.ds(pl.multiple_of(slots[n] * 8, 8), 8), :] for n in (at, at + 1)]
        out = jnp.dot(
            jnp.concatenate(picked).astype(BF16),
            jnp.concatenate([held[at], held[at + 1]], axis=1),
            preferred_element_type=F32,
        )
        waiting.append(((at, out[:8, :lanes]), (at + 1, out[8:, lanes:])))
        if len(waiting) > LAG:
            place(waiting.pop(0))
    for pair in waiting:
        place(pair)
    for k in range(2):
        seen[k] = sums[pl.ds(k, rows, stride=8), :]


def backward(slots, block_column, returned, weight, rows):
    devices, bound, _ = returned.shape
    nonzeros, lanes, _ = weight.shape
    hbm = pl.BlockSpec(memory_space=pltpu.HBM)
    vmem = pl.BlockSpec(memory_space=pltpu.VMEM)
    return pl.pallas_call(
        backward_kernel,
        in_specs=[hbm, hbm, vmem, hbm],
        out_specs=vmem,
        out_shape=jax.ShapeDtypeStruct((2, rows, lanes), F32),
        scratch_shapes=[
            pltpu.VMEM(weight.shape, BF16),
            pltpu.SemaphoreType.DMA((PARTS,)),
            pltpu.VMEM((devices * bound * 8, lanes), F32),
            pltpu.VMEM((rows * 8, lanes), F32),
            pltpu.SMEM(slots.shape, jnp.int32),
            pltpu.SMEM(slots.shape, jnp.int32),
            pltpu.SemaphoreType.DMA((2,)),
        ],
        compiler_params=pltpu.CompilerParams(vmem_limit_bytes=16 * MIB),
        name="backward_blocks",
    )(*in_hbm(slots, block_column), returned, *in_hbm(weight))


def local(
    air_state,
    coupling,
    forcing,
    surface_temp,
    remap_weight,
    block_owner,
    block_row,
    block_column,
    land_mask,
    ocean_temp,
    ocean_ice,
    layer_depth,
):
    devices = lax.axis_size("comp") * lax.axis_size("gx") * lax.axis_size("gy")
    nonzeros = remap_weight.shape[0]
    bound = max(4, (nonzeros + devices - 1) // devices)
    rows_a, rows_b = pack_rows(air_state)
    got_b = lax.ppermute(rows_b, ALL, row_swaps(1))
    got_a = lax.ppermute(rows_a, ALL, row_swaps(0))
    *own, lowest, first_half = pack_cols(air_state, remap_weight)
    to_g, to_x = make_strips(got_a, got_b, *own)
    got_x = lax.ppermute(to_x, ("comp", "gy"), col_swaps(1))
    got_g = lax.ppermute(to_g, ("comp", "gy"), col_swaps(0))
    halo = (got_a, got_b, got_g, got_x)
    inverse = pivots(coupling)
    halo, inverse = lax.optimization_barrier((halo, inverse))
    payload, slots, source = forward(
        block_owner[:, 0], block_row, block_column, lowest, forcing, surface_temp, halo, own,
        first_half, remap_weight, air_state.shape[1], devices, bound,
    )
    arrived = lax.all_to_all(payload, ALL, split_axis=0, concat_axis=0, tiled=True)
    reduced = columns_up(air_state, coupling, inverse, halo, own, source)
    arrived, reduced = lax.optimization_barrier((arrived, reduced))
    ocean_temp_new, ocean_ice_new, replies = ocean(
        arrived, land_mask, ocean_temp, ocean_ice, layer_depth
    )
    returned = lax.all_to_all(replies, ALL, split_axis=0, concat_axis=0, tiled=True)
    air_new = columns_down(reduced, coupling, inverse)
    returned, air_new = lax.optimization_barrier((returned, air_new))
    surface_seen = backward(slots, block_column, returned, remap_weight, surface_temp.shape[0])
    return (air_new, surface_seen, ocean_temp_new, ocean_ice_new)


def solution(mesh):
    in_specs = (
        P(None, None, "gx", ("comp", "gy")),
        P(None, "gx", ("comp", "gy")),
        P(None, "gx", ("comp", "gy")),
        P("gx", ("comp", "gy")),
        P(ALL, None, None),
        P(ALL, None),
        P(ALL),
        P(ALL),
        P(ALL, None),
        P(ALL, None),
        P(ALL, None),
        P(ALL, None),
    )
    out_specs = (
        P(None, None, "gx", ("comp", "gy")),
        P(None, "gx", ("comp", "gy")),
        P(ALL, None),
        P(ALL, None),
    )
    return jax.shard_map(local, mesh=mesh, in_specs=in_specs, out_specs=out_specs, check_vma=False)
```

```python
import functools

import jax
import jax.numpy as jnp
from jax import lax
from jax.experimental import pallas as pl
from jax.experimental.pallas import tpu as pltpu
from jax.sharding import PartitionSpec as P

F32 = jnp.float32
BF16 = jnp.bfloat16
ALL = ("comp", "gx", "gy")
NF = 8
SENT = 5
SURFACE_STEP = 0.5
MIX = 0.2
MIB = 1 << 20
PARTS = 8
STEP = 8
GROUP = 4
LAG = 8
NEAR = 64


def in_vmem(*arrays):
    return [pltpu.with_memory_space_constraint(x, pltpu.VMEM) for x in arrays]


def in_hbm(*arrays):
    return [pltpu.with_memory_space_constraint(x, pltpu.HBM) for x in arrays]


def row_swaps(first):
    n_gx, n_gy = lax.axis_size("gx"), lax.axis_size("gy")
    pairs = []
    for comp in range(lax.axis_size("comp")):
        for gx in range(n_gx):
            for gy in range(n_gy):
                other = gx + 1 if (gx - first) % 2 == 0 else gx - 1
                to, core = (other, gy) if 0 <= other < n_gx else (gx, gy ^ 1)
                pairs.append(((comp * n_gx + gx) * n_gy + gy, (comp * n_gx + to) * n_gy + core))
    return pairs


def col_swaps(first):
    count = lax.axis_size("comp") * lax.axis_size("gy")
    return [(i, (i + 1 if (i - first) % 2 == 0 else i - 1) % count) for i in range(count)]


def grid_place():
    gx, n_gx = lax.axis_index("gx"), lax.axis_size("gx")
    c = lax.axis_index("comp") * lax.axis_size("gy") + lax.axis_index("gy")
    n_c = lax.axis_size("comp") * lax.axis_size("gy")
    there = lambda yes: jnp.where(yes, 1.0, 0.0).astype(F32)
    return gx % 2 == 0, c % 2 == 0, there(gx > 0), there(gx < n_gx - 1), there(c > 0), there(c < n_c - 1)


def rows_kernel(air, rows_a, rows_b, first, last, sem):
    even_row = grid_place()[0]
    count, tile, lanes = first.shape
    rows = air.shape[1]
    copies = [
        pltpu.make_async_copy(air.at[:, pl.ds(0, tile)], first, sem.at[0]),
        pltpu.make_async_copy(air.at[:, pl.ds(rows - tile, tile)], last, sem.at[1]),
    ]
    for c in copies:
        c.start()
    for c in copies:
        c.wait()
    first, last = [x.reshape(count * tile, lanes) for x in (first, last)]
    for k in range(2):
        low, high = first[pl.ds(k, count, stride=tile), :], last[pl.ds(tile - 1 - k, count, stride=tile), :]
        to = slice(k * lanes, (k + 1) * lanes)
        rows_a[:, to] = jnp.where(even_row, high, low).astype(BF16)
        rows_b[:, to] = jnp.where(even_row, low, high).astype(BF16)


def pack_rows(air):
    fields, levels, rows, lanes = air.shape
    out = jax.ShapeDtypeStruct((fields * levels, 2 * lanes), BF16)
    edge = pltpu.VMEM((fields * levels, 8, lanes), F32)
    return pl.pallas_call(
        rows_kernel,
        in_specs=[pl.BlockSpec(memory_space=pltpu.HBM)],
        out_specs=[pl.BlockSpec(memory_space=pltpu.VMEM)] * 2,
        out_shape=[out, out],
        scratch_shapes=[edge, edge, pltpu.SemaphoreType.DMA((2,))],
        compiler_params=pltpu.CompilerParams(vmem_limit_bytes=8 * MIB),
        name="pack_rows",
    )(*in_hbm(air.reshape(fields * levels, rows, lanes)))


def cols_kernel(air, weight, own_left, own_right, lowest, first_half, held, sem, sem_w, chunk):
    fields, levels, rows, lanes = air.shape
    copies = []
    for i in range(levels // chunk):
        part = pl.ds(i * chunk, chunk)
        copies.append(pltpu.make_async_copy(air.at[:, part], held.at[:, part], sem.at[i]))
        copies[i].start()
    weights = fetch(weight.at[pl.ds(0, first_half.shape[0])], first_half, sem_w)
    pair = lax.broadcasted_iota(jnp.int32, (rows, lanes), 1) >> 1
    left, right = [[jnp.zeros((rows, lanes), F32)] * fields for _ in range(2)]
    for i in range(levels // chunk):
        copies[i].wait()
        if i == 0:
            lowest[...] = held[:, 0]
        for level in range(i * chunk, (i + 1) * chunk):
            for field in range(fields):
                turned = pltpu.roll(held[field, level], 2 * level % lanes, axis=1)
                left[field] = jnp.where(pair == level, turned, left[field])
                right[field] = jnp.where(pair == (level - 1) % levels, turned, right[field])
    for field in range(fields):
        own_left[field] = left[field]
        own_right[field] = pltpu.roll(right[field], 2, axis=1)
    for c in weights:
        c.wait()


def pack_cols(air, weight):
    fields, levels, rows, lanes = air.shape
    chunk = 8
    vmem = pl.BlockSpec(memory_space=pltpu.VMEM)
    out = jax.ShapeDtypeStruct((fields, rows, lanes), F32)
    return pl.pallas_call(
        functools.partial(cols_kernel, chunk=chunk),
        in_specs=[pl.BlockSpec(memory_space=pltpu.HBM)] * 2,
        out_specs=[vmem] * 4,
        out_shape=[out, out, out, pltpu.VMEM((weight.shape[0] // 2, lanes, lanes), BF16)],
        scratch_shapes=[
            pltpu.VMEM(air.shape, F32),
            pltpu.SemaphoreType.DMA((levels // chunk,)),
            pltpu.SemaphoreType.DMA((PARTS,)),
        ],
        compiler_params=pltpu.CompilerParams(vmem_limit_bytes=12 * MIB),
        cost_estimate=pl.CostEstimate(flops=4 * air.size, bytes_accessed=4 * air.size, transcendentals=0),
        name="pack_cols",
    )(*in_hbm(air, weight))


def with_row(strip, row, first):
    rows = strip.shape[0]
    index = lax.broadcasted_iota(jnp.int32, strip.shape, 0)
    if first:
        return jnp.where(index == 0, row, pltpu.roll(strip, 1, axis=0))
    return jnp.where(index == rows - 1, row, pltpu.roll(strip, rows - 1, axis=0))


def strips_kernel(got_a, got_b, own_left, own_right, to_g, to_x):
    even_col = grid_place()[1]
    fields, rows, lanes = own_left.shape
    top, _, low, _ = row_halo(got_a, got_b)
    levels = top.shape[0] // fields
    level = lax.broadcasted_iota(jnp.int32, (levels, lanes), 0)
    pair = lax.broadcasted_iota(jnp.int32, (levels, lanes), 1) >> 1
    spread = jnp.where(level == pair, 1.0, 0.0).astype(BF16)
    odd = (lax.broadcasted_iota(jnp.int32, (rows, lanes), 1) & 1) == 1
    for field in range(fields):
        at = slice(field * levels, (field + 1) * levels)
        above, below = [
            lax.dot_general(h[at].astype(BF16), spread, (((0,), (0,)), ((), ())), preferred_element_type=F32)
            for h in (top, low)
        ]
        left, right = own_left[field], own_right[field]
        edge = pltpu.roll(left, 1, axis=1)
        around = with_row(edge, 2.0 * above[0:1], True) + with_row(edge, 2.0 * below[0:1], False)
        west = jnp.where(odd, MIX * (edge + left + around), left)
        edge = pltpu.roll(right, lanes - 1, axis=1)
        around = with_row(edge, 2.0 * above[lanes - 1 :], True) + with_row(edge, 2.0 * below[lanes - 1 :], False)
        east = jnp.where(odd, right, MIX * (edge + right + around))
        to_g[field] = jnp.where(even_col, east, west).astype(BF16)
        to_x[field] = jnp.where(even_col, west, east).astype(BF16)


def make_strips(got_a, got_b, own_left, own_right):
    vmem = pl.BlockSpec(memory_space=pltpu.VMEM)
    out = jax.ShapeDtypeStruct(own_left.shape, BF16)
    return pl.pallas_call(
        strips_kernel,
        in_specs=[vmem] * 4,
        out_specs=[vmem] * 2,
        out_shape=[out, out],
        compiler_params=pltpu.CompilerParams(vmem_limit_bytes=8 * MIB),
        name="strips",
    )(got_a, got_b, own_left, own_right)


def side_strips(field, got_g, got_x, own_left, own_right):
    _, even_col, _, _, has_left, has_right = grid_place()
    rows, lanes = got_g.shape[1], got_g.shape[2]
    from_g, from_x = got_g[field].astype(F32), got_x[field].astype(F32)
    west = jnp.where(even_col, from_x, from_g) * has_left
    east = jnp.where(even_col, from_g, from_x) * has_right
    next_west = pltpu.roll(west + MIX * own_left[field], 1, axis=1) * has_left
    next_east = pltpu.roll(east + MIX * own_right[field], lanes - 1, axis=1) * has_right
    odd = (lax.broadcasted_iota(jnp.int32, (rows, lanes), 1) & 1) == 1
    return jnp.where(odd, west, east), jnp.where(odd, next_west, next_east)


def row_halo(got_a, got_b):
    even_row, _, has_top, has_low, _, _ = grid_place()
    from_a, from_b = got_a[...].astype(F32), got_b[...].astype(F32)
    top = jnp.where(even_row, from_b, from_a) * has_top
    low = jnp.where(even_row, from_a, from_b) * has_low
    lanes = top.shape[1] // 2
    return top[:, :lanes], top[:, lanes:], low[:, :lanes], low[:, lanes:]


def sides_of_row(row):
    lanes = row.shape[1]
    lane = lax.broadcasted_iota(jnp.int32, row.shape, 1)
    from_left = jnp.where(lane == 0, 0.0, pltpu.roll(row, 1, axis=1))
    from_right = jnp.where(lane == lanes - 1, 0.0, pltpu.roll(row, lanes - 1, axis=1))
    return from_left + from_right


def substep(block, above, below, sides):
    lanes = block.shape[1]
    lane = lax.broadcasted_iota(jnp.int32, block.shape, 1)
    from_left = jnp.where(lane == 0, sides, pltpu.roll(block, 1, axis=1))
    from_right = jnp.where(lane == lanes - 1, sides, pltpu.roll(block, lanes - 1, axis=1))
    around = with_row(block, above, True) + with_row(block, below, False)
    return MIX * (block + around + (from_left + from_right))


def next_rows(top1, top2, low1, low2):
    return MIX * (top1 + top2 + sides_of_row(top1)), MIX * (low1 + low2 + sides_of_row(low1))


def mixed_level(block, top, next_top, low, next_low, sides0, sides1):
    rows = block.shape[0]
    _, _, has_top, has_low, _, _ = grid_place()
    once = substep(block, top, low, sides0)
    next_top = next_top + has_top * MIX * block[0:1]
    next_low = next_low + has_low * MIX * block[rows - 1 : rows]
    return substep(once, next_top, next_low, sides1)


def forward_kernel(
    owner_far, row_far, column_far, air, forcing, surface_temp, got_a, got_b, got_g, got_x,
    own_left, own_right, first_half, weight, payload, slots_far, source, held, sem, flux_rows, found, tags,
    counts, owner, block_row, block_column, slots, sem_i,
    bound, levels, group,
):
    blocks = weight.shape[0]
    rows, lanes = surface_temp.shape
    devices = payload.shape[0]
    total = devices * bound
    half = held.shape[0]
    copies = fetch(weight.at[pl.ds(half, half)], held, sem)
    indices = fetch_indices((owner_far, row_far, column_far), (owner, block_row, block_column), sem_i)
    top1, top2, low1, low2 = [jnp.concatenate([h[0:1], h[levels : levels + 1]]) for h in row_halo(got_a, got_b)]
    next_top, next_low = next_rows(top1, top2, low1, low2)
    lowest = []
    for field in range(2):
        sides0, sides1 = side_strips(field, got_g, got_x, own_left, own_right)
        lowest.append(
            mixed_level(
                air[field],
                *[h[field : field + 1] for h in (top1, next_top, low1, next_low)],
                pltpu.roll(sides0, lanes - 1, axis=1),
                pltpu.roll(sides1, lanes - 1, axis=1),
            )
        )
    u, v = forcing[0], forcing[1]
    ts = surface_temp[...]
    speed = jnp.sqrt(u * u + v * v + 1.0)
    fluxes = [
        speed * (ts - lowest[0]),
        speed * (0.5 * ts - lowest[1]),
        speed * u,
        speed * v,
        forcing[2],
        forcing[3] - 0.3 * ts,
        forcing[4],
        forcing[5],
    ]
    source[0] = fluxes[0]
    source[1] = fluxes[1]
    for field in range(NF):
        flux_rows[pl.ds(field, rows, stride=NF), :] = fluxes[field]
    if total > blocks:
        tags[...] = jnp.full_like(tags, -1.0)
        found[...] = jnp.zeros_like(found)

    def clear(i, _):
        counts[i] = 0
        return 0

    lax.fori_loop(0, devices, clear, 0)
    for c in indices:
        c.wait()

    def place(pair):
        for at, out in pair:
            to = owner[at]
            rank = counts[to]
            counts[to] = rank + 1
            slot = to * bound + rank
            slots[at] = slot
            found[pl.ds(pl.multiple_of(slot * NF, NF), NF), :] = out
            tags[pl.ds(slot, 1), :] = jnp.full((1, lanes), block_row[at], jnp.int32).astype(F32)

    def some(first, start, half):
        waiting = []
        for k in range(0, group, 2):
            at = start + first + k
            picked = [
                flux_rows[pl.ds(pl.multiple_of(block_column[n] * NF, NF), NF), :] for n in (at, at + 1)
            ]
            out = lax.dot_general(
                jnp.concatenate(picked).astype(BF16),
                half[pl.ds(first + k, 2)].reshape(2 * lanes, lanes),
                (((1,), (1,)), ((), ())),
                preferred_element_type=F32,
            )
            waiting.append(((at, out[:NF, :lanes]), (at + 1, out[NF:, lanes:])))
            if len(waiting) > LAG:
                place(waiting.pop(0))
        for pair in waiting:
            place(pair)

    all_of(first_half, 0, group, some)
    for c in copies:
        c.wait()
    all_of(held, half, group, some)
    (kept,) = fetch_indices((slots,), (slots_far,), sem_i)
    f = [found[pl.ds(k, total, stride=NF), :] for k in range(NF)]
    heat = (f[0] + f[1]) + (f[4] + f[5])
    heat_hi = heat.astype(BF16).astype(F32)
    lane = lax.broadcasted_iota(jnp.int32, (total, lanes), 1)
    heat_lo = jnp.where(lane == 0, tags[...], heat - heat_hi)
    shape = payload.shape[:2] + (lanes,)
    for k, part in enumerate((heat_hi, heat_lo, f[2], f[3], f[6] - f[7])):
        payload[:, :, k * lanes : (k + 1) * lanes] = part.reshape(shape).astype(BF16)
    kept.wait()


def fetch(source, held, sem):
    parts = sem.shape[0]
    size = source.shape[0] // parts
    copies = []
    for i in range(parts):
        at = pl.ds(i * size, size)
        copies.append(pltpu.make_async_copy(source.at[at], held.at[at], sem.at[i]))
        copies[i].start()
    return copies


def fetch_indices(sources, targets, sem):
    copies = [pltpu.make_async_copy(a, b, sem.at[i]) for i, (a, b) in enumerate(zip(sources, targets))]
    for c in copies:
        c.start()
    return copies


def all_of(weight, start, group, some):
    def body(g, carry):
        some(g * group, start, weight)
        return carry

    lax.fori_loop(0, weight.shape[0] // group, body, 0)


def forward(
    owner, block_row, block_column, lowest, forcing, surface_temp, halo, own, first_half, weight, levels,
    devices, bound,
):
    _, rows, lanes = lowest.shape
    nonzeros = weight.shape[0]
    hbm = pl.BlockSpec(memory_space=pltpu.HBM)
    vmem = pl.BlockSpec(memory_space=pltpu.VMEM)
    args = (forcing, surface_temp, *halo, *own)
    total = devices * bound
    return pl.pallas_call(
        functools.partial(forward_kernel, bound=bound, levels=levels, group=128),
        in_specs=[hbm, hbm, hbm]
        + [vmem] * (len(args) + 2)
        + [pl.BlockSpec(memory_space=pltpu.HBM)],
        out_specs=[vmem, hbm, vmem],
        out_shape=[
            jax.ShapeDtypeStruct((devices, bound, SENT * lanes), BF16),
            pltpu.HBM((nonzeros,), jnp.int32),
            jax.ShapeDtypeStruct((2, rows, lanes), F32),
        ],
        scratch_shapes=[
            pltpu.VMEM(first_half.shape, BF16),
            pltpu.SemaphoreType.DMA((PARTS,)),
            pltpu.VMEM((rows * NF, lanes), F32),
            pltpu.VMEM((total * NF, lanes), F32),
            pltpu.VMEM((total, lanes), F32),
            pltpu.SMEM((devices,), jnp.int32),
            pltpu.SMEM((nonzeros,), jnp.int32),
            pltpu.SMEM((nonzeros,), jnp.int32),
            pltpu.SMEM((nonzeros,), jnp.int32),
            pltpu.SMEM((nonzeros,), jnp.int32),
            pltpu.SemaphoreType.DMA((3,)),
        ],
        compiler_params=pltpu.CompilerParams(vmem_limit_bytes=20 * MIB),
        name="forward_blocks",
    )(*in_hbm(owner, block_row, block_column), lowest, *args, *in_vmem(first_half), *in_hbm(weight))


def pivot_kernel(coupling, out, held, inverse, sem, out_sem):
    levels = inverse.shape[0]
    copies = fetch_levels([(coupling, held)], sem, levels - 1)

    def one(level, ratio, last=False):
        below = held[level - 1]
        diagonal = 1.0 + below
        if not last:
            diagonal = diagonal + held[level]
        inv = 1.0 / (diagonal - below * ratio)
        inverse[level] = inv
        return inv if last else held[level] * inv

    outs = []
    for i, part in enumerate(copies):
        for c in part:
            c.wait()
        if i == 0:
            inv = 1.0 / (1.0 + held[0])
            inverse[0] = inv
            ratio = held[0] * inv
        start = max(1, i * STEP)
        stop = min((i + 1) * STEP, levels - 1)
        ratio = lax.fori_loop(start, stop, one, ratio)
        if stop == levels - 1:
            one(levels - 1, ratio, True)
        at = pl.ds(i * STEP, STEP)
        outs.append(pltpu.make_async_copy(inverse.at[at], out.at[at], out_sem.at[i]))
        outs[i].start()
    for c in outs:
        c.wait()


def fetch_levels(pairs, sem, levels, order=1):
    copies = []
    starts = list(range(0, levels, STEP))[::order]
    for i, start in enumerate(starts):
        part = []
        for k, (source, held) in enumerate(pairs):
            at = pl.ds(start, min(STEP, source.shape[-3] - start))
            if len(source.shape) == 4:
                part.append(pltpu.make_async_copy(source.at[:, at], held.at[:, at], sem.at[k * len(starts) + i]))
            else:
                part.append(pltpu.make_async_copy(source.at[at], held.at[at], sem.at[k * len(starts) + i]))
        for c in part:
            c.start()
        copies.append(part)
    return copies


def pivots(coupling):
    levels, rows, lanes = coupling.shape
    shape = (levels + 1, rows, lanes)
    return pl.pallas_call(
        pivot_kernel,
        in_specs=[pl.BlockSpec(memory_space=pltpu.HBM)],
        out_specs=pl.BlockSpec(memory_space=pltpu.HBM),
        out_shape=pltpu.HBM(shape, F32),
        scratch_shapes=[
            pltpu.VMEM(coupling.shape, F32),
            pltpu.VMEM(shape, F32),
            pltpu.SemaphoreType.DMA(((levels + STEP) // STEP,)),
            pltpu.SemaphoreType.DMA(((levels + STEP) // STEP,)),
        ],
        compiler_params=pltpu.CompilerParams(vmem_limit_bytes=12 * MIB),
        cost_estimate=pl.CostEstimate(flops=8 * coupling.size, bytes_accessed=8 * coupling.size, transcendentals=0),
        name="pivots",
    )(*in_hbm(coupling))


def beside(block, shifts):
    high = block.astype(BF16)
    low = (block - high.astype(F32)).astype(BF16)
    return jnp.dot(jnp.concatenate([high, low], axis=1), shifts, preferred_element_type=F32)


def stepped(block, above, below, inside, sides, edge):
    around = with_row(block, above, True) + with_row(block, below, False)
    return MIX * (block + around + (inside + jnp.where(edge, sides, 0.0)))


def up_kernel(
    air, coupling, inverse, got_a, got_b, got_g, got_x, own_left, own_right, source, reduced,
    held, held_c, held_i, done, halo_rows, strips, shifts, inside, once, sem, out_sem,
):
    fields, levels, rows, lanes = air.shape
    copies = fetch_levels([(air, held), (inverse, held_i), (coupling, held_c)], sem, levels)
    _, _, has_top, has_low, _, _ = grid_place()
    halo = row_halo(got_a, got_b)
    for k, h in enumerate((halo[0], halo[2], *next_rows(*halo))):
        halo_rows[k] = h
    for field in range(fields):
        sides0, sides1 = side_strips(field, got_g, got_x, own_left, own_right)
        strips[field, 0] = sides0
        strips[field, 1] = sides1
    row = lax.broadcasted_iota(jnp.int32, (2 * lanes, lanes), 0) % lanes
    column = lax.broadcasted_iota(jnp.int32, (2 * lanes, lanes), 1)
    shifts[...] = jnp.where(jnp.abs(row - column) == 1, 1.0, 0.0).astype(BF16)
    lane = lax.broadcasted_iota(jnp.int32, (rows, lanes), 1)
    edge = (lane == 0) | (lane == lanes - 1)
    groups = levels // GROUP
    members = [(field, k) for k in range(GROUP) for field in range(fields)]

    def place(k, field):
        return slice((k * fields + field) * rows, (k * fields + field + 1) * rows)

    def first_inside(g):
        block = jnp.concatenate([held[field, g * GROUP + k] for field, k in members])
        inside[0, g % 2] = beside(block, shifts[...])

    def first_step(g):
        for field, k in members:
            level = g * GROUP + k
            at = field * levels + level
            sides = pltpu.roll(strips[field, 0], (2 * lanes - 1 - 2 * level) % lanes, axis=1)
            once[g % 2, place(k, field)] = stepped(
                held[field, level], halo_rows[0, at : at + 1], halo_rows[1, at : at + 1],
                inside[0, g % 2, place(k, field)], sides, edge,
            )
        inside[1, g % 2] = beside(once[g % 2], shifts[...])

    def second_step(g):
        for field, k in members:
            level = g * GROUP + k
            at = field * levels + level
            sides = pltpu.roll(strips[field, 1], (2 * lanes - 1 - 2 * level) % lanes, axis=1)
            top = halo_rows[2, at : at + 1] + has_top * MIX * held[field, level, 0:1]
            low = halo_rows[3, at : at + 1] + has_low * MIX * held[field, level, rows - 1 : rows]
            right = stepped(
                once[g % 2, place(k, field)], top, low, inside[1, g % 2, place(k, field)], sides, edge
            )
            if level == 0:
                right = right + SURFACE_STEP * source[field]
            else:
                right = right + held_c[level - 1] * done[field, level - 1]
            done[field, level] = right * held_i[level]

    outs = []
    for g in range(groups + 2):
        if g < groups:
            if g * GROUP % STEP == 0:
                for c in copies[g * GROUP // STEP]:
                    c.wait()
            first_inside(g)
        if 0 <= g - 1 < groups:
            first_step(g - 1)
        if g >= 2:
            second_step(g - 2)
            end = (g - 1) * GROUP
            if end % STEP == 0:
                at = pl.ds(end - STEP, STEP)
                outs.append(pltpu.make_async_copy(done.at[:, at], reduced.at[:, at], out_sem.at[end // STEP - 1]))
                outs[-1].start()
    for c in outs:
        c.wait()


def columns_up(air, coupling, inverse, halo, own, source):
    fields, levels, rows, lanes = air.shape
    args = (air, coupling, inverse, *halo, *own, source)
    hbm = pl.BlockSpec(memory_space=pltpu.HBM)
    parts = levels // STEP
    return pl.pallas_call(
        up_kernel,
        in_specs=[hbm] * 3 + [pl.BlockSpec(memory_space=pltpu.VMEM)] * (len(args) - 3),
        out_specs=hbm,
        out_shape=pltpu.HBM(air.shape, F32),
        scratch_shapes=[
            pltpu.VMEM(air.shape, F32),
            pltpu.VMEM(coupling.shape, F32),
            pltpu.VMEM(inverse.shape, F32),
            pltpu.VMEM(air.shape, F32),
            pltpu.VMEM((4, fields * levels, lanes), F32),
            pltpu.VMEM((fields, 2, rows, lanes), F32),
            pltpu.VMEM((2 * lanes, lanes), BF16),
            pltpu.VMEM((2, 2, GROUP * fields * rows, lanes), F32),
            pltpu.VMEM((2, GROUP * fields * rows, lanes), F32),
            pltpu.SemaphoreType.DMA((3 * parts,)),
            pltpu.SemaphoreType.DMA((parts,)),
        ],
        compiler_params=pltpu.CompilerParams(vmem_limit_bytes=24 * MIB),
        cost_estimate=pl.CostEstimate(flops=40 * air.size, bytes_accessed=12 * air.size, transcendentals=0),
        name="columns_up",
    )(*in_hbm(*args[:3]), *args[3:])


def down_kernel(
    reduced, coupling, inverse, weight, air_new, near, held, held_c, held_i, sem, out_sem, sem_w
):
    _, levels, rows, lanes = reduced.shape
    copies = fetch_levels([(reduced, held), (inverse, held_i), (coupling, held_c)], sem, levels, -1)
    weights = fetch(weight.at[pl.ds(0, near.shape[0])], near, sem_w)
    outs = []
    for i, part in enumerate(copies):
        for c in part:
            c.wait()
        top = levels - 1 - i * STEP

        def one(k, _, top=top):
            level = top - k
            ratio = held_c[level] * held_i[level]
            for field in range(2):
                held[field, level] = held[field, level] + ratio * held[field, level + 1]
            return 0

        lax.fori_loop(1 if i == 0 else 0, STEP, one, 0)
        at = pl.ds(levels - (i + 1) * STEP, STEP)
        outs.append(pltpu.make_async_copy(held.at[:, at], air_new.at[:, at], out_sem.at[i]))
        outs[i].start()
    for c in outs + weights:
        c.wait()


def columns_down(reduced, coupling, inverse, weight):
    levels = reduced.shape[1]
    hbm = pl.BlockSpec(memory_space=pltpu.HBM)
    parts = levels // STEP
    return pl.pallas_call(
        down_kernel,
        in_specs=[hbm] * 4,
        out_specs=[hbm, pl.BlockSpec(memory_space=pltpu.VMEM)],
        out_shape=[pltpu.HBM(reduced.shape, F32), pltpu.VMEM((NEAR,) + weight.shape[1:], BF16)],
        scratch_shapes=[
            pltpu.VMEM(reduced.shape, F32),
            pltpu.VMEM(coupling.shape, F32),
            pltpu.VMEM(inverse.shape, F32),
            pltpu.SemaphoreType.DMA((3 * parts,)),
            pltpu.SemaphoreType.DMA((parts,)),
            pltpu.SemaphoreType.DMA((4,)),
        ],
        compiler_params=pltpu.CompilerParams(vmem_limit_bytes=16 * MIB),
        cost_estimate=pl.CostEstimate(flops=8 * reduced.size, bytes_accessed=12 * reduced.size, transcendentals=0),
        name="columns_down",
    )(*in_hbm(reduced, coupling, inverse, weight))


def ocean_kernel(arrived, land_mask, ocean_temp, ocean_ice, layer_depth, temp_new, ice_new, replies):
    blocks, lanes = ocean_temp.shape
    total = arrived.shape[0] * arrived.shape[1]
    wide = arrived.shape[2]
    block = arrived[...].astype(F32).reshape(total, wide)
    lane = lax.broadcasted_iota(jnp.int32, (total, wide), 1)
    tag = block[:, lanes : lanes + 1].astype(jnp.int32)
    block = jnp.where(lane == lanes, 0.0, block).astype(BF16)
    slot_of = (tag == lax.broadcasted_iota(jnp.int32, (total, blocks), 1)).astype(F32).astype(BF16)
    sums = lax.dot_general(slot_of, block, (((0,), (0,)), ((), ())), preferred_element_type=F32)
    sums = [sums[:, k * lanes : (k + 1) * lanes] for k in range(SENT)]
    heat = sums[0] + sums[1]
    stress = sums[2] * sums[2] + sums[3] * sums[3]
    wet = land_mask[...].astype(F32)
    temp = ocean_temp[...]
    temp = temp + wet * (0.3 * heat / layer_depth[...] - 0.01 * stress * temp)
    ice = jnp.clip(ocean_ice[...] - wet * 0.05 * (heat + sums[4]), 0.0, 1.0)
    temp_new[...] = temp
    ice_new[...] = ice
    pair = jnp.concatenate([temp, ice], axis=1).astype(BF16)
    answer = jnp.dot(slot_of, pair, preferred_element_type=F32)
    replies[...] = answer.reshape(replies.shape).astype(BF16)


def ocean(arrived, land_mask, ocean_temp, ocean_ice, layer_depth):
    devices, bound, _ = arrived.shape
    blocks, lanes = ocean_temp.shape
    vmem = pl.BlockSpec(memory_space=pltpu.VMEM)
    return pl.pallas_call(
        ocean_kernel,
        in_specs=[vmem] * 5,
        out_specs=[vmem] * 3,
        out_shape=[
            jax.ShapeDtypeStruct((blocks, lanes), F32),
            jax.ShapeDtypeStruct((blocks, lanes), F32),
            jax.ShapeDtypeStruct((devices, bound, 2 * lanes), BF16),
        ],
        compiler_params=pltpu.CompilerParams(vmem_limit_bytes=16 * MIB),
        name="ocean",
    )(arrived, land_mask, ocean_temp, ocean_ice, layer_depth)


def backward_kernel(
    slots_far, column_far, returned, near, weight, seen, held, sem, pairs, sums, slots, block_column, sem_i
):
    lanes = weight.shape[1]
    total = returned.shape[0] * returned.shape[1]
    rows = seen.shape[1]
    first, blocks = near.shape[0], weight.shape[0]
    copies = fetch(weight.at[pl.ds(first, blocks - first)], held, sem)
    indices = fetch_indices((slots_far, column_far), (slots, block_column), sem_i)
    pairs[...] = jnp.zeros_like(pairs)
    sums[...] = jnp.zeros_like(sums)
    for k in range(2):
        part = returned[:, :, k * lanes : (k + 1) * lanes].astype(F32).reshape(total, lanes)
        pairs[pl.ds(k, total, stride=8), :] = part

    def place(pair):
        for at, out in pair:
            sums[pl.ds(pl.multiple_of(block_column[at] * 8, 8), 8), :] += out

    size = held.shape[0] // PARTS
    for c in indices:
        c.wait()
    waiting = []
    for at in range(0, blocks, 2):
        if at >= first and (at - first) % size == 0:
            copies[(at - first) // size].wait()
        block, k = (near, at) if at < first else (held, at - first)
        picked = [pairs[pl.ds(pl.multiple_of(slots[n] * 8, 8), 8), :] for n in (at, at + 1)]
        out = jnp.dot(
            jnp.concatenate(picked).astype(BF16),
            jnp.concatenate([block[k], block[k + 1]], axis=1),
            preferred_element_type=F32,
        )
        waiting.append(((at, out[:8, :lanes]), (at + 1, out[8:, lanes:])))
        if len(waiting) > LAG:
            place(waiting.pop(0))
    for pair in waiting:
        place(pair)
    for k in range(2):
        seen[k] = sums[pl.ds(k, rows, stride=8), :]


def backward(slots, block_column, returned, near, weight, rows):
    devices, bound, _ = returned.shape
    nonzeros, lanes, _ = weight.shape
    hbm = pl.BlockSpec(memory_space=pltpu.HBM)
    vmem = pl.BlockSpec(memory_space=pltpu.VMEM)
    return pl.pallas_call(
        backward_kernel,
        in_specs=[hbm, hbm, vmem, vmem, hbm],
        out_specs=vmem,
        out_shape=jax.ShapeDtypeStruct((2, rows, lanes), F32),
        scratch_shapes=[
            pltpu.VMEM((nonzeros - NEAR, lanes, lanes), BF16),
            pltpu.SemaphoreType.DMA((PARTS,)),
            pltpu.VMEM((devices * bound * 8, lanes), F32),
            pltpu.VMEM((rows * 8, lanes), F32),
            pltpu.SMEM(slots.shape, jnp.int32),
            pltpu.SMEM(slots.shape, jnp.int32),
            pltpu.SemaphoreType.DMA((2,)),
        ],
        compiler_params=pltpu.CompilerParams(vmem_limit_bytes=16 * MIB),
        name="backward_blocks",
    )(*in_hbm(slots, block_column), returned, *in_vmem(near), *in_hbm(weight))


def local(
    air_state,
    coupling,
    forcing,
    surface_temp,
    remap_weight,
    block_owner,
    block_row,
    block_column,
    land_mask,
    ocean_temp,
    ocean_ice,
    layer_depth,
):
    devices = lax.axis_size("comp") * lax.axis_size("gx") * lax.axis_size("gy")
    nonzeros = remap_weight.shape[0]
    bound = max(4, (nonzeros + devices - 1) // devices)
    rows_a, rows_b = pack_rows(air_state)
    got_b = lax.ppermute(rows_b, ALL, row_swaps(1))
    got_a = lax.ppermute(rows_a, ALL, row_swaps(0))
    *own, lowest, first_half = pack_cols(air_state, remap_weight)
    to_g, to_x = make_strips(got_a, got_b, *own)
    got_x = lax.ppermute(to_x, ("comp", "gy"), col_swaps(1))
    got_g = lax.ppermute(to_g, ("comp", "gy"), col_swaps(0))
    halo = (got_a, got_b, got_g, got_x)
    inverse = pivots(coupling)
    halo, inverse = lax.optimization_barrier((halo, inverse))
    payload, slots, source = forward(
        block_owner[:, 0], block_row, block_column, lowest, forcing, surface_temp, halo, own,
        first_half, remap_weight, air_state.shape[1], devices, bound,
    )
    arrived = lax.all_to_all(payload, ALL, split_axis=0, concat_axis=0, tiled=True)
    reduced = columns_up(air_state, coupling, inverse, halo, own, source)
    arrived, reduced = lax.optimization_barrier((arrived, reduced))
    ocean_temp_new, ocean_ice_new, replies = ocean(
        arrived, land_mask, ocean_temp, ocean_ice, layer_depth
    )
    returned = lax.all_to_all(replies, ALL, split_axis=0, concat_axis=0, tiled=True)
    air_new, near = columns_down(reduced, coupling, inverse, remap_weight)
    returned, air_new = lax.optimization_barrier((returned, air_new))
    surface_seen = backward(slots, block_column, returned, near, remap_weight, surface_temp.shape[0])
    return (air_new, surface_seen, ocean_temp_new, ocean_ice_new)


def solution(mesh):
    in_specs = (
        P(None, None, "gx", ("comp", "gy")),
        P(None, "gx", ("comp", "gy")),
        P(None, "gx", ("comp", "gy")),
        P("gx", ("comp", "gy")),
        P(ALL, None, None),
        P(ALL, None),
        P(ALL),
        P(ALL),
        P(ALL, None),
        P(ALL, None),
        P(ALL, None),
        P(ALL, None),
    )
    out_specs = (
        P(None, None, "gx", ("comp", "gy")),
        P(None, "gx", ("comp", "gy")),
        P(ALL, None),
        P(ALL, None),
    )
    return jax.shard_map(local, mesh=mesh, in_specs=in_specs, out_specs=out_specs, check_vma=False)
```

```python
import functools

import jax
import jax.numpy as jnp
from jax import lax
from jax.experimental import pallas as pl
from jax.experimental.pallas import tpu as pltpu
from jax.sharding import PartitionSpec as P

F32 = jnp.float32
BF16 = jnp.bfloat16
ALL = ("comp", "gx", "gy")
NF = 8
SENT = 5
SURFACE_STEP = 0.5
MIX = 0.2
MIB = 1 << 20
PARTS = 16
STEP = 8
GROUP = 4
LAG = 8
NEAR = 64


def in_vmem(*arrays):
    return [pltpu.with_memory_space_constraint(x, pltpu.VMEM) for x in arrays]


def in_hbm(*arrays):
    return [pltpu.with_memory_space_constraint(x, pltpu.HBM) for x in arrays]


def row_swaps(first):
    n_gx, n_gy = lax.axis_size("gx"), lax.axis_size("gy")
    pairs = []
    for comp in range(lax.axis_size("comp")):
        for gx in range(n_gx):
            for gy in range(n_gy):
                other = gx + 1 if (gx - first) % 2 == 0 else gx - 1
                to, core = (other, gy) if 0 <= other < n_gx else (gx, gy ^ 1)
                pairs.append(((comp * n_gx + gx) * n_gy + gy, (comp * n_gx + to) * n_gy + core))
    return pairs


def col_swaps(first):
    count = lax.axis_size("comp") * lax.axis_size("gy")
    return [(i, (i + 1 if (i - first) % 2 == 0 else i - 1) % count) for i in range(count)]


def grid_place():
    gx, n_gx = lax.axis_index("gx"), lax.axis_size("gx")
    c = lax.axis_index("comp") * lax.axis_size("gy") + lax.axis_index("gy")
    n_c = lax.axis_size("comp") * lax.axis_size("gy")
    there = lambda yes: jnp.where(yes, 1.0, 0.0).astype(F32)
    return gx % 2 == 0, c % 2 == 0, there(gx > 0), there(gx < n_gx - 1), there(c > 0), there(c < n_c - 1)


def rows_kernel(air, rows_a, rows_b, first, last, sem):
    even_row = grid_place()[0]
    count, tile, lanes = first.shape
    rows = air.shape[1]
    copies = [
        pltpu.make_async_copy(air.at[:, pl.ds(0, tile)], first, sem.at[0]),
        pltpu.make_async_copy(air.at[:, pl.ds(rows - tile, tile)], last, sem.at[1]),
    ]
    for c in copies:
        c.start()
    for c in copies:
        c.wait()
    first, last = [x.reshape(count * tile, lanes) for x in (first, last)]
    for k in range(2):
        low, high = first[pl.ds(k, count, stride=tile), :], last[pl.ds(tile - 1 - k, count, stride=tile), :]
        to = slice(k * lanes, (k + 1) * lanes)
        rows_a[:, to] = jnp.where(even_row, high, low).astype(BF16)
        rows_b[:, to] = jnp.where(even_row, low, high).astype(BF16)


def pack_rows(air):
    fields, levels, rows, lanes = air.shape
    out = jax.ShapeDtypeStruct((fields * levels, 2 * lanes), BF16)
    edge = pltpu.VMEM((fields * levels, 8, lanes), F32)
    return pl.pallas_call(
        rows_kernel,
        in_specs=[pl.BlockSpec(memory_space=pltpu.HBM)],
        out_specs=[pl.BlockSpec(memory_space=pltpu.VMEM)] * 2,
        out_shape=[out, out],
        scratch_shapes=[edge, edge, pltpu.SemaphoreType.DMA((2,))],
        compiler_params=pltpu.CompilerParams(vmem_limit_bytes=8 * MIB),
        name="pack_rows",
    )(*in_hbm(air.reshape(fields * levels, rows, lanes)))


def cols_kernel(air, weight, own_left, own_right, lowest, first_half, held, sem, sem_w, chunk):
    fields, levels, rows, lanes = air.shape
    copies = []
    for i in range(levels // chunk):
        part = pl.ds(i * chunk, chunk)
        copies.append(pltpu.make_async_copy(air.at[:, part], held.at[:, part], sem.at[i]))
        copies[i].start()
    weights = fetch(weight.at[pl.ds(0, first_half.shape[0])], first_half, sem_w)
    pair = lax.broadcasted_iota(jnp.int32, (rows, lanes), 1) >> 1
    left, right = [[jnp.zeros((rows, lanes), F32)] * fields for _ in range(2)]
    for i in range(levels // chunk):
        copies[i].wait()
        if i == 0:
            lowest[...] = held[:, 0]
        for level in range(i * chunk, (i + 1) * chunk):
            for field in range(fields):
                turned = pltpu.roll(held[field, level], 2 * level % lanes, axis=1)
                left[field] = jnp.where(pair == level, turned, left[field])
                right[field] = jnp.where(pair == (level - 1) % levels, turned, right[field])
    for field in range(fields):
        own_left[field] = left[field]
        own_right[field] = pltpu.roll(right[field], 2, axis=1)
    for c in weights:
        c.wait()


def pack_cols(air, weight):
    fields, levels, rows, lanes = air.shape
    chunk = 8
    vmem = pl.BlockSpec(memory_space=pltpu.VMEM)
    out = jax.ShapeDtypeStruct((fields, rows, lanes), F32)
    return pl.pallas_call(
        functools.partial(cols_kernel, chunk=chunk),
        in_specs=[pl.BlockSpec(memory_space=pltpu.HBM)] * 2,
        out_specs=[vmem] * 4,
        out_shape=[out, out, out, pltpu.VMEM((weight.shape[0] // 2, lanes, lanes), BF16)],
        scratch_shapes=[
            pltpu.VMEM(air.shape, F32),
            pltpu.SemaphoreType.DMA((levels // chunk,)),
            pltpu.SemaphoreType.DMA((PARTS,)),
        ],
        compiler_params=pltpu.CompilerParams(vmem_limit_bytes=12 * MIB),
        cost_estimate=pl.CostEstimate(flops=4 * air.size, bytes_accessed=4 * air.size, transcendentals=0),
        name="pack_cols",
    )(*in_hbm(air, weight))


def with_row(strip, row, first):
    rows = strip.shape[0]
    index = lax.broadcasted_iota(jnp.int32, strip.shape, 0)
    if first:
        return jnp.where(index == 0, row, pltpu.roll(strip, 1, axis=0))
    return jnp.where(index == rows - 1, row, pltpu.roll(strip, rows - 1, axis=0))


def strips_kernel(got_a, got_b, own_left, own_right, to_g, to_x):
    even_col = grid_place()[1]
    fields, rows, lanes = own_left.shape
    top, _, low, _ = row_halo(got_a, got_b)
    levels = top.shape[0] // fields
    level = lax.broadcasted_iota(jnp.int32, (levels, lanes), 0)
    pair = lax.broadcasted_iota(jnp.int32, (levels, lanes), 1) >> 1
    spread = jnp.where(level == pair, 1.0, 0.0).astype(BF16)
    odd = (lax.broadcasted_iota(jnp.int32, (rows, lanes), 1) & 1) == 1
    for field in range(fields):
        at = slice(field * levels, (field + 1) * levels)
        above, below = [
            lax.dot_general(h[at].astype(BF16), spread, (((0,), (0,)), ((), ())), preferred_element_type=F32)
            for h in (top, low)
        ]
        left, right = own_left[field], own_right[field]
        edge = pltpu.roll(left, 1, axis=1)
        around = with_row(edge, 2.0 * above[0:1], True) + with_row(edge, 2.0 * below[0:1], False)
        west = jnp.where(odd, MIX * (edge + left + around), left)
        edge = pltpu.roll(right, lanes - 1, axis=1)
        around = with_row(edge, 2.0 * above[lanes - 1 :], True) + with_row(edge, 2.0 * below[lanes - 1 :], False)
        east = jnp.where(odd, right, MIX * (edge + right + around))
        to_g[field] = jnp.where(even_col, east, west).astype(BF16)
        to_x[field] = jnp.where(even_col, west, east).astype(BF16)


def make_strips(got_a, got_b, own_left, own_right):
    vmem = pl.BlockSpec(memory_space=pltpu.VMEM)
    out = jax.ShapeDtypeStruct(own_left.shape, BF16)
    return pl.pallas_call(
        strips_kernel,
        in_specs=[vmem] * 4,
        out_specs=[vmem] * 2,
        out_shape=[out, out],
        compiler_params=pltpu.CompilerParams(vmem_limit_bytes=8 * MIB),
        name="strips",
    )(got_a, got_b, own_left, own_right)


def side_strips(field, got_g, got_x, own_left, own_right):
    _, even_col, _, _, has_left, has_right = grid_place()
    rows, lanes = got_g.shape[1], got_g.shape[2]
    from_g, from_x = got_g[field].astype(F32), got_x[field].astype(F32)
    west = jnp.where(even_col, from_x, from_g) * has_left
    east = jnp.where(even_col, from_g, from_x) * has_right
    next_west = pltpu.roll(west + MIX * own_left[field], 1, axis=1) * has_left
    next_east = pltpu.roll(east + MIX * own_right[field], lanes - 1, axis=1) * has_right
    odd = (lax.broadcasted_iota(jnp.int32, (rows, lanes), 1) & 1) == 1
    return jnp.where(odd, west, east), jnp.where(odd, next_west, next_east)


def row_halo(got_a, got_b):
    even_row, _, has_top, has_low, _, _ = grid_place()
    from_a, from_b = got_a[...].astype(F32), got_b[...].astype(F32)
    top = jnp.where(even_row, from_b, from_a) * has_top
    low = jnp.where(even_row, from_a, from_b) * has_low
    lanes = top.shape[1] // 2
    return top[:, :lanes], top[:, lanes:], low[:, :lanes], low[:, lanes:]


def sides_of_row(row):
    lanes = row.shape[1]
    lane = lax.broadcasted_iota(jnp.int32, row.shape, 1)
    from_left = jnp.where(lane == 0, 0.0, pltpu.roll(row, 1, axis=1))
    from_right = jnp.where(lane == lanes - 1, 0.0, pltpu.roll(row, lanes - 1, axis=1))
    return from_left + from_right


def substep(block, above, below, sides):
    lanes = block.shape[1]
    lane = lax.broadcasted_iota(jnp.int32, block.shape, 1)
    from_left = jnp.where(lane == 0, sides, pltpu.roll(block, 1, axis=1))
    from_right = jnp.where(lane == lanes - 1, sides, pltpu.roll(block, lanes - 1, axis=1))
    around = with_row(block, above, True) + with_row(block, below, False)
    return MIX * (block + around + (from_left + from_right))


def next_rows(top1, top2, low1, low2):
    return MIX * (top1 + top2 + sides_of_row(top1)), MIX * (low1 + low2 + sides_of_row(low1))


def mixed_level(block, top, next_top, low, next_low, sides0, sides1):
    rows = block.shape[0]
    _, _, has_top, has_low, _, _ = grid_place()
    once = substep(block, top, low, sides0)
    next_top = next_top + has_top * MIX * block[0:1]
    next_low = next_low + has_low * MIX * block[rows - 1 : rows]
    return substep(once, next_top, next_low, sides1)


def forward_kernel(
    owner_far, row_far, column_far, air, forcing, surface_temp, got_a, got_b, got_g, got_x,
    own_left, own_right, first_half, weight, payload, slots_far, source, held, sem, flux_rows, found, tags,
    counts, owner, block_row, block_column, slots, sem_i,
    bound, levels, group,
):
    blocks = weight.shape[0]
    rows, lanes = surface_temp.shape
    devices = payload.shape[0]
    total = devices * bound
    half = held.shape[0]
    copies = fetch(weight.at[pl.ds(half, half)], held, sem)
    indices = fetch_indices((owner_far, row_far, column_far), (owner, block_row, block_column), sem_i)
    top1, top2, low1, low2 = [jnp.concatenate([h[0:1], h[levels : levels + 1]]) for h in row_halo(got_a, got_b)]
    next_top, next_low = next_rows(top1, top2, low1, low2)
    lowest = []
    for field in range(2):
        sides0, sides1 = side_strips(field, got_g, got_x, own_left, own_right)
        lowest.append(
            mixed_level(
                air[field],
                *[h[field : field + 1] for h in (top1, next_top, low1, next_low)],
                pltpu.roll(sides0, lanes - 1, axis=1),
                pltpu.roll(sides1, lanes - 1, axis=1),
            )
        )
    u, v = forcing[0], forcing[1]
    ts = surface_temp[...]
    speed = jnp.sqrt(u * u + v * v + 1.0)
    fluxes = [
        speed * (ts - lowest[0]),
        speed * (0.5 * ts - lowest[1]),
        speed * u,
        speed * v,
        forcing[2],
        forcing[3] - 0.3 * ts,
        forcing[4],
        forcing[5],
    ]
    source[0] = fluxes[0]
    source[1] = fluxes[1]
    for field in range(NF):
        flux_rows[pl.ds(field, rows, stride=NF), :] = fluxes[field]
    if total > blocks:
        tags[...] = jnp.full_like(tags, -1.0)
        found[...] = jnp.zeros_like(found)

    def clear(i, _):
        counts[i] = 0
        return 0

    lax.fori_loop(0, devices, clear, 0)
    for c in indices:
        c.wait()

    def place(pair):
        for at, out in pair:
            to = owner[at]
            rank = counts[to]
            counts[to] = rank + 1
            slot = to * bound + rank
            slots[at] = slot
            found[pl.ds(pl.multiple_of(slot * NF, NF), NF), :] = out
            tags[pl.ds(slot, 1), :] = jnp.full((1, lanes), block_row[at], jnp.int32).astype(F32)

    def some(first, start, half):
        waiting = []
        for k in range(0, group, 2):
            at = start + first + k
            picked = [
                flux_rows[pl.ds(pl.multiple_of(block_column[n] * NF, NF), NF), :] for n in (at, at + 1)
            ]
            out = lax.dot_general(
                jnp.concatenate(picked).astype(BF16),
                half[pl.ds(first + k, 2)].reshape(2 * lanes, lanes),
                (((1,), (1,)), ((), ())),
                preferred_element_type=F32,
            )
            waiting.append(((at, out[:NF, :lanes]), (at + 1, out[NF:, lanes:])))
            if len(waiting) > LAG:
                place(waiting.pop(0))
        for pair in waiting:
            place(pair)

    all_of(first_half, 0, group, some)
    for c in copies:
        c.wait()
    all_of(held, half, group, some)
    (kept,) = fetch_indices((slots,), (slots_far,), sem_i)
    f = [found[pl.ds(k, total, stride=NF), :] for k in range(NF)]
    heat = (f[0] + f[1]) + (f[4] + f[5])
    heat_hi = heat.astype(BF16).astype(F32)
    lane = lax.broadcasted_iota(jnp.int32, (total, lanes), 1)
    heat_lo = jnp.where(lane == 0, tags[...], heat - heat_hi)
    shape = payload.shape[:2] + (lanes,)
    for k, part in enumerate((heat_hi, heat_lo, f[2], f[3], f[6] - f[7])):
        payload[:, :, k * lanes : (k + 1) * lanes] = part.reshape(shape).astype(BF16)
    kept.wait()


def fetch(source, held, sem):
    parts = sem.shape[0]
    size = source.shape[0] // parts
    copies = []
    for i in range(parts):
        at = pl.ds(i * size, size)
        copies.append(pltpu.make_async_copy(source.at[at], held.at[at], sem.at[i]))
        copies[i].start()
    return copies


def fetch_indices(sources, targets, sem):
    copies = [pltpu.make_async_copy(a, b, sem.at[i]) for i, (a, b) in enumerate(zip(sources, targets))]
    for c in copies:
        c.start()
    return copies


def all_of(weight, start, group, some):
    def body(g, carry):
        some(g * group, start, weight)
        return carry

    lax.fori_loop(0, weight.shape[0] // group, body, 0)


def forward(
    owner, block_row, block_column, lowest, forcing, surface_temp, halo, own, first_half, weight, levels,
    devices, bound,
):
    _, rows, lanes = lowest.shape
    nonzeros = weight.shape[0]
    hbm = pl.BlockSpec(memory_space=pltpu.HBM)
    vmem = pl.BlockSpec(memory_space=pltpu.VMEM)
    args = (forcing, surface_temp, *halo, *own)
    total = devices * bound
    return pl.pallas_call(
        functools.partial(forward_kernel, bound=bound, levels=levels, group=128),
        in_specs=[hbm, hbm, hbm]
        + [vmem] * (len(args) + 2)
        + [pl.BlockSpec(memory_space=pltpu.HBM)],
        out_specs=[vmem, hbm, vmem],
        out_shape=[
            jax.ShapeDtypeStruct((devices, bound, SENT * lanes), BF16),
            pltpu.HBM((nonzeros,), jnp.int32),
            jax.ShapeDtypeStruct((2, rows, lanes), F32),
        ],
        scratch_shapes=[
            pltpu.VMEM(first_half.shape, BF16),
            pltpu.SemaphoreType.DMA((PARTS,)),
            pltpu.VMEM((rows * NF, lanes), F32),
            pltpu.VMEM((total * NF, lanes), F32),
            pltpu.VMEM((total, lanes), F32),
            pltpu.SMEM((devices,), jnp.int32),
            pltpu.SMEM((nonzeros,), jnp.int32),
            pltpu.SMEM((nonzeros,), jnp.int32),
            pltpu.SMEM((nonzeros,), jnp.int32),
            pltpu.SMEM((nonzeros,), jnp.int32),
            pltpu.SemaphoreType.DMA((3,)),
        ],
        compiler_params=pltpu.CompilerParams(vmem_limit_bytes=20 * MIB),
        name="forward_blocks",
    )(*in_hbm(owner, block_row, block_column), lowest, *args, *in_vmem(first_half), *in_hbm(weight))


def pivot_kernel(coupling, out, held, inverse, sem, out_sem):
    levels = inverse.shape[0]
    copies = fetch_levels([(coupling, held)], sem, levels - 1)

    def one(level, ratio, last=False):
        below = held[level - 1]
        diagonal = 1.0 + below
        if not last:
            diagonal = diagonal + held[level]
        inv = 1.0 / (diagonal - below * ratio)
        inverse[level] = inv
        return inv if last else held[level] * inv

    outs = []
    for i, part in enumerate(copies):
        for c in part:
            c.wait()
        if i == 0:
            inv = 1.0 / (1.0 + held[0])
            inverse[0] = inv
            ratio = held[0] * inv
        start = max(1, i * STEP)
        stop = min((i + 1) * STEP, levels - 1)
        ratio = lax.fori_loop(start, stop, one, ratio)
        if stop == levels - 1:
            one(levels - 1, ratio, True)
        at = pl.ds(i * STEP, STEP)
        outs.append(pltpu.make_async_copy(inverse.at[at], out.at[at], out_sem.at[i]))
        outs[i].start()
    for c in outs:
        c.wait()


def fetch_levels(pairs, sem, levels, order=1):
    copies = []
    starts = list(range(0, levels, STEP))[::order]
    for i, start in enumerate(starts):
        part = []
        for k, (source, held) in enumerate(pairs):
            at = pl.ds(start, min(STEP, source.shape[-3] - start))
            if len(source.shape) == 4:
                part.append(pltpu.make_async_copy(source.at[:, at], held.at[:, at], sem.at[k * len(starts) + i]))
            else:
                part.append(pltpu.make_async_copy(source.at[at], held.at[at], sem.at[k * len(starts) + i]))
        for c in part:
            c.start()
        copies.append(part)
    return copies


def pivots(coupling):
    levels, rows, lanes = coupling.shape
    shape = (levels + 1, rows, lanes)
    return pl.pallas_call(
        pivot_kernel,
        in_specs=[pl.BlockSpec(memory_space=pltpu.HBM)],
        out_specs=pl.BlockSpec(memory_space=pltpu.HBM),
        out_shape=pltpu.HBM(shape, F32),
        scratch_shapes=[
            pltpu.VMEM(coupling.shape, F32),
            pltpu.VMEM(shape, F32),
            pltpu.SemaphoreType.DMA(((levels + STEP) // STEP,)),
            pltpu.SemaphoreType.DMA(((levels + STEP) // STEP,)),
        ],
        compiler_params=pltpu.CompilerParams(vmem_limit_bytes=12 * MIB),
        cost_estimate=pl.CostEstimate(flops=8 * coupling.size, bytes_accessed=8 * coupling.size, transcendentals=0),
        name="pivots",
    )(*in_hbm(coupling))


def beside(block, shifts):
    high = block.astype(BF16)
    low = (block - high.astype(F32)).astype(BF16)
    return jnp.dot(jnp.concatenate([high, low], axis=1), shifts, preferred_element_type=F32)


def stepped(block, above, below, inside, sides, edge):
    around = with_row(block, above, True) + with_row(block, below, False)
    return MIX * (block + around + (inside + jnp.where(edge, sides, 0.0)))


def up_kernel(
    air, coupling, inverse, got_a, got_b, got_g, got_x, own_left, own_right, source, reduced,
    held, held_c, held_i, done, halo_rows, strips, shifts, inside, once, sem, out_sem,
):
    fields, levels, rows, lanes = air.shape
    copies = fetch_levels([(air, held), (inverse, held_i), (coupling, held_c)], sem, levels)
    _, _, has_top, has_low, _, _ = grid_place()
    halo = row_halo(got_a, got_b)
    for k, h in enumerate((halo[0], halo[2], *next_rows(*halo))):
        halo_rows[k] = h
    for field in range(fields):
        sides0, sides1 = side_strips(field, got_g, got_x, own_left, own_right)
        strips[field, 0] = sides0
        strips[field, 1] = sides1
    row = lax.broadcasted_iota(jnp.int32, (2 * lanes, lanes), 0) % lanes
    column = lax.broadcasted_iota(jnp.int32, (2 * lanes, lanes), 1)
    shifts[...] = jnp.where(jnp.abs(row - column) == 1, 1.0, 0.0).astype(BF16)
    lane = lax.broadcasted_iota(jnp.int32, (rows, lanes), 1)
    edge = (lane == 0) | (lane == lanes - 1)
    groups = levels // GROUP
    members = [(field, k) for k in range(GROUP) for field in range(fields)]

    def place(k, field):
        return slice((k * fields + field) * rows, (k * fields + field + 1) * rows)

    def first_inside(g):
        block = jnp.concatenate([held[field, g * GROUP + k] for field, k in members])
        inside[0, g % 2] = beside(block, shifts[...])

    def first_step(g):
        for field, k in members:
            level = g * GROUP + k
            at = field * levels + level
            sides = pltpu.roll(strips[field, 0], (2 * lanes - 1 - 2 * level) % lanes, axis=1)
            once[g % 2, place(k, field)] = stepped(
                held[field, level], halo_rows[0, at : at + 1], halo_rows[1, at : at + 1],
                inside[0, g % 2, place(k, field)], sides, edge,
            )
        inside[1, g % 2] = beside(once[g % 2], shifts[...])

    def second_step(g):
        for field, k in members:
            level = g * GROUP + k
            at = field * levels + level
            sides = pltpu.roll(strips[field, 1], (2 * lanes - 1 - 2 * level) % lanes, axis=1)
            top = halo_rows[2, at : at + 1] + has_top * MIX * held[field, level, 0:1]
            low = halo_rows[3, at : at + 1] + has_low * MIX * held[field, level, rows - 1 : rows]
            right = stepped(
                once[g % 2, place(k, field)], top, low, inside[1, g % 2, place(k, field)], sides, edge
            )
            if level == 0:
                right = right + SURFACE_STEP * source[field]
            else:
                right = right + held_c[level - 1] * done[field, level - 1]
            done[field, level] = right * held_i[level]

    outs = []
    for g in range(groups + 2):
        if g < groups:
            if g * GROUP % STEP == 0:
                for c in copies[g * GROUP // STEP]:
                    c.wait()
            first_inside(g)
        if 0 <= g - 1 < groups:
            first_step(g - 1)
        if g >= 2:
            second_step(g - 2)
            end = (g - 1) * GROUP
            if end % STEP == 0:
                at = pl.ds(end - STEP, STEP)
                outs.append(pltpu.make_async_copy(done.at[:, at], reduced.at[:, at], out_sem.at[end // STEP - 1]))
                outs[-1].start()
    for c in outs:
        c.wait()


def columns_up(air, coupling, inverse, halo, own, source):
    fields, levels, rows, lanes = air.shape
    args = (air, coupling, inverse, *halo, *own, source)
    hbm = pl.BlockSpec(memory_space=pltpu.HBM)
    parts = levels // STEP
    return pl.pallas_call(
        up_kernel,
        in_specs=[hbm] * 3 + [pl.BlockSpec(memory_space=pltpu.VMEM)] * (len(args) - 3),
        out_specs=hbm,
        out_shape=pltpu.HBM(air.shape, F32),
        scratch_shapes=[
            pltpu.VMEM(air.shape, F32),
            pltpu.VMEM(coupling.shape, F32),
            pltpu.VMEM(inverse.shape, F32),
            pltpu.VMEM(air.shape, F32),
            pltpu.VMEM((4, fields * levels, lanes), F32),
            pltpu.VMEM((fields, 2, rows, lanes), F32),
            pltpu.VMEM((2 * lanes, lanes), BF16),
            pltpu.VMEM((2, 2, GROUP * fields * rows, lanes), F32),
            pltpu.VMEM((2, GROUP * fields * rows, lanes), F32),
            pltpu.SemaphoreType.DMA((3 * parts,)),
            pltpu.SemaphoreType.DMA((parts,)),
        ],
        compiler_params=pltpu.CompilerParams(vmem_limit_bytes=24 * MIB),
        cost_estimate=pl.CostEstimate(flops=40 * air.size, bytes_accessed=12 * air.size, transcendentals=0),
        name="columns_up",
    )(*in_hbm(*args[:3]), *args[3:])


def down_kernel(
    reduced, coupling, inverse, weight, air_new, near, held, held_c, held_i, sem, out_sem, sem_w
):
    _, levels, rows, lanes = reduced.shape
    copies = fetch_levels([(reduced, held), (inverse, held_i), (coupling, held_c)], sem, levels, -1)
    weights = fetch(weight.at[pl.ds(0, near.shape[0])], near, sem_w)
    outs = []
    for i, part in enumerate(copies):
        for c in part:
            c.wait()
        top = levels - 1 - i * STEP

        def one(k, _, top=top):
            level = top - k
            ratio = held_c[level] * held_i[level]
            for field in range(2):
                held[field, level] = held[field, level] + ratio * held[field, level + 1]
            return 0

        lax.fori_loop(1 if i == 0 else 0, STEP, one, 0)
        at = pl.ds(levels - (i + 1) * STEP, STEP)
        outs.append(pltpu.make_async_copy(held.at[:, at], air_new.at[:, at], out_sem.at[i]))
        outs[i].start()
    for c in outs + weights:
        c.wait()


def columns_down(reduced, coupling, inverse, weight):
    levels = reduced.shape[1]
    hbm = pl.BlockSpec(memory_space=pltpu.HBM)
    parts = levels // STEP
    return pl.pallas_call(
        down_kernel,
        in_specs=[hbm] * 4,
        out_specs=[hbm, pl.BlockSpec(memory_space=pltpu.VMEM)],
        out_shape=[pltpu.HBM(reduced.shape, F32), pltpu.VMEM((NEAR,) + weight.shape[1:], BF16)],
        scratch_shapes=[
            pltpu.VMEM(reduced.shape, F32),
            pltpu.VMEM(coupling.shape, F32),
            pltpu.VMEM(inverse.shape, F32),
            pltpu.SemaphoreType.DMA((3 * parts,)),
            pltpu.SemaphoreType.DMA((parts,)),
            pltpu.SemaphoreType.DMA((4,)),
        ],
        compiler_params=pltpu.CompilerParams(vmem_limit_bytes=16 * MIB),
        cost_estimate=pl.CostEstimate(flops=8 * reduced.size, bytes_accessed=12 * reduced.size, transcendentals=0),
        name="columns_down",
    )(*in_hbm(reduced, coupling, inverse, weight))


def ocean_kernel(arrived, land_mask, ocean_temp, ocean_ice, layer_depth, temp_new, ice_new, replies):
    blocks, lanes = ocean_temp.shape
    total = arrived.shape[0] * arrived.shape[1]
    wide = arrived.shape[2]
    block = arrived[...].astype(F32).reshape(total, wide)
    lane = lax.broadcasted_iota(jnp.int32, (total, wide), 1)
    tag = block[:, lanes : lanes + 1].astype(jnp.int32)
    block = jnp.where(lane == lanes, 0.0, block).astype(BF16)
    slot_of = (tag == lax.broadcasted_iota(jnp.int32, (total, blocks), 1)).astype(F32).astype(BF16)
    sums = lax.dot_general(slot_of, block, (((0,), (0,)), ((), ())), preferred_element_type=F32)
    sums = [sums[:, k * lanes : (k + 1) * lanes] for k in range(SENT)]
    heat = sums[0] + sums[1]
    stress = sums[2] * sums[2] + sums[3] * sums[3]
    wet = land_mask[...].astype(F32)
    temp = ocean_temp[...]
    temp = temp + wet * (0.3 * heat / layer_depth[...] - 0.01 * stress * temp)
    ice = jnp.clip(ocean_ice[...] - wet * 0.05 * (heat + sums[4]), 0.0, 1.0)
    temp_new[...] = temp
    ice_new[...] = ice
    pair = jnp.concatenate([temp, ice], axis=1).astype(BF16)
    answer = jnp.dot(slot_of, pair, preferred_element_type=F32)
    replies[...] = answer.reshape(replies.shape).astype(BF16)


def ocean(arrived, land_mask, ocean_temp, ocean_ice, layer_depth):
    devices, bound, _ = arrived.shape
    blocks, lanes = ocean_temp.shape
    vmem = pl.BlockSpec(memory_space=pltpu.VMEM)
    return pl.pallas_call(
        ocean_kernel,
        in_specs=[vmem] * 5,
        out_specs=[vmem] * 3,
        out_shape=[
            jax.ShapeDtypeStruct((blocks, lanes), F32),
            jax.ShapeDtypeStruct((blocks, lanes), F32),
            jax.ShapeDtypeStruct((devices, bound, 2 * lanes), BF16),
        ],
        compiler_params=pltpu.CompilerParams(vmem_limit_bytes=16 * MIB),
        name="ocean",
    )(arrived, land_mask, ocean_temp, ocean_ice, layer_depth)


def backward_kernel(
    slots_far, column_far, returned, near, weight, seen, held, sem, pairs, sums, slots, block_column, sem_i
):
    lanes = weight.shape[1]
    total = returned.shape[0] * returned.shape[1]
    rows = seen.shape[1]
    first, blocks = near.shape[0], weight.shape[0]
    copies = fetch(weight.at[pl.ds(first, blocks - first)], held, sem)
    indices = fetch_indices((slots_far, column_far), (slots, block_column), sem_i)
    pairs[...] = jnp.zeros_like(pairs)
    sums[...] = jnp.zeros_like(sums)
    for k in range(2):
        part = returned[:, :, k * lanes : (k + 1) * lanes].astype(F32).reshape(total, lanes)
        pairs[pl.ds(k, total, stride=8), :] = part

    def place(pair):
        for at, out in pair:
            sums[pl.ds(pl.multiple_of(block_column[at] * 8, 8), 8), :] += out

    size = held.shape[0] // PARTS
    for c in indices:
        c.wait()
    waiting = []
    for at in range(0, blocks, 2):
        if at >= first and (at - first) % size == 0:
            copies[(at - first) // size].wait()
        block, k = (near, at) if at < first else (held, at - first)
        picked = [pairs[pl.ds(pl.multiple_of(slots[n] * 8, 8), 8), :] for n in (at, at + 1)]
        out = jnp.dot(
            jnp.concatenate(picked).astype(BF16),
            jnp.concatenate([block[k], block[k + 1]], axis=1),
            preferred_element_type=F32,
        )
        waiting.append(((at, out[:8, :lanes]), (at + 1, out[8:, lanes:])))
        if len(waiting) > LAG:
            place(waiting.pop(0))
    for pair in waiting:
        place(pair)
    for k in range(2):
        seen[k] = sums[pl.ds(k, rows, stride=8), :]


def backward(slots, block_column, returned, near, weight, rows):
    devices, bound, _ = returned.shape
    nonzeros, lanes, _ = weight.shape
    hbm = pl.BlockSpec(memory_space=pltpu.HBM)
    vmem = pl.BlockSpec(memory_space=pltpu.VMEM)
    return pl.pallas_call(
        backward_kernel,
        in_specs=[hbm, hbm, vmem, vmem, hbm],
        out_specs=vmem,
        out_shape=jax.ShapeDtypeStruct((2, rows, lanes), F32),
        scratch_shapes=[
            pltpu.VMEM((nonzeros - NEAR, lanes, lanes), BF16),
            pltpu.SemaphoreType.DMA((PARTS,)),
            pltpu.VMEM((devices * bound * 8, lanes), F32),
            pltpu.VMEM((rows * 8, lanes), F32),
            pltpu.SMEM(slots.shape, jnp.int32),
            pltpu.SMEM(slots.shape, jnp.int32),
            pltpu.SemaphoreType.DMA((2,)),
        ],
        compiler_params=pltpu.CompilerParams(vmem_limit_bytes=16 * MIB),
        name="backward_blocks",
    )(*in_hbm(slots, block_column), returned, *in_vmem(near), *in_hbm(weight))


def local(
    air_state,
    coupling,
    forcing,
    surface_temp,
    remap_weight,
    block_owner,
    block_row,
    block_column,
    land_mask,
    ocean_temp,
    ocean_ice,
    layer_depth,
):
    devices = lax.axis_size("comp") * lax.axis_size("gx") * lax.axis_size("gy")
    nonzeros = remap_weight.shape[0]
    bound = max(4, (nonzeros + devices - 1) // devices)
    rows_a, rows_b = pack_rows(air_state)
    got_b = lax.ppermute(rows_b, ALL, row_swaps(1))
    got_a = lax.ppermute(rows_a, ALL, row_swaps(0))
    *own, lowest, first_half = pack_cols(air_state, remap_weight)
    to_g, to_x = make_strips(got_a, got_b, *own)
    got_x = lax.ppermute(to_x, ("comp", "gy"), col_swaps(1))
    got_g = lax.ppermute(to_g, ("comp", "gy"), col_swaps(0))
    halo = (got_a, got_b, got_g, got_x)
    inverse = pivots(coupling)
    halo, inverse = lax.optimization_barrier((halo, inverse))
    payload, slots, source = forward(
        block_owner[:, 0], block_row, block_column, lowest, forcing, surface_temp, halo, own,
        first_half, remap_weight, air_state.shape[1], devices, bound,
    )
    arrived = lax.all_to_all(payload, ALL, split_axis=0, concat_axis=0, tiled=True)
    reduced = columns_up(air_state, coupling, inverse, halo, own, source)
    arrived, reduced = lax.optimization_barrier((arrived, reduced))
    ocean_temp_new, ocean_ice_new, replies = ocean(
        arrived, land_mask, ocean_temp, ocean_ice, layer_depth
    )
    returned = lax.all_to_all(replies, ALL, split_axis=0, concat_axis=0, tiled=True)
    air_new, near = columns_down(reduced, coupling, inverse, remap_weight)
    returned, air_new = lax.optimization_barrier((returned, air_new))
    surface_seen = backward(slots, block_column, returned, near, remap_weight, surface_temp.shape[0])
    return (air_new, surface_seen, ocean_temp_new, ocean_ice_new)


def solution(mesh):
    in_specs = (
        P(None, None, "gx", ("comp", "gy")),
        P(None, "gx", ("comp", "gy")),
        P(None, "gx", ("comp", "gy")),
        P("gx", ("comp", "gy")),
        P(ALL, None, None),
        P(ALL, None),
        P(ALL),
        P(ALL),
        P(ALL, None),
        P(ALL, None),
        P(ALL, None),
        P(ALL, None),
    )
    out_specs = (
        P(None, None, "gx", ("comp", "gy")),
        P(None, "gx", ("comp", "gy")),
        P(ALL, None),
        P(ALL, None),
    )
    return jax.shard_map(local, mesh=mesh, in_specs=in_specs, out_specs=out_specs, check_vma=False)
```
